128 devices in a mesh: dp: 32 (over x_hi, y, z), gen: 4 (over x_lo, core).
Axes of the slice: x: 4 (x_hi: 2, x_lo: 2; x = x_hi * 2 + x_lo), y: 4, z: 4, core: 2. Of those that a mesh axis runs over, the one named last changes fastest.
Arguments:
- src_ids: int32 [256, 256], P('dp'), may hold values from 0 to 32127
- tgt_ids: int32 [256, 128], P('dp'), may hold values from 0 to 32127
- task_ids: int32 [256], P('dp'), may hold values from 0 to 7
- task_len: int32 [8], replicated, may hold values from 64 to 256, as said below
- tgt_count: int32 [256], P('dp'), may hold values from 32 to 128, as said below
- table: bfloat16 [32128, 512], P('gen')
- attn_w: bfloat16 [3, 512, 2048], replicated, may hold values from -0.25 to 0.25
- ffn_in: bfloat16 [2, 512, 2048], replicated, may hold values from -0.25 to 0.25
- ffn_out: bfloat16 [2, 2048, 512], replicated, may hold values from -0.125 to 0.125
- gains: float32 [7, 512], replicated, may hold values from 0.5 to 1.5
- embeds: float32 [10, 64], replicated, may hold values from -4 to 4
- embeds_m: float32 [10, 64], replicated, may hold values from -4.7683716e-07 to 4.7683716e-07
- embeds_v: float32 [10, 64], replicated, may hold values from 6.289751e-16 to 2.5159005e-15
- proj_one: float32 [64, 128], replicated, may hold values from -4 to 4
- proj_one_m: float32 [64, 128], replicated, may hold values from -4.7683716e-07 to 4.7683716e-07
- proj_one_v: float32 [64, 128], replicated, may hold values from 6.289751e-16 to 2.5159005e-15
- proj_two: float32 [128, 64], replicated, may hold values from -4 to 4
- proj_two_m: float32 [128, 64], replicated, may hold values from -4.7683716e-07 to 4.7683716e-07
- proj_two_v: float32 [128, 64], replicated, may hold values from 6.289751e-16 to 2.5159005e-15
- hyper: float32 [64, 24576], P(None, 'gen'), may hold values from -1 to 1
- hyper_m: float32 [64, 24576], P(None, 'gen'), may hold values from -4.7683716e-07 to 4.7683716e-07
- hyper_v: float32 [64, 24576], P(None, 'gen'), may hold values from 6.289751e-16 to 2.5159005e-15
Outputs:
- loss_sum: float32 [], replicated
- token_count: float32 [], replicated
- grad_norm: float32 [], replicated
- new_embeds: float32 [10, 64], replicated
- new_embeds_m: float32 [10, 64], replicated
- new_embeds_v: float32 [10, 64], replicated
- new_proj_one: float32 [64, 128], replicated
- new_proj_one_m: float32 [64, 128], replicated
- new_proj_one_v: float32 [64, 128], replicated
- new_proj_two: float32 [128, 64], replicated
- new_proj_two_m: float32 [128, 64], replicated
- new_proj_two_v: float32 [128, 64], replicated
- new_hyper: float32 [64, 24576], P(None, 'gen')
- new_hyper_m: float32 [64, 24576], P(None, 'gen')
- new_hyper_v: float32 [64, 24576], P(None, 'gen')
The draws below stay inside these ranges and needn't reach their ends.
Inputs may be any that keep to these rules, and one draw needn't show every extreme that they name: `task_len`: one task has exactly 256 input positions and another a quarter of 256. `tgt_count`: the counted positions of a sequence are its first ones; the first sequence counts a quarter of 128, the last all 128.
All inputs are finite; a program needn't handle non-finite values.
Results may differ from the reference program's by a relative error of at most 0.00215.
Values may be sent and summed in bfloat16 or wider, within the bound.
A program may use at most 192 MiB of HBM per device.

```python
import math
from functools import partial
import jax
import jax.numpy as jnp
from jax import lax

D = 512
HEADS = 8
FF = 2048
VOCAB = 32128
ADAPTER = 24
TASKS = 8
TASK_DIM = 64
PROJ_HIDDEN = 128
Z_DIM = 64
LAYERS = 2
SRC = 256
TGT = 128
STEP = 5
GEN_WIDTH = 24576
SEQ_DEV = 2
GROUP = 8
SEQS = 256


def draw_table(key, part):
    key = jax.random.fold_in(key, 1)
    position = jnp.arange(VOCAB, dtype=jnp.float32) / VOCAB
    scale = 1.0 + 2.0 * position
    values = jax.random.normal(key, (VOCAB, D), jnp.float32)
    return (values * scale[:, None]).astype(jnp.bfloat16)


def draw_task_len(key, part):
    key = jax.random.fold_in(key, 2)
    first, second = jax.random.split(key)
    lengths = jax.random.randint(first, (TASKS,), SRC // 4, SRC + 1)
    chosen = jax.random.randint(second, (), 0, TASKS)
    lengths = lengths.at[chosen].set(SRC)
    return lengths.at[(chosen + 1) % TASKS].set(SRC // 4)


def draw_tgt_count(key, part):
    key = jax.random.fold_in(key, 3)
    position = jnp.arange(SEQS)
    rank_dp = position // GROUP
    rank_gen = position % GROUP // SEQ_DEV
    last_dp = SEQS // GROUP - 1
    last_gen = GROUP // SEQ_DEV - 1
    rise = (rank_dp * last_gen + rank_gen * last_dp) * (TGT // 4) // (last_dp * last_gen)
    counts = TGT // 4 + rise + jax.random.randint(key, (SEQS,), 0, TGT // 8 + 1)
    counts = jnp.minimum(counts, TGT)
    return counts.at[0].set(TGT // 4).at[SEQS - 1].set(TGT)


def draw_tgt_ids(key, part):
    key = jax.random.fold_in(key, 4)
    first, second = jax.random.split(key)
    base = jax.random.randint(first, (SEQS, TGT), 0, VOCAB)
    base = base.at[0, 0].set(0).at[SEQS - 1, 0].set(VOCAB - 1)
    repeat = jax.random.randint(second, (SEQS, TGT), 0, 2)
    column = jnp.arange(TGT)[None, :] * jnp.ones((SEQS, 1), jnp.int32)
    fresh = jnp.where((repeat == 0) | (column == 0), column, 0)
    source = lax.cummax(fresh, axis=1)
    return jnp.take_along_axis(base, source, axis=1).astype(jnp.int32)


def draw_embeds(key, part):
    key = jax.random.fold_in(key, 5)
    shape = (TASKS + LAYERS, TASK_DIM)
    values = jnp.clip(jax.random.normal(key, shape, jnp.float32), -4.0, 4.0)
    return values


def draw_proj_one(key, part):
    key = jax.random.fold_in(key, 6)
    shape = (TASK_DIM, PROJ_HIDDEN)
    values = jnp.clip(jax.random.normal(key, shape, jnp.float32), -4.0, 4.0)
    return values * TASK_DIM ** (-0.5)


def draw_proj_two(key, part):
    key = jax.random.fold_in(key, 7)
    shape = (PROJ_HIDDEN, Z_DIM)
    values = jnp.clip(jax.random.normal(key, shape, jnp.float32), -4.0, 4.0)
    return values * PROJ_HIDDEN ** (-0.5)


def draw_hyper(key, part):
    key = jax.random.fold_in(key, 8)
    shape = (Z_DIM, GEN_WIDTH)
    values = jnp.clip(jax.random.normal(key, shape, jnp.float32), -4.0, 4.0)
    return values * (Z_DIM * D) ** (-0.5)


def set_ends(drawn, own_key, low, top_value):
    spot = [jax.random.randint(jax.random.fold_in(own_key, axis), (), 0, length) for axis, length in enumerate(drawn.shape)]
    widest = drawn.shape.index(max(drawn.shape))
    next_to = spot[:widest] + [(spot[widest] + 1) % drawn.shape[widest]] + spot[widest + 1:]
    return drawn.at[tuple(spot)].set(low).at[tuple(next_to)].set(top_value)


def steps_of(rng, extent, shards, smallest, high):
    loudness, own = 1.0, jax.random.fold_in(rng, 6)
    for dim, blocks in shards:
        heights = jnp.exp(jax.random.uniform(jax.random.fold_in(own, dim), (blocks,), jnp.float32, smallest / len(shards), high / len(shards)))
        loudness = loudness * jnp.repeat(heights, extent[dim] // blocks).reshape([-1 if axis == dim else 1 for axis in range(len(extent))])
    return loudness


def normal_values(own_key, shape, deviation, bound, cuts=(), held_as=jnp.bfloat16):
    factor_of = steps_of(own_key, shape, cuts, -0.22, 0.18) if cuts else 1.0
    array = jax.random.normal(own_key, shape, jnp.float32) * deviation * factor_of
    return jnp.minimum(jnp.maximum(array, -bound), bound).astype(held_as)


def setup_inputs(seed: int = 0) -> dict:
    key_list = jax.random.split(jax.random.key(seed), 23)
    src_ids = set_ends(jax.random.randint(key_list[0], (SEQS, SRC), 0, VOCAB), jax.random.fold_in(key_list[0], 1), 0, VOCAB - 1).astype(jnp.int32)
    tgt_ids = draw_tgt_ids(jax.random.fold_in(key_list[22], 71), 0)
    task_ids = set_ends(jax.random.randint(key_list[2], (SEQS,), 0, TASKS), jax.random.fold_in(key_list[2], 1), 0, TASKS - 1).astype(jnp.int32)
    task_len = draw_task_len(jax.random.fold_in(key_list[22], 71), 0)
    tgt_count = draw_tgt_count(jax.random.fold_in(key_list[22], 71), 0)
    table = draw_table(jax.random.fold_in(key_list[22], 71), 0)
    attn_w = normal_values(key_list[6], (3, D, 4 * D), D ** -0.5, 0.25)
    ffn_in = normal_values(key_list[7], (2, D, FF), D ** -0.5, 0.25)
    ffn_out = normal_values(key_list[8], (2, FF, D), FF ** -0.5, 0.125)
    gains = jnp.clip(1.0 + 0.1 * jax.random.normal(key_list[9], (7, D), jnp.float32), 0.5, 1.5)
    embeds = draw_embeds(jax.random.fold_in(key_list[22], 71), 0)
    embeds_m = normal_values(key_list[11], (TASKS + LAYERS, TASK_DIM), (0.11 * 0.001 / ((TASKS + LAYERS) * TASK_DIM + TASK_DIM * PROJ_HIDDEN + PROJ_HIDDEN * Z_DIM + Z_DIM * GEN_WIDTH) ** 0.5), 4.76837158203125e-07, (), jnp.float32)
    embeds_v = jnp.clip(jnp.exp(jax.random.uniform(key_list[12], (TASKS + LAYERS, TASK_DIM), jnp.float32, math.log(6.289751146537582e-16), math.log(2.515900458615033e-15))), 6.289751146537582e-16, 2.515900458615033e-15)
    proj_one = draw_proj_one(jax.random.fold_in(key_list[22], 71), 0)
    proj_one_m = normal_values(key_list[14], (TASK_DIM, PROJ_HIDDEN), (0.11 * 0.001 / ((TASKS + LAYERS) * TASK_DIM + TASK_DIM * PROJ_HIDDEN + PROJ_HIDDEN * Z_DIM + Z_DIM * GEN_WIDTH) ** 0.5), 4.76837158203125e-07, (), jnp.float32)
    proj_one_v = jnp.clip(jnp.exp(jax.random.uniform(key_list[15], (TASK_DIM, PROJ_HIDDEN), jnp.float32, math.log(6.289751146537582e-16), math.log(2.515900458615033e-15))), 6.289751146537582e-16, 2.515900458615033e-15)
    proj_two = draw_proj_two(jax.random.fold_in(key_list[22], 71), 0)
    proj_two_m = normal_values(key_list[17], (PROJ_HIDDEN, Z_DIM), (0.11 * 0.001 / ((TASKS + LAYERS) * TASK_DIM + TASK_DIM * PROJ_HIDDEN + PROJ_HIDDEN * Z_DIM + Z_DIM * GEN_WIDTH) ** 0.5), 4.76837158203125e-07, (), jnp.float32)
    proj_two_v = jnp.clip(jnp.exp(jax.random.uniform(key_list[18], (PROJ_HIDDEN, Z_DIM), jnp.float32, math.log(6.289751146537582e-16), math.log(2.515900458615033e-15))), 6.289751146537582e-16, 2.515900458615033e-15)
    hyper = draw_hyper(jax.random.fold_in(key_list[22], 71), 0)
    hyper_m = normal_values(key_list[20], (Z_DIM, GEN_WIDTH), (0.11 * 0.001 / ((TASKS + LAYERS) * TASK_DIM + TASK_DIM * PROJ_HIDDEN + PROJ_HIDDEN * Z_DIM + Z_DIM * GEN_WIDTH) ** 0.5), 4.76837158203125e-07, ((1, 4),), jnp.float32)
    hyper_v = jnp.clip(jnp.exp(math.log(2.515900458615033e-15) - 1.3862944 * jax.random.uniform(key_list[21], (Z_DIM, GEN_WIDTH), jnp.float32) ** steps_of(key_list[21], (Z_DIM, GEN_WIDTH), ((1, 4),), -0.2, 0.2)), 6.289751146537582e-16, 2.515900458615033e-15)
    return {"src_ids": src_ids, "tgt_ids": tgt_ids, "task_ids": task_ids, "task_len": task_len, "tgt_count": tgt_count, "table": table, "attn_w": attn_w, "ffn_in": ffn_in, "ffn_out": ffn_out, "gains": gains, "embeds": embeds, "embeds_m": embeds_m, "embeds_v": embeds_v, "proj_one": proj_one, "proj_one_m": proj_one_m, "proj_one_v": proj_one_v, "proj_two": proj_two, "proj_two_m": proj_two_m, "proj_two_v": proj_two_v, "hyper": hyper, "hyper_m": hyper_m, "hyper_v": hyper_v}


@jax.custom_vjp
def low(v):
    return lax.optimization_barrier(v.astype(jnp.bfloat16)).astype(jnp.float32)

@jax.custom_vjp
def low_back(v):
    return v

def low_keep(v):
    return (low(v), None)

def low_pass(kept, grad):
    return (grad,)

def back_keep(v):
    return (v, None)

def back_low(kept, grad):
    return (low(grad),)
low.defvjp(low_keep, low_pass)
low_back.defvjp(back_keep, back_low)
epsilon = 1e-06
clip_limit = 0.001
beta_one = 0.9
beta_two = 0.999
adam_floor = 1e-08
weight_decay = 0.01
rates = (0.5, 0.1, 0.1, 0.005)
blocked = -1000000000.0
highest = lax.Precision.HIGHEST

def both(value):
    return low_back(low(value))

def mix(form, left, right):
    return jnp.einsum(form, left, right, precision=highest)

def rmsnorm(value, gain):
    return value * lax.rsqrt(lax.optimization_barrier(jnp.mean(value * value, axis=-1, keepdims=True)) + epsilon) * gain

def heads_of(value):
    return value.reshape(value.shape[:2] + (HEADS, -1))

def attend(normed, source, weight, allowed):
    width = normed.shape[-1]
    scale = (width // HEADS) ** (-0.5)
    query = both(mix('btd,de->bte', normed, weight[:, :width]))
    keys = both(mix('btd,de->bte', source, weight[:, width:2 * width]))
    values = both(mix('btd,de->bte', source, weight[:, 2 * width:3 * width]))
    raw = mix('bqhd,bkhd->bhqk', heads_of(query), heads_of(keys)) * scale
    scores = jnp.where(allowed[:, None], low_back(raw), blocked)
    probs = low(jax.nn.softmax(scores, axis=-1))
    mixed = both(mix('bhqk,bkhd->bqhd', probs, heads_of(values)).reshape(normed.shape))
    return low_back(mix('btd,de->bte', mixed, weight[:, 3 * width:]))

def feed(state, gain, inner, outer, down, up):
    normed = low(rmsnorm(state, gain))
    hidden = low_back(mix('btd,df->btf', normed, inner))
    branch = low_back(mix('btf,fd->btd', low(jax.nn.gelu(hidden)), outer))
    lowered = low_back(mix('btd,bda->bta', low(branch), down))
    adapted = low_back(math.sqrt(D / ADAPTER) * mix('bta,bad->btd', low(jax.nn.gelu(lowered)), up))
    return state + branch + adapted

def sequences_loss(items, table, attn_w, ffn_in, ffn_out, gains):
    src, dec_in, targets, lengths, counts, adapters = items
    rows = src.shape[0]
    area = D * ADAPTER
    downs = adapters[:, :, :area].reshape(rows, LAYERS, D, ADAPTER)
    ups = adapters[:, :, area:].reshape(rows, LAYERS, ADAPTER, D)
    enc_allowed = jnp.arange(SRC)[None, None, :] < lengths[:, None, None]
    causal = (jnp.arange(TGT)[:, None] >= jnp.arange(TGT)[None, :])[None]
    state = table[src]
    normed = low(rmsnorm(state, gains[0]))
    state = state + attend(normed, normed, attn_w[0], enc_allowed)
    state = feed(state, gains[1], ffn_in[0], ffn_out[0], downs[:, 0], ups[:, 0])
    memory = low(rmsnorm(state, gains[2]))
    state = table[dec_in]
    normed = low(rmsnorm(state, gains[3]))
    state = state + attend(normed, normed, attn_w[1], causal)
    state = state + attend(low(rmsnorm(state, gains[4])), memory, attn_w[2], enc_allowed)
    state = feed(state, gains[5], ffn_in[1], ffn_out[1], downs[:, 1], ups[:, 1])
    final = low(rmsnorm(state, gains[6]))
    logits = low_back(mix('btd,vd->btv', final, table) * D ** (-0.5))
    logsum = jax.nn.logsumexp(logits, axis=-1)
    picked = jnp.take_along_axis(logits, targets[..., None], axis=-1)[..., 0]
    valid = (jnp.arange(TGT)[None] < counts[:, None]).astype(jnp.float32)
    return jnp.sum((logsum - picked) * valid)

def forward(trained, fixed):
    embeds, proj_one, proj_two, hyper = trained
    src_ids, tgt_ids, task_ids, task_len, tgt_count, table, attn_w, ffn_in, ffn_out, gains = fixed
    pairs = (embeds[:TASKS, None, :] + embeds[None, TASKS:, :]).reshape(TASKS * LAYERS, -1)
    coded = jnp.dot(jax.nn.gelu(jnp.dot(pairs, proj_one, precision=highest)), proj_two, precision=highest)
    generated = low(jnp.dot(coded, hyper, precision=highest))
    adapters = generated[task_ids[:, None] * LAYERS + jnp.arange(LAYERS)[None]]
    dec_in = jnp.concatenate([jnp.zeros_like(tgt_ids[:, :1]), tgt_ids[:, :-1]], axis=1)
    lengths = task_len[task_ids]
    per_block = 8

    def blocked_view(value):
        return value.reshape((-1, per_block) + value.shape[1:])
    items = tuple((blocked_view(value) for value in (src_ids, dec_in, tgt_ids, lengths, tgt_count, adapters)))
    piece_loss = jax.checkpoint(partial(sequences_loss, table=table, attn_w=attn_w, ffn_in=ffn_in, ffn_out=ffn_out, gains=gains))

    def accumulate(total, item):
        return (total + piece_loss(item), None)
    total, _ = lax.scan(accumulate, jnp.zeros((), jnp.float32), items)
    return total

def adamw(weight, first, second, grad, rate):
    first = beta_one * first + (1.0 - beta_one) * grad
    second = beta_two * second + (1.0 - beta_two) * grad * grad
    corrected = first / (1.0 - beta_one ** STEP)
    spread = jnp.sqrt(second / (1.0 - beta_two ** STEP)) + adam_floor
    return (weight - rate * (corrected / spread + weight_decay * weight), first, second)

def reference(src_ids, tgt_ids, task_ids, task_len, tgt_count, table, attn_w, ffn_in, ffn_out, gains, embeds, embeds_m, embeds_v, proj_one, proj_one_m, proj_one_v, proj_two, proj_two_m, proj_two_v, hyper, hyper_m, hyper_v):
    fixed = (src_ids, tgt_ids, task_ids, task_len, tgt_count, table.astype(jnp.float32), attn_w.astype(jnp.float32), ffn_in.astype(jnp.float32), ffn_out.astype(jnp.float32), gains)
    trained = (embeds, proj_one, proj_two, hyper)
    loss_sum, pullback = jax.vjp(lambda *weights: forward(weights, fixed), *trained)
    grads = pullback(jnp.ones((), jnp.float32))
    token_count = jnp.sum(tgt_count).astype(jnp.float32)
    grads = [grad / token_count for grad in grads]
    grad_norm = jnp.sqrt(sum((jnp.sum(grad * grad) for grad in grads)))
    factor = jnp.minimum(1.0, clip_limit / (grad_norm + 1e-06))
    firsts = (embeds_m, proj_one_m, proj_two_m, hyper_m)
    seconds = (embeds_v, proj_one_v, proj_two_v, hyper_v)
    updated = [adamw(trained[index], firsts[index], seconds[index], grads[index] * factor, rates[index]) for index in range(4)]
    return (loss_sum, token_count, grad_norm, updated[0][0], updated[0][1], updated[0][2], updated[1][0], updated[1][1], updated[1][2], updated[2][0], updated[2][1], updated[2][2], updated[3][0], updated[3][1], updated[3][2])
```

```python
import math

import jax
import jax.numpy as jnp
from jax import lax
from jax.experimental import pallas as pl
from jax.experimental.pallas import tpu as pltpu
from jax.sharding import PartitionSpec as P

D = 512
HEADS = 8
ADAPTER = 24
TASKS = 8
LAYERS = 2
SRC = 256
TGT = 128
FF = 2048
SEQ_DEV = 2
GEN = 4
LOW = 128
ROWS = 392
STEP = 5


epsilon = 1e-06
clip_limit = 0.001
beta_one = 0.9
beta_two = 0.999
adam_floor = 1e-08
weight_decay = 0.01
rates = (0.5, 0.1, 0.1, 0.005)
blocked = -1000000000.0
highest = lax.Precision.HIGHEST
LOGIT_SCALE = D ** (-0.5)
EXP_SCALE = LOGIT_SCALE / math.log(2.0)
UPSCALE = math.sqrt(D / ADAPTER)
GELU_A = math.sqrt(2.0 / math.pi)
GELU_B = 0.044715
VOCAB_TILE = 2048
MESH = pl.DeviceIdType.MESH


def adamw(weight, first, second, grad, rate):
    first = beta_one * first + (1.0 - beta_one) * grad
    second = beta_two * second + (1.0 - beta_two) * grad * grad
    corrected = first / (1.0 - beta_one**STEP)
    spread = jnp.sqrt(second / (1.0 - beta_two**STEP)) + adam_floor
    return (weight - rate * (corrected / spread + weight_decay * weight), first, second)


def encode(embed_rows, first, second):
    pairs = (embed_rows[:TASKS, None, :] + embed_rows[None, TASKS:, :]).reshape(TASKS * LAYERS, -1)
    return jnp.dot(jax.nn.gelu(jnp.dot(pairs, first, precision=highest)), second, precision=highest)


def mm(left, right):
    return lax.dot_general(
        left, right, (((1,), (0,)), ((), ())), preferred_element_type=jnp.float32
    )


def mm_last(left, right):
    return lax.dot_general(
        left, right, (((1,), (1,)), ((), ())), preferred_element_type=jnp.float32
    )


def mm_first(left, right):
    return lax.dot_general(
        left, right, (((0,), (0,)), ((), ())), preferred_element_type=jnp.float32
    )


def norm_scale(value):
    return lax.rsqrt(jnp.mean(value * value, axis=-1, keepdims=True) + epsilon)


def normed(value, gain):
    return (value * norm_scale(value) * gain).astype(jnp.bfloat16)


def norm_back(value, gain, grad):
    scale = norm_scale(value)
    weighted = grad * gain
    return scale * weighted - value * (
        scale * scale * scale * jnp.mean(weighted * value, axis=-1, keepdims=True)
    )


def gelu_tanh(value):
    return jnp.tanh(value * (GELU_A + (GELU_A * GELU_B) * (value * value)))


def gelu(value):
    return (0.5 * value) * (1.0 + gelu_tanh(value))


def gelu_slope(value, tanh):
    return 0.5 * (1.0 + tanh) + (0.5 * value) * (1.0 - tanh * tanh) * (
        GELU_A + (3.0 * GELU_A * GELU_B) * (value * value)
    )


def halves():
    lane = lax.broadcasted_iota(jnp.int32, (1, 128), 1)
    return [(lane // 64 == half) for half in range(2)]


def attend(q_ref, kv_ref, k_col, v_col, q_len, k_len, allow, out_ref, probs_ref=None):
    sides = halves()
    masks = [side.astype(jnp.float32).astype(jnp.bfloat16) for side in sides]

    def pair_step(pair, carry):
        lanes = pl.multiple_of(pair * 128, 128)
        for seq in range(SEQ_DEV):
            q_rows = pl.ds(seq * q_len, q_len)
            k_rows = pl.ds(seq * k_len, k_len)
            query = q_ref[q_rows, pl.ds(lanes, 128)]
            keys = kv_ref[k_rows, pl.ds(k_col + lanes, 128)]
            values = kv_ref[k_rows, pl.ds(v_col + lanes, 128)]
            outs = []
            for half in range(2):
                scores = mm_last(query * masks[half], keys) * 0.125
                scores = jnp.where(allow(seq), scores, blocked)
                peak = jnp.max(scores, axis=-1, keepdims=True)
                weights = jnp.exp(scores - peak)
                probs = weights * (1.0 / jnp.sum(weights, axis=-1, keepdims=True))
                if probs_ref is not None:
                    probs_ref[(pair * SEQ_DEV + seq) * 2 + half] = probs
                outs.append(mm(probs.astype(jnp.bfloat16), values))
            out_ref[q_rows, pl.ds(lanes, 128)] = jnp.where(sides[0], outs[0], outs[1]).astype(
                jnp.bfloat16
            )
        return carry

    lax.fori_loop(0, HEADS // 2, pair_step, 0)


def attend_back(grad_ref, q_ref, kv_ref, probs_ref, q_len, k_len, joined_ref):
    sides = halves()
    masks = [side.astype(jnp.float32).astype(jnp.bfloat16) for side in sides]

    def pair_step(pair, carry):
        lanes = pl.multiple_of(pair * 128, 128)
        for seq in range(SEQ_DEV):
            q_rows = pl.ds(seq * q_len, q_len)
            k_rows = pl.ds(seq * k_len, k_len)
            grad = grad_ref[q_rows, pl.ds(lanes, 128)]
            query = q_ref[q_rows, pl.ds(lanes, 128)]
            values = kv_ref[k_rows, pl.ds(D + lanes, 128)]
            key_grads, value_grads = [], []
            for half in range(2):
                probs = probs_ref[(pair * SEQ_DEV + seq) * 2 + half]
                grad_probs = mm_last(grad * masks[half], values)
                value_grads.append(mm_first(probs.astype(jnp.bfloat16), grad))
                inner = jnp.sum(grad_probs * probs, axis=-1, keepdims=True)
                grad_scores = (probs * (grad_probs - inner)).astype(jnp.bfloat16)
                key_grads.append(mm_first(grad_scores, query))
            joined_ref[k_rows, pl.ds(lanes, 128)] = (
                jnp.where(sides[0], key_grads[0], key_grads[1]) * 0.125
            ).astype(jnp.bfloat16)
            joined_ref[k_rows, pl.ds(D + lanes, 128)] = jnp.where(
                sides[0], value_grads[0], value_grads[1]
            ).astype(jnp.bfloat16)
        return carry

    lax.fori_loop(0, HEADS // 2, pair_step, 0)


def feed(state_ref, gain, inner_ref, outer_ref, act_ref, slope_ref, down_ref, up_ref, length,
         plain_ref, low_ref, after_ref):
    rows = SEQ_DEV * length
    act_rows = pl.ds(0, rows)
    source = normed(state_ref[...], gain)
    for block in range(FF // D):
        columns = slice(block * D, (block + 1) * D)
        hidden = mm(source, inner_ref[:, columns])
        tanh = gelu_tanh(hidden)
        act_ref[act_rows, columns] = ((0.5 * hidden) * (1.0 + tanh)).astype(jnp.bfloat16)
        if slope_ref is not None:
            slope_ref[:, columns] = gelu_slope(hidden, tanh)
    branch = mm(act_ref[act_rows, :], outer_ref[...])
    plain_ref[...] = branch.astype(jnp.bfloat16)
    for seq in range(SEQ_DEV):
        span = slice(seq * length, (seq + 1) * length)
        lowered = mm(plain_ref[span, :], down_ref[seq])
        low_ref[span, :] = lowered
        adapted = mm(gelu(lowered).astype(jnp.bfloat16), up_ref[seq]) * UPSCALE
        after_ref[span, :] = state_ref[span, :] + branch[span, :] + adapted


def adapter_back(grad_ref, low_ref, plain_ref, down_ref, up_ref, length, grad_down_ref,
                 grad_up_ref, branch_ref=None):
    for seq in range(SEQ_DEV):
        span = slice(seq * length, (seq + 1) * length)
        grad = grad_ref[span, :]
        grad_low = grad.astype(jnp.bfloat16)
        lowered = low_ref[span, :]
        tanh = gelu_tanh(lowered)
        bottleneck = ((0.5 * lowered) * (1.0 + tanh)).astype(jnp.bfloat16)
        grad_bottle = mm_last(grad_low, up_ref[seq]) * UPSCALE
        grad_up_ref[seq] = mm_first(bottleneck, grad_low)[:ADAPTER] * UPSCALE
        grad_lowered = (grad_bottle * gelu_slope(lowered, tanh)).astype(jnp.bfloat16)
        grad_down_ref[seq] = mm_first(plain_ref[span, :], grad_lowered)
        if branch_ref is not None:
            branch_ref[span, :] = (grad + mm_last(grad_lowered, down_ref[seq])).astype(
                jnp.bfloat16
            )


def step_kernel(
    rows_ref,
    down_ref,
    up_ref,
    allow_ref,
    valid_ref,
    gains_ref,
    attn_hbm,
    inner_hbm,
    outer_hbm,
    table_hbm,
    grad_down_ref,
    grad_up_ref,
    loss_ref,
    attn,
    inner,
    outer,
    table,
    state,
    after_e,
    plain_e,
    low_e,
    qkv,
    mixed,
    act,
    memory,
    y1,
    y2,
    y3,
    q_cross,
    kv_cross,
    probs,
    slope,
    plain_d,
    low_d,
    feats,
    total,
    results,
    arrived,
    stats,
    stats_in,
    grad,
    grad_low,
    joined,
    load_sem,
    feat_send,
    feat_recv,
    result_send,
    result_recv,
    stat_send,
    stat_recv,
):
    member = lax.axis_index("gen")
    barrier = pltpu.get_barrier_semaphore()

    def peer(order):
        chip = lax.rem(member // 2 + lax.rem((order + 1) // 2, 2), 2)
        return chip * 2 + lax.rem(lax.rem(member, 2) + order // 2, 2)

    for order in range(1, GEN):
        pl.semaphore_signal(
            barrier, inc=1, device_id={"gen": peer(order)}, device_id_type=MESH
        )

    loads = []
    for source, target in (
        (attn_hbm.at[0], attn.at[0]),
        (inner_hbm.at[0], inner.at[0]),
        (outer_hbm.at[0], outer.at[0]),
        (attn_hbm.at[1], attn.at[1]),
        (attn_hbm.at[2], attn.at[2]),
        (inner_hbm.at[1], inner.at[1]),
        (outer_hbm.at[1], outer.at[1]),
        (table_hbm, table),
    ):
        loads.append(pltpu.make_async_copy(source, target, load_sem.at[len(loads)]))
        loads[-1].start()

    embedded = jnp.concatenate([rows_ref[seq, :SRC] for seq in range(SEQ_DEV)], axis=0).astype(
        jnp.float32
    )
    entry = normed(embedded, gains_ref[0:1])
    loads[0].wait()
    for block in range(3):
        columns = slice(block * D, (block + 1) * D)
        qkv[:, columns] = mm(entry, attn[0, :, columns]).astype(jnp.bfloat16)
    attend(qkv, qkv, D, 2 * D, SRC, SRC, lambda seq: allow_ref[seq : seq + 1, :] > 0.0, mixed)
    state[...] = embedded + mm(mixed[...], attn[0, :, 3 * D :])
    loads[1].wait()
    loads[2].wait()
    feed(state, gains_ref[1:2], inner.at[0], outer.at[0], act, None, down_ref.at[0], up_ref.at[0],
         SRC, plain_e, low_e, after_e)
    memory[...] = normed(after_e[...], gains_ref[2:3])

    targets = SEQ_DEV * TGT
    inputs = jnp.concatenate(
        [rows_ref[seq, SRC : SRC + TGT] for seq in range(SEQ_DEV)], axis=0
    ).astype(jnp.float32)
    entry = normed(inputs, gains_ref[3:4])
    loads[3].wait()
    own = pl.ds(0, targets)
    for block in range(3):
        columns = slice(block * D, (block + 1) * D)
        qkv[own, columns] = mm(entry, attn[1, :, columns]).astype(jnp.bfloat16)
    causal = lax.broadcasted_iota(jnp.int32, (TGT, TGT), 0) >= lax.broadcasted_iota(
        jnp.int32, (TGT, TGT), 1
    )
    attend(qkv, qkv, D, 2 * D, TGT, TGT, lambda seq: causal, mixed)
    y1[...] = inputs + mm(mixed[own, :], attn[1, :, 3 * D :])
    loads[4].wait()
    q_cross[...] = mm(normed(y1[...], gains_ref[4:5]), attn[2, :, :D]).astype(jnp.bfloat16)
    for block in range(2):
        columns = slice(block * D, (block + 1) * D)
        kv_cross[:, columns] = mm(
            memory[...], attn[2, :, (block + 1) * D : (block + 2) * D]
        ).astype(jnp.bfloat16)
    attend(q_cross, kv_cross, 0, D, TGT, SRC, lambda seq: allow_ref[seq : seq + 1, :] > 0.0,
           mixed, probs)
    y2[...] = y1[...] + mm(mixed[own, :], attn[2, :, 3 * D :])
    loads[5].wait()
    loads[6].wait()
    feed(y2, gains_ref[5:6], inner.at[1], outer.at[1], act, slope, down_ref.at[1], up_ref.at[1],
         TGT, plain_d, low_d, y3)
    feats[0] = normed(y3[...], gains_ref[6:7])

    pl.semaphore_wait(barrier, GEN - 1)

    def feature_copy(order):
        return pltpu.make_async_remote_copy(
            src_ref=feats.at[0],
            dst_ref=feats.at[order],
            send_sem=feat_send.at[order],
            recv_sem=feat_recv.at[order],
            device_id={"gen": peer(order)},
            device_id_type=MESH,
        )

    def result_copy(order):
        return pltpu.make_async_remote_copy(
            src_ref=results.at[order],
            dst_ref=arrived.at[order],
            send_sem=result_send.at[order],
            recv_sem=result_recv.at[order],
            device_id={"gen": peer(order)},
            device_id_type=MESH,
        )

    def stat_copy(order):
        return pltpu.make_async_remote_copy(
            src_ref=stats.at[order],
            dst_ref=stats_in.at[order],
            send_sem=stat_send.at[order],
            recv_sem=stat_recv.at[order],
            device_id={"gen": peer(order)},
            device_id_type=MESH,
        )

    for order in range(1, GEN):
        feature_copy(order).start()
    loads[7].wait()
    same = lax.broadcasted_iota(jnp.int32, (targets, targets), 0) == lax.broadcasted_iota(
        jnp.int32, (targets, targets), 1
    )

    def as_row(column):
        return jnp.sum(jnp.where(same, column, 0.0), axis=0, keepdims=True)

    def as_column(row):
        return jnp.sum(jnp.where(same, row, 0.0), axis=1, keepdims=True)

    def block_step(order, carry):
        @pl.when(order > 0)
        def _():
            feature_copy(order).wait_recv()

        query = feats[order]
        ends = list(range(0, table.shape[0], VOCAB_TILE)) + [table.shape[0]]
        tiles = [(ends[i], ends[i + 1]) for i in range(len(ends) - 1)]
        peak = scale = None
        scores = mm_last(query, table[tiles[0][0] : tiles[0][1], :])
        for index, (first, last) in enumerate(tiles):
            following = None
            if index + 1 < len(tiles):
                following = mm_last(query, table[tiles[index + 1][0] : tiles[index + 1][1], :])
            top = jnp.max(scores, axis=-1, keepdims=True)
            if index > 0:
                top = jnp.maximum(peak, top)
            weights = jnp.exp2((scores - top) * EXP_SCALE)
            amount = jnp.sum(weights, axis=-1, keepdims=True)
            part = mm(weights.astype(jnp.bfloat16), table[first:last, :])
            if index == 0:
                total[...] = part
                scale = amount
            else:
                shrink = jnp.exp2((peak - top) * EXP_SCALE)
                total[...] = total[...] * shrink + part
                scale = scale * shrink + amount
            peak, scores = top, following
        results[order] = total[...].astype(jnp.bfloat16)
        stats[order] = jnp.concatenate(
            [as_row(peak), as_row(scale), jnp.zeros((6, targets), jnp.float32)], axis=0
        )

        @pl.when(order > 0)
        def _():
            result_copy(order).start()
            stat_copy(order).start()

        return carry

    lax.fori_loop(0, GEN, block_step, 0)
    stats_in[0] = stats[0]
    for order in range(1, GEN):
        stat_copy(order).wait_recv()
    peaks = [as_column(stats_in[order, 0:1, :]) for order in range(GEN)]
    sums = [as_column(stats_in[order, 1:2, :]) for order in range(GEN)]
    top = jnp.maximum(jnp.maximum(peaks[0], peaks[1]), jnp.maximum(peaks[2], peaks[3]))
    shares = [jnp.exp2((peaks[order] - top) * EXP_SCALE) for order in range(GEN)]
    amount = sum(shares[order] * sums[order] for order in range(GEN))
    logsum = top * LOGIT_SCALE + jnp.log(amount)
    inverse = 1.0 / amount
    expected = total_rows = None
    total[...] = results[0].astype(jnp.float32) * (shares[0] * inverse)
    for order in range(1, GEN):
        result_copy(order).wait_recv()
        total[...] = total[...] + arrived[order].astype(jnp.float32) * (shares[order] * inverse)
    wanted = jnp.concatenate(
        [
            rows_ref[seq, SRC : SRC + TGT + 8].astype(jnp.float32)[1 : TGT + 1]
            for seq in range(SEQ_DEV)
        ],
        axis=0,
    )
    picked = jnp.sum(feats[0].astype(jnp.float32) * wanted, axis=-1, keepdims=True) * LOGIT_SCALE
    counted = valid_ref[:, 0:1]
    loss = jnp.sum((logsum - picked) * counted, axis=0, keepdims=True)
    loss_ref[...] = jnp.broadcast_to(loss, (8, 128))

    grad[own, :] = norm_back(
        y3[...], gains_ref[6:7], (total[...] - wanted) * (counted * LOGIT_SCALE)
    )
    adapter_back(grad.at[own], low_d, plain_d, down_ref.at[1], up_ref.at[1], TGT,
                 grad_down_ref.at[1], grad_up_ref.at[1], grad_low)
    for block in range(FF // D):
        columns = slice(block * D, (block + 1) * D)
        act[own, columns] = (
            mm_last(grad_low[...], outer[1, columns, :]) * slope[:, columns]
        ).astype(jnp.bfloat16)
    grad_entry = mm_last(act[own, :], inner[1])
    grad_state = grad[own, :] + norm_back(y2[...], gains_ref[5:6], grad_entry)
    mixed[own, :] = mm_last(grad_state.astype(jnp.bfloat16), attn[2, :, 3 * D :]).astype(
        jnp.bfloat16
    )
    attend_back(mixed, q_cross, kv_cross, probs, TGT, SRC, joined)
    grad_memory = mm_last(joined[...], attn[2, :, D : 3 * D])

    grad[...] = norm_back(after_e[...], gains_ref[2:3], grad_memory)
    adapter_back(grad, low_e, plain_e, down_ref.at[0], up_ref.at[0], SRC,
                 grad_down_ref.at[0], grad_up_ref.at[0])
    for order in range(1, GEN):
        feature_copy(order).wait_send()
        result_copy(order).wait_send()
        stat_copy(order).wait_send()


def step(rows, down, up, allow, valid, gains, attn_w, ffn_in, ffn_out, table):
    vmem = pl.BlockSpec(memory_space=pltpu.VMEM)
    whole = pl.BlockSpec(memory_space=pl.ANY)
    low, full = jnp.bfloat16, jnp.float32
    sources, targets = SEQ_DEV * SRC, SEQ_DEV * TGT
    return pl.pallas_call(
        step_kernel,
        out_shape=(
            jax.ShapeDtypeStruct((LAYERS, SEQ_DEV, D, LOW), full),
            jax.ShapeDtypeStruct((LAYERS, SEQ_DEV, ADAPTER, D), full),
            jax.ShapeDtypeStruct((8, 128), full),
        ),
        in_specs=[vmem] * 6 + [whole] * 4,
        out_specs=(vmem, vmem, vmem),
        scratch_shapes=[
            pltpu.VMEM(attn_w.shape, low),
            pltpu.VMEM(ffn_in.shape, low),
            pltpu.VMEM(ffn_out.shape, low),
            pltpu.VMEM(table.shape, low),
            pltpu.VMEM((sources, D), full),
            pltpu.VMEM((sources, D), full),
            pltpu.VMEM((sources, D), low),
            pltpu.VMEM((sources, LOW), full),
            pltpu.VMEM((sources, 3 * D), low),
            pltpu.VMEM((sources, D), low),
            pltpu.VMEM((sources, FF), low),
            pltpu.VMEM((sources, D), low),
            pltpu.VMEM((targets, D), full),
            pltpu.VMEM((targets, D), full),
            pltpu.VMEM((targets, D), full),
            pltpu.VMEM((targets, D), low),
            pltpu.VMEM((sources, 2 * D), low),
            pltpu.VMEM((SEQ_DEV * HEADS, TGT, SRC), full),
            pltpu.VMEM((targets, FF), full),
            pltpu.VMEM((targets, D), low),
            pltpu.VMEM((targets, LOW), full),
            pltpu.VMEM((GEN, targets, D), low),
            pltpu.VMEM((targets, D), full),
            pltpu.VMEM((GEN, targets, D), low),
            pltpu.VMEM((GEN, targets, D), low),
            pltpu.VMEM((GEN, 8, targets), full),
            pltpu.VMEM((GEN, 8, targets), full),
            pltpu.VMEM((sources, D), full),
            pltpu.VMEM((targets, D), low),
            pltpu.VMEM((sources, 2 * D), low),
            pltpu.SemaphoreType.DMA((8,)),
            pltpu.SemaphoreType.DMA((GEN,)),
            pltpu.SemaphoreType.DMA((GEN,)),
            pltpu.SemaphoreType.DMA((GEN,)),
            pltpu.SemaphoreType.DMA((GEN,)),
            pltpu.SemaphoreType.DMA((GEN,)),
            pltpu.SemaphoreType.DMA((GEN,)),
        ],
        compiler_params=pltpu.CompilerParams(
            collective_id=1, has_side_effects=True, vmem_limit_bytes=60 * 1024 * 1024
        ),
        name="forward_vocab_backward",
    )(rows, down, up, allow, valid, gains, attn_w, ffn_in, ffn_out, table)


def sum_kernel(
    slots_ref,
    totals_ref,
    coded_ref,
    hyper_ref,
    out_ref,
    small_ref,
    outgoing,
    incoming,
    shares,
    outgoing_small,
    incoming_small,
    send_sem,
    recv_sem,
    share_send_sem,
    share_recv_sem,
    small_send_sem,
    small_recv_sem,
):
    rank = lax.axis_index("dp")
    count = outgoing.shape[0]
    width = shares.shape[2]
    per_half = slots_ref.shape[1] // width
    member = lax.axis_index("gen")
    barrier = pltpu.get_barrier_semaphore()

    def greet(step, carry):
        pl.semaphore_signal(
            barrier, inc=1, device_id={"dp": lax.rem(rank + step, count)}, device_id_type=MESH
        )
        return carry

    lax.fori_loop(1, count, greet, 0)
    for step in range(1, GEN):
        pl.semaphore_signal(
            barrier, inc=1, device_id={"gen": lax.rem(member + step, GEN)}, device_id_type=MESH
        )
    for piece in range(count):
        row, column = piece // per_half * 8, piece % per_half * width
        outgoing[piece, :, :width] = slots_ref[row : row + 8, column : column + width]
        outgoing[piece, :, width:] = totals_ref[...]
    pl.semaphore_wait(barrier, count + GEN - 2)

    def scatter_to(step):
        target = lax.rem(rank + step, count)
        return pltpu.make_async_remote_copy(
            src_ref=outgoing.at[target],
            dst_ref=incoming.at[rank],
            send_sem=send_sem.at[target],
            recv_sem=recv_sem.at[rank],
            device_id={"dp": target},
            device_id_type=MESH,
        )

    def scatter_from(step):
        source = lax.rem(rank + step, count)
        return pltpu.make_async_remote_copy(
            src_ref=outgoing.at[source],
            dst_ref=incoming.at[source],
            send_sem=send_sem.at[source],
            recv_sem=recv_sem.at[source],
            device_id={"dp": source},
            device_id_type=MESH,
        )

    def share_to(step):
        target = lax.rem(rank + step, count)
        return pltpu.make_async_remote_copy(
            src_ref=shares.at[rank],
            dst_ref=shares.at[rank],
            send_sem=share_send_sem.at[target],
            recv_sem=share_recv_sem.at[rank],
            device_id={"dp": target},
            device_id_type=MESH,
        )

    def share_from(step):
        source = lax.rem(rank + step, count)
        return pltpu.make_async_remote_copy(
            src_ref=shares.at[rank],
            dst_ref=shares.at[source],
            send_sem=share_send_sem.at[source],
            recv_sem=share_recv_sem.at[source],
            device_id={"dp": source},
            device_id_type=MESH,
        )

    def each(make, act):
        def body(step, carry):
            act(make(step))
            return carry

        lax.fori_loop(1, count, body, 0)

    each(scatter_to, lambda copy: copy.start())
    incoming[rank] = outgoing[rank]
    each(scatter_from, lambda copy: copy.wait_recv())
    summed = incoming[0]
    for source in range(1, count):
        summed = summed + incoming[source]
    shares[rank] = summed[:, :width]
    each(share_to, lambda copy: copy.start())
    each(scatter_to, lambda copy: copy.wait_send())
    each(share_from, lambda copy: copy.wait_recv())
    for piece in range(count):
        row, column = piece // per_half * 8, piece % per_half * width
        out_ref[row : row + 8, column : column + width] = shares[piece]
    slots = out_ref[...]
    coded_part = lax.dot_general(
        slots, hyper_ref[...], (((1,), (1,)), ((), ())), precision=highest,
        preferred_element_type=jnp.float32,
    )
    hyper_grad = lax.dot_general(
        coded_ref[...], slots, (((0,), (0,)), ((), ())), precision=highest,
        preferred_element_type=jnp.float32,
    )
    square = jnp.sum(hyper_grad * hyper_grad, axis=0, keepdims=True)
    outgoing_small[0:16, :] = jnp.concatenate(
        [coded_part, jnp.zeros((16, 64), jnp.float32)], axis=1
    )
    outgoing_small[16:24, :] = jnp.broadcast_to(
        jnp.sum(square, axis=1, keepdims=True), (8, 128)
    )
    outgoing_small[24:32, :] = summed[:, width:]
    copies = [
        pltpu.make_async_remote_copy(
            src_ref=outgoing_small,
            dst_ref=incoming_small.at[member],
            send_sem=small_send_sem.at[step],
            recv_sem=small_recv_sem.at[step],
            device_id={"gen": lax.rem(member + step, GEN)},
            device_id_type=MESH,
        )
        for step in range(1, GEN)
    ]
    for copy in copies:
        copy.start()
    incoming_small[member] = outgoing_small[...]
    each(share_to, lambda copy: copy.wait_send())
    for copy in copies:
        copy.wait()
    small_ref[...] = (incoming_small[0] + incoming_small[1]) + (
        incoming_small[2] + incoming_small[3]
    )


def summed_over_devices(slots, totals, coded, hyper):
    vmem = pl.BlockSpec(memory_space=pltpu.VMEM)
    count = lax.axis_size("dp")
    width = slots.shape[0] * slots.shape[1] // (8 * count)
    return pl.pallas_call(
        sum_kernel,
        out_shape=(
            jax.ShapeDtypeStruct(slots.shape, jnp.float32),
            jax.ShapeDtypeStruct((32, 128), jnp.float32),
        ),
        in_specs=[vmem] * 4,
        out_specs=(vmem, vmem),
        scratch_shapes=[
            pltpu.VMEM((count, 8, width + 128), jnp.float32),
            pltpu.VMEM((count, 8, width + 128), jnp.float32),
            pltpu.VMEM((count, 8, width), jnp.float32),
            pltpu.VMEM((32, 128), jnp.float32),
            pltpu.VMEM((GEN, 32, 128), jnp.float32),
            pltpu.SemaphoreType.DMA((count,)),
            pltpu.SemaphoreType.DMA((count,)),
            pltpu.SemaphoreType.DMA((count,)),
            pltpu.SemaphoreType.DMA((count,)),
            pltpu.SemaphoreType.DMA((GEN,)),
            pltpu.SemaphoreType.DMA((GEN,)),
        ],
        compiler_params=pltpu.CompilerParams(
            collective_id=0, has_side_effects=True, vmem_limit_bytes=32 * 1024 * 1024
        ),
        name="sum_over_devices",
    )(slots, totals, coded, hyper)


def per_device(
    src_ids,
    tgt_ids,
    task_ids,
    task_len,
    tgt_count,
    table,
    attn_w,
    ffn_in,
    ffn_out,
    gains,
    embeds,
    embeds_m,
    embeds_v,
    proj_one,
    proj_one_m,
    proj_one_v,
    proj_two,
    proj_two_m,
    proj_two_v,
    hyper,
    hyper_m,
    hyper_v,
):
    groups = lax.axis_size("gen")
    member = lax.axis_index("gen")
    vocab_part = table.shape[0]
    offset = member * vocab_part
    area = D * ADAPTER
    coded, pullback = jax.vjp(encode, embeds, proj_one, proj_two)
    generated = jnp.dot(coded, hyper, precision=highest)
    sequences = groups * SEQ_DEV
    tokens = jnp.concatenate(
        [src_ids, jnp.zeros_like(tgt_ids[:, :1]), tgt_ids, jnp.zeros_like(tgt_ids[:, :7])], axis=1
    ).reshape(-1)
    token = tokens - offset
    inside = (token >= 0) & (token < vocab_part)
    rows = jnp.take(table, jnp.clip(token, 0, vocab_part - 1), axis=0)
    rows = lax.psum_scatter(
        jnp.where(inside[:, None], rows, jnp.zeros_like(rows)),
        "gen",
        scatter_dimension=0,
        tiled=True,
    ).reshape(SEQ_DEV, ROWS, -1)
    row_index = (task_ids[:, None] * LAYERS + jnp.arange(LAYERS)[None]).reshape(-1)
    select = (row_index[:, None] == jnp.arange(TASKS * LAYERS)[None]).astype(jnp.float32)
    piece = jnp.dot(select, generated, precision=highest).astype(jnp.bfloat16)
    adapters = lax.all_to_all(piece, "gen", split_axis=0, concat_axis=1, tiled=True).reshape(
        SEQ_DEV, LAYERS, -1
    )
    adapters = adapters.transpose(1, 0, 2)
    down = jnp.pad(
        adapters[..., :area].reshape(LAYERS, SEQ_DEV, D, ADAPTER),
        ((0, 0), (0, 0), (0, 0), (0, LOW - ADAPTER)),
    )
    up = jnp.pad(
        adapters[..., area:].reshape(LAYERS, SEQ_DEV, ADAPTER, D),
        ((0, 0), (0, 0), (0, LOW - ADAPTER), (0, 0)),
    )
    lengths = jnp.sum(jnp.where(task_ids[:, None] == jnp.arange(TASKS)[None], task_len[None], 0), axis=1)
    own_len = lax.dynamic_slice_in_dim(lengths, member * SEQ_DEV, SEQ_DEV)
    own_count = lax.dynamic_slice_in_dim(tgt_count, member * SEQ_DEV, SEQ_DEV)
    allow = (jnp.arange(SRC)[None, :] < own_len[:, None]).astype(jnp.float32)
    allow = jnp.pad(allow, ((0, 8 - SEQ_DEV), (0, 0)))
    valid = (jnp.arange(TGT)[None] < own_count[:, None]).reshape(-1, 1).astype(jnp.float32)
    valid = jnp.broadcast_to(valid, (SEQ_DEV * TGT, 128))
    gains = jnp.pad(gains, ((0, 1), (0, 0)))
    grad_down, grad_up, loss = step(
        rows, down, up, allow, valid, gains, attn_w, ffn_in, ffn_out, table
    )
    grad_rows = jnp.concatenate(
        [
            grad_down[..., :ADAPTER].reshape(LAYERS, SEQ_DEV, -1),
            grad_up.reshape(LAYERS, SEQ_DEV, -1),
        ],
        axis=-1,
    )
    grad_rows = grad_rows.transpose(1, 0, 2).reshape(SEQ_DEV * LAYERS, -1)
    returned = lax.all_to_all(grad_rows, "gen", split_axis=1, concat_axis=0, tiled=True)
    slots = jnp.dot(select.T, returned, precision=highest)
    count_local = jnp.sum(own_count).astype(jnp.float32)
    lane = lax.broadcasted_iota(jnp.int32, (8, 128), 1)
    totals = jnp.where(lane == 0, loss, jnp.where(lane == 1, count_local, 0.0))
    slots, small = summed_over_devices(slots, totals, coded, hyper)
    coded_grad = small[:16, :64]
    hyper_square = small[16, 0]
    loss_sum = small[24, 0]
    token_count = small[24, 1]
    hyper_grad = jnp.dot(coded.T, slots, precision=highest)
    grad_embeds, grad_one, grad_two = pullback(coded_grad)
    count_scale = 1.0 / token_count
    grads = [grad * count_scale for grad in (grad_embeds, grad_one, grad_two, hyper_grad)]
    square = (
        hyper_square * count_scale * count_scale
        + jnp.sum(grads[0] * grads[0])
        + jnp.sum(grads[1] * grads[1])
        + jnp.sum(grads[2] * grads[2])
    )
    grad_norm = jnp.sqrt(square)
    factor = jnp.minimum(1.0, clip_limit / (grad_norm + 1e-06))
    weights = (embeds, proj_one, proj_two, hyper)
    firsts = (embeds_m, proj_one_m, proj_two_m, hyper_m)
    seconds = (embeds_v, proj_one_v, proj_two_v, hyper_v)
    updated = [
        adamw(weights[index], firsts[index], seconds[index], grads[index] * factor, rates[index])
        for index in range(4)
    ]
    return (
        loss_sum,
        token_count,
        grad_norm,
        updated[0][0],
        updated[0][1],
        updated[0][2],
        updated[1][0],
        updated[1][1],
        updated[1][2],
        updated[2][0],
        updated[2][1],
        updated[2][2],
        updated[3][0],
        updated[3][1],
        updated[3][2],
    )


def solution(mesh):
    return jax.shard_map(
        per_device,
        mesh=mesh,
        in_specs=(
            P("dp", None),
            P("dp", None),
            P("dp"),
            P(),
            P("dp"),
            P("gen", None),
            P(),
            P(),
            P(),
            P(),
            P(),
            P(),
            P(),
            P(),
            P(),
            P(),
            P(),
            P(),
            P(),
            P(None, "gen"),
            P(None, "gen"),
            P(None, "gen"),
        ),
        out_specs=(
            P(),
            P(),
            P(),
            P(),
            P(),
            P(),
            P(),
            P(),
            P(),
            P(),
            P(),
            P(),
            P(None, "gen"),
            P(None, "gen"),
            P(None, "gen"),
        ),
        check_vma=False,
    )
```

```python
import math

import jax
import jax.numpy as jnp
from jax import lax
from jax.experimental import pallas as pl
from jax.experimental.pallas import tpu as pltpu
from jax.sharding import PartitionSpec as P

D = 512
HEADS = 8
ADAPTER = 24
TASKS = 8
LAYERS = 2
SRC = 256
TGT = 128
FF = 2048
SEQ_DEV = 2
GEN = 4
LOW = 128
SRC_CAP = 176
TGT_CAP = 128
TGT_ROWS = TGT_CAP + 16
FLAT = 48
STEP = 5


epsilon = 1e-06
clip_limit = 0.001
beta_one = 0.9
beta_two = 0.999
adam_floor = 1e-08
weight_decay = 0.01
rates = (0.5, 0.1, 0.1, 0.005)
blocked = -1000000000.0
highest = lax.Precision.HIGHEST
LOGIT_SCALE = D ** (-0.5)
EXP_SCALE = LOGIT_SCALE / math.log(2.0)
UPSCALE = math.sqrt(D / ADAPTER)
GELU_A = math.sqrt(2.0 / math.pi)
GELU_B = 0.044715
VOCAB_TILE = 2048
UPDATE_STEPS = 6
MESH = pl.DeviceIdType.MESH


def adamw(weight, first, second, grad, rate):
    first = beta_one * first + (1.0 - beta_one) * grad
    second = beta_two * second + (1.0 - beta_two) * grad * grad
    corrected = first / (1.0 - beta_one**STEP)
    spread = jnp.sqrt(second / (1.0 - beta_two**STEP)) + adam_floor
    return (weight - rate * (corrected / spread + weight_decay * weight), first, second)


def mm(left, right):
    return lax.dot_general(
        left, right, (((1,), (0,)), ((), ())), preferred_element_type=jnp.float32
    )


def mm_last(left, right):
    return lax.dot_general(
        left, right, (((1,), (1,)), ((), ())), preferred_element_type=jnp.float32
    )


def mm_first(left, right):
    return lax.dot_general(
        left, right, (((0,), (0,)), ((), ())), preferred_element_type=jnp.float32
    )


def exact(left, right, dims):
    return lax.dot_general(
        left, right, (dims, ((), ())), precision=highest, preferred_element_type=jnp.float32
    )


def norm_scale(value):
    return lax.rsqrt(jnp.mean(value * value, axis=-1, keepdims=True) + epsilon)


def normed(value, gain):
    return (value * norm_scale(value) * gain).astype(jnp.bfloat16)


def norm_back(value, gain, grad):
    scale = norm_scale(value)
    weighted = grad * gain
    return scale * weighted - value * (
        scale * scale * scale * jnp.mean(weighted * value, axis=-1, keepdims=True)
    )


def gelu_tanh(value):
    return jnp.tanh(value * (GELU_A + (GELU_A * GELU_B) * (value * value)))


def gelu(value):
    return (0.5 * value) * (1.0 + gelu_tanh(value))


def gelu_slope(value, tanh):
    return 0.5 * (1.0 + tanh) + (0.5 * value) * (1.0 - tanh * tanh) * (
        GELU_A + (3.0 * GELU_A * GELU_B) * (value * value)
    )


def halves():
    lane = lax.broadcasted_iota(jnp.int32, (1, 128), 1)
    return [(lane // 64 == half) for half in range(2)]


def attend(q_ref, kv_ref, k_col, v_col, q_len, k_len, allow, out_ref, probs_ref=None):
    sides = halves()
    masks = [side.astype(jnp.float32).astype(jnp.bfloat16) for side in sides]

    def pair_step(pair, carry):
        lanes = pl.multiple_of(pair * 128, 128)
        for seq in range(SEQ_DEV):
            q_rows = pl.ds(seq * q_len, q_len)
            k_rows = pl.ds(seq * k_len, k_len)
            query = q_ref[q_rows, pl.ds(lanes, 128)]
            keys = kv_ref[k_rows, pl.ds(k_col + lanes, 128)]
            values = kv_ref[k_rows, pl.ds(v_col + lanes, 128)]
            outs = []
            for half in range(2):
                scores = mm_last(query * masks[half], keys) * 0.125
                scores = jnp.where(allow(seq), scores, blocked)
                peak = jnp.max(scores, axis=-1, keepdims=True)
                weights = jnp.exp(scores - peak)
                probs = weights * (1.0 / jnp.sum(weights, axis=-1, keepdims=True))
                if probs_ref is not None:
                    probs_ref[(pair * SEQ_DEV + seq) * 2 + half] = probs
                outs.append(mm(probs.astype(jnp.bfloat16), values))
            out_ref[q_rows, pl.ds(lanes, 128)] = jnp.where(sides[0], outs[0], outs[1]).astype(
                jnp.bfloat16
            )
        return carry

    lax.fori_loop(0, HEADS // 2, pair_step, 0)


def attend_back(grad_ref, q_ref, kv_ref, probs_ref, q_len, k_len, joined_ref):
    sides = halves()
    masks = [side.astype(jnp.float32).astype(jnp.bfloat16) for side in sides]

    def pair_step(pair, carry):
        lanes = pl.multiple_of(pair * 128, 128)
        for seq in range(SEQ_DEV):
            q_rows = pl.ds(seq * q_len, q_len)
            k_rows = pl.ds(seq * k_len, k_len)
            grad = grad_ref[q_rows, pl.ds(lanes, 128)]
            query = q_ref[q_rows, pl.ds(lanes, 128)]
            values = kv_ref[k_rows, pl.ds(D + lanes, 128)]
            key_grads, value_grads = [], []
            for half in range(2):
                probs = probs_ref[(pair * SEQ_DEV + seq) * 2 + half]
                grad_probs = mm_last(grad * masks[half], values)
                value_grads.append(mm_first(probs.astype(jnp.bfloat16), grad))
                inner = jnp.sum(grad_probs * probs, axis=-1, keepdims=True)
                grad_scores = (probs * (grad_probs - inner)).astype(jnp.bfloat16)
                key_grads.append(mm_first(grad_scores, query))
            joined_ref[k_rows, pl.ds(lanes, 128)] = (
                jnp.where(sides[0], key_grads[0], key_grads[1]) * 0.125
            ).astype(jnp.bfloat16)
            joined_ref[k_rows, pl.ds(D + lanes, 128)] = jnp.where(
                sides[0], value_grads[0], value_grads[1]
            ).astype(jnp.bfloat16)
        return carry

    lax.fori_loop(0, HEADS // 2, pair_step, 0)


def feed(state_ref, gain, inner_ref, outer_ref, act_ref, slope_ref, down_ref, up_ref, length,
         plain_ref, low_ref, after_ref):
    rows = SEQ_DEV * length
    act_rows = pl.ds(0, rows)
    source = normed(state_ref[...], gain)
    for block in range(FF // D):
        columns = slice(block * D, (block + 1) * D)
        hidden = mm(source, inner_ref[:, columns])
        tanh = gelu_tanh(hidden)
        act_ref[act_rows, columns] = ((0.5 * hidden) * (1.0 + tanh)).astype(jnp.bfloat16)
        if slope_ref is not None:
            slope_ref[:, columns] = gelu_slope(hidden, tanh)
    branch = mm(act_ref[act_rows, :], outer_ref[...])
    plain_ref[...] = branch.astype(jnp.bfloat16)
    for seq in range(SEQ_DEV):
        span = slice(seq * length, (seq + 1) * length)
        lowered = mm(plain_ref[span, :], down_ref[seq])
        low_ref[span, :] = lowered
        adapted = mm(gelu(lowered).astype(jnp.bfloat16), up_ref[seq]) * UPSCALE
        after_ref[span, :] = state_ref[span, :] + branch[span, :] + adapted


def adapter_back(grad_ref, low_ref, plain_ref, down_ref, up_ref, length, grad_down_ref,
                 grad_up_ref, branch_ref=None):
    for seq in range(SEQ_DEV):
        span = slice(seq * length, (seq + 1) * length)
        grad = grad_ref[span, :]
        grad_low = grad.astype(jnp.bfloat16)
        lowered = low_ref[span, :]
        tanh = gelu_tanh(lowered)
        bottleneck = ((0.5 * lowered) * (1.0 + tanh)).astype(jnp.bfloat16)
        grad_bottle = mm_last(grad_low, up_ref[seq]) * UPSCALE
        grad_up_ref[seq] = mm_first(bottleneck, grad_low)[:ADAPTER] * UPSCALE
        grad_lowered = (grad_bottle * gelu_slope(lowered, tanh)).astype(jnp.bfloat16)
        grad_down_ref[seq] = mm_first(plain_ref[span, :], grad_lowered)
        if branch_ref is not None:
            branch_ref[span, :] = (grad + mm_last(grad_lowered, down_ref[seq])).astype(
                jnp.bfloat16
            )


def pair_rows(embeds):
    return jnp.concatenate(
        [
            embeds[task : task + 1, :] + embeds[TASKS + layer : TASKS + layer + 1, :]
            for task in range(TASKS)
            for layer in range(LAYERS)
        ],
        axis=0,
    )


def prep_kernel(
    task_ref,
    len_ref,
    count_ref,
    src_ref,
    tgt_ref,
    embeds_ref,
    one_ref,
    two_ref,
    hyper_ref,
    table_hbm,
    rows_ref,
    adapters_ref,
    info_ref,
    sel_ref,
    coded_ref,
    crowded_ref,
    table,
    wide,
    generated,
    index_vmem,
    index,
    picked,
    load_sem,
    index_sem,
):
    member = lax.axis_index("gen")
    part = table.shape[0]
    offset = member * part
    cuts = [0, 2048, 4096, 6144, part]
    loads = [
        pltpu.make_async_copy(
            table_hbm.at[pl.ds(cuts[i], cuts[i + 1] - cuts[i])],
            table.at[pl.ds(cuts[i], cuts[i + 1] - cuts[i])],
            load_sem.at[i],
        )
        for i in range(4)
    ]
    for load in loads:
        load.start()

    wide_tokens = SEQ_DEV * SRC
    order = lax.broadcasted_iota(jnp.int32, (wide_tokens, wide_tokens), 0)
    upto = (
        (order <= lax.broadcasted_iota(jnp.int32, (wide_tokens, wide_tokens), 1))
        .astype(jnp.float32)
        .astype(jnp.bfloat16)
    )
    own_first = member * SEQ_DEV
    crowded = jnp.zeros((), jnp.int32)
    slots = []
    for ids_ref, length, cap, rows, start in (
        (src_ref, SRC, SRC_CAP, SRC_CAP, 0),
        (tgt_ref, TGT, TGT_CAP, TGT_ROWS, SRC_CAP),
    ):
        count = SEQ_DEV * length
        ids = jnp.concatenate(
            [
                jnp.concatenate(
                    [ids_ref[SEQ_DEV * t + s : SEQ_DEV * t + s + 1, :] for s in range(SEQ_DEV)],
                    axis=1,
                )
                for t in range(GEN)
            ],
            axis=0,
        )
        own = jnp.concatenate([ids_ref[pl.ds(own_first + s, 1), :] for s in range(SEQ_DEV)], axis=1)
        local = ids - offset
        inside = ((local >= 0) & (local < part)).astype(jnp.float32)
        held = [
            ((own >= part * o) & (own < part * (o + 1))).astype(jnp.float32) for o in range(GEN)
        ]
        marks = jnp.concatenate([inside] + held, axis=0)
        ranks = mm(marks.astype(jnp.bfloat16), upto[:count, :count]) - 1.0
        most = jnp.zeros((GEN, 1), jnp.float32)
        for o in range(GEN):
            amount = ((ids >= part * o) & (ids < part * (o + 1))).astype(jnp.float32)
            most = jnp.maximum(most, jnp.sum(amount, axis=1, keepdims=True))
        crowded = crowded + (jnp.max(most) > float(cap)).astype(jnp.int32)
        for t in range(GEN):
            place = jnp.where(inside[t : t + 1] > 0.0, ranks[t : t + 1], -1.0)
            spot = lax.broadcasted_iota(jnp.int32, (rows, count), 0).astype(jnp.float32)
            chosen = (spot == place).astype(jnp.float32).astype(jnp.bfloat16)
            token = local[t : t + 1]
            digits = jnp.concatenate(
                [
                    lax.shift_right_logical(token, 6).astype(jnp.float32) * inside[t : t + 1],
                    lax.bitwise_and(token, 63).astype(jnp.float32) * inside[t : t + 1],
                    jnp.zeros((6, count), jnp.float32),
                ],
                axis=0,
            ).astype(jnp.bfloat16)
            found = mm_last(digits, chosen)
            index_vmem[t : t + 1, start : start + rows] = (
                found[0:1] * 64.0 + found[1:2]
            ).astype(jnp.int32)
        slot = jnp.zeros((1, count), jnp.float32)
        for o in range(GEN):
            slot = slot + held[o] * (ranks[GEN + o : GEN + o + 1] + float(o * rows))
        slots.append(slot)
    index_copy = pltpu.make_async_copy(index_vmem, index, index_sem)
    index_copy.start()

    use_fast = jnp.where(crowded == 0, 1.0, 0.0)
    lane = lax.broadcasted_iota(jnp.int32, (1, SEQ_DEV * TGT), 1)
    shifted = jnp.where(
        lax.rem(lane, TGT) == 0, float(TGT_CAP), pltpu.roll(slots[1], 1, axis=1)
    )
    position = lax.broadcasted_iota(jnp.int32, (1, SRC), 1)
    allow = jnp.concatenate(
        [
            (position < len_ref[task_ref[own_first + s]]).astype(jnp.float32)
            for s in range(SEQ_DEV)
        ],
        axis=1,
    )
    place = lax.broadcasted_iota(jnp.int32, (1, TGT), 1)
    valid = jnp.concatenate(
        [(place < count_ref[own_first + s]).astype(jnp.float32) for s in range(SEQ_DEV)], axis=1
    )
    tokens = jnp.zeros((1, SEQ_DEV * TGT), jnp.float32) + sum(
        count_ref[own_first + s] for s in range(SEQ_DEV)
    ).astype(jnp.float32)

    def switch(slot):
        return jnp.where(use_fast > 0.0, slot, -1.0)

    info_ref[...] = jnp.concatenate(
        [
            switch(slots[0]),
            jnp.concatenate([switch(shifted), switch(slots[1])], axis=1),
            allow,
            jnp.concatenate([valid, tokens], axis=1),
            jnp.zeros((4, wide_tokens), jnp.float32),
        ],
        axis=0,
    )
    crowded_ref[0] = crowded

    coded = exact(
        gelu(exact(pair_rows(embeds_ref[...]), one_ref[...], ((1,), (0,)))),
        two_ref[...],
        ((1,), (0,)),
    )
    coded_ref[...] = coded
    flat = exact(coded, hyper_ref[...], ((1,), (0,)))
    pairs = TASKS * LAYERS
    for tile in range(FLAT):
        generated[pl.ds(tile, pairs, stride=FLAT), :] = flat[:, 128 * tile : 128 * (tile + 1)]
    selector = jnp.zeros((pairs, 128), jnp.float32)
    row_of = lax.broadcasted_iota(jnp.int32, (pairs, 128), 0)
    column_of = lax.broadcasted_iota(jnp.int32, (pairs, 128), 1)
    sequences = GEN * SEQ_DEV
    for seq in range(sequences):
        for layer in range(LAYERS):
            pair = task_ref[seq] * LAYERS + layer
            begin = ((seq % SEQ_DEV) * LAYERS + layer) * FLAT
            adapters_ref[seq // SEQ_DEV, begin : begin + FLAT, :] = generated[
                pl.ds(pl.multiple_of(pair * FLAT, 8), FLAT), :
            ].astype(jnp.bfloat16)
            selector = jnp.where(
                (row_of == pair) & (column_of == layer * sequences + seq), 1.0, selector
            )
    sel_ref[...] = selector

    chunk = 32
    for i in range(4):
        loads[i].wait()

        def widen(step, carry):
            begin = pl.multiple_of(cuts[i] + step * chunk, chunk)
            wide[pl.ds(begin, chunk), :] = table[pl.ds(begin, chunk), :].astype(jnp.float32)
            return carry

        lax.fori_loop(0, (cuts[i + 1] - cuts[i]) // chunk, widen, 0)
    index_copy.wait()
    for t in range(GEN):

        def fetch(step, carry):
            begin = pl.multiple_of(step * 16, 16)
            for k in range(16):
                picked[pl.ds(begin + k, 1), :] = wide[pl.ds(index[t, begin + k], 1), :]
            return carry

        lax.fori_loop(0, (SRC_CAP + TGT_ROWS) // 16, fetch, 0)
        rows_ref[t] = picked[...].astype(jnp.bfloat16)


def prep(task_ids, task_len, tgt_count, src_ids, tgt_ids, embeds, one, two, hyper, table):
    vmem = pl.BlockSpec(memory_space=pltpu.VMEM)
    smem = pl.BlockSpec(memory_space=pltpu.SMEM)
    whole = pl.BlockSpec(memory_space=pl.ANY)
    low, full = jnp.bfloat16, jnp.float32
    rows = SRC_CAP + TGT_ROWS
    pairs = TASKS * LAYERS
    return pl.pallas_call(
        prep_kernel,
        out_shape=(
            jax.ShapeDtypeStruct((GEN, rows, D), low),
            jax.ShapeDtypeStruct((GEN, SEQ_DEV * LAYERS * FLAT, 128), low),
            jax.ShapeDtypeStruct((8, SEQ_DEV * SRC), full),
            jax.ShapeDtypeStruct((pairs, 128), full),
            jax.ShapeDtypeStruct((pairs, two.shape[1]), full),
            jax.ShapeDtypeStruct((1,), jnp.int32),
        ),
        in_specs=[smem] * 3 + [vmem] * 6 + [whole],
        out_specs=(vmem, vmem, vmem, vmem, vmem, smem),
        scratch_shapes=[
            pltpu.VMEM(table.shape, low),
            pltpu.VMEM(table.shape, full),
            pltpu.VMEM((pairs * FLAT, 128), full),
            pltpu.VMEM((8, 384), jnp.int32),
            pltpu.SMEM((8, 384), jnp.int32),
            pltpu.VMEM((rows, D), full),
            pltpu.SemaphoreType.DMA((4,)),
            pltpu.SemaphoreType.DMA,
        ],
        compiler_params=pltpu.CompilerParams(vmem_limit_bytes=60 * 1024 * 1024),
        name="prepare",
    )(task_ids, task_len, tgt_count, src_ids, tgt_ids, embeds, one, two, hyper, table)


def crowded_kernel(rows_ref, out_ref, incoming, send_sem, recv_sem):
    member = lax.axis_index("gen")
    barrier = pltpu.get_barrier_semaphore()
    for step in range(1, GEN):
        pl.semaphore_signal(
            barrier, inc=1, device_id={"gen": lax.rem(member + step, GEN)}, device_id_type=MESH
        )
    pl.semaphore_wait(barrier, GEN - 1)
    copies = []
    for step in range(1, GEN):
        target = lax.rem(member + step, GEN)
        copies.append(
            pltpu.make_async_remote_copy(
                src_ref=rows_ref.at[target],
                dst_ref=incoming.at[step],
                send_sem=send_sem.at[step],
                recv_sem=recv_sem.at[step],
                device_id={"gen": target},
                device_id_type=MESH,
            )
        )
        copies[-1].start()
    total = rows_ref[member].astype(jnp.float32)
    for step in range(1, GEN):
        copies[step - 1].wait()
        total = total + incoming[step].astype(jnp.float32)
    out_ref[...] = total.astype(jnp.bfloat16)


def crowded_rows(src_ids, tgt_ids, table):
    member = lax.axis_index("gen")
    inputs = jnp.concatenate([jnp.zeros_like(tgt_ids[:, :1]), tgt_ids[:, :-1]], axis=1)
    tokens = jnp.concatenate(
        [
            ids.reshape(GEN, -1)
            for ids in (src_ids, inputs, tgt_ids)
        ],
        axis=1,
    )
    token = tokens - member * table.shape[0]
    inside = (token >= 0) & (token < table.shape[0])
    rows = jnp.take(table, jnp.clip(token, 0, table.shape[0] - 1).reshape(-1), axis=0)
    rows = jnp.where(inside.reshape(-1, 1), rows, jnp.zeros_like(rows)).reshape(
        GEN, tokens.shape[1], -1
    )
    vmem = pl.BlockSpec(memory_space=pltpu.VMEM)
    return pl.pallas_call(
        crowded_kernel,
        out_shape=jax.ShapeDtypeStruct(rows.shape[1:], jnp.bfloat16),
        in_specs=[vmem],
        out_specs=vmem,
        scratch_shapes=[
            pltpu.VMEM(rows.shape, jnp.bfloat16),
            pltpu.SemaphoreType.DMA((GEN,)),
            pltpu.SemaphoreType.DMA((GEN,)),
        ],
        compiler_params=pltpu.CompilerParams(
            collective_id=2, has_side_effects=True, vmem_limit_bytes=40 * 1024 * 1024
        ),
        name="crowded_rows",
    )(rows)


def step_kernel(
    adapters_ref,
    info_ref,
    sel_ref,
    coded_ref,
    gains_ref,
    rows_hbm,
    slow_hbm,
    hyper_hbm,
    attn_hbm,
    inner_hbm,
    outer_hbm,
    table_hbm,
    out_ref,
    small_ref,
    attn,
    inner,
    outer,
    table,
    state,
    after_e,
    plain_e,
    low_e,
    qkv,
    mixed,
    act,
    memory,
    y1,
    y2,
    y3,
    q_cross,
    kv_cross,
    probs,
    slope,
    plain_d,
    low_d,
    feats,
    total,
    results,
    arrived,
    stats,
    stats_in,
    grad,
    grad_low,
    joined,
    src_in,
    tgt_in,
    adapters_in,
    slow,
    flat_in,
    spread,
    down_ref,
    up_ref,
    grad_down_ref,
    grad_up_ref,
    wanted,
    pack,
    grads_in,
    hyper,
    outgoing,
    incoming,
    shares,
    outgoing_small,
    incoming_small,
    load_sem,
    row_send,
    src_recv,
    tgt_recv,
    adapter_recv,
    grad_send,
    grad_recv,
    scatter_sem,
    share_sem,
    small_send,
    small_recv,
    feat_send,
    feat_recv,
    result_send,
    result_recv,
    stat_send,
    stat_recv,
):
    member = lax.axis_index("gen")
    barrier = pltpu.get_barrier_semaphore()

    def peer(order):
        chip = lax.rem(member // 2 + lax.rem((order + 1) // 2, 2), 2)
        return chip * 2 + lax.rem(lax.rem(member, 2) + order // 2, 2)

    rank = lax.axis_index("dp")
    count = outgoing.shape[0]
    width = shares.shape[2]
    per_half = out_ref.shape[1] // width
    for order in range(1, GEN):
        pl.semaphore_signal(
            barrier, inc=1, device_id={"gen": peer(order)}, device_id_type=MESH
        )

    def greet(step, carry):
        pl.semaphore_signal(
            barrier, inc=1, device_id={"dp": lax.rem(rank + step, count)}, device_id_type=MESH
        )
        return carry

    lax.fori_loop(1, count, greet, 0)

    loads = []
    for source, target in (
        (attn_hbm.at[0], attn.at[0]),
        (inner_hbm.at[0], inner.at[0]),
        (outer_hbm.at[0], outer.at[0]),
        (attn_hbm.at[1], attn.at[1]),
        (attn_hbm.at[2], attn.at[2]),
        (inner_hbm.at[1], inner.at[1]),
        (outer_hbm.at[1], outer.at[1]),
        (table_hbm, table),
        (slow_hbm, slow),
        (hyper_hbm, hyper),
    ):
        loads.append(pltpu.make_async_copy(source, target, load_sem.at[len(loads)]))
        loads[-1].start()

    pl.semaphore_wait(barrier, GEN + count - 2)

    def source_copy(owner, target):
        return pltpu.make_async_remote_copy(
            src_ref=rows_hbm.at[target, pl.ds(0, SRC_CAP)],
            dst_ref=src_in.at[owner],
            send_sem=row_send.at[0, target],
            recv_sem=src_recv.at[owner],
            device_id={"gen": target},
            device_id_type=MESH,
        )

    def target_copy(owner, target):
        return pltpu.make_async_remote_copy(
            src_ref=rows_hbm.at[target, pl.ds(SRC_CAP, TGT_ROWS)],
            dst_ref=tgt_in.at[owner],
            send_sem=row_send.at[1, target],
            recv_sem=tgt_recv.at[owner],
            device_id={"gen": target},
            device_id_type=MESH,
        )

    def adapter_copy(owner, target):
        return pltpu.make_async_remote_copy(
            src_ref=adapters_ref.at[target],
            dst_ref=adapters_in.at[owner],
            send_sem=row_send.at[2, target],
            recv_sem=adapter_recv.at[owner],
            device_id={"gen": target},
            device_id_type=MESH,
        )

    for order in range(1, GEN):
        source_copy(member, peer(order)).start()
    for order in range(1, GEN):
        adapter_copy(member, peer(order)).start()
    for order in range(1, GEN):
        target_copy(member, peer(order)).start()
    own_source = pltpu.make_async_copy(
        rows_hbm.at[member, pl.ds(0, SRC_CAP)], src_in.at[member], src_recv.at[member]
    )
    own_source.start()
    own_target = pltpu.make_async_copy(
        rows_hbm.at[member, pl.ds(SRC_CAP, TGT_ROWS)], tgt_in.at[member], tgt_recv.at[member]
    )
    own_target.start()
    adapters_in[member] = adapters_ref[member]

    def spread_rows(row, lanes, incoming_rows, owner):
        height = incoming_rows.shape[1]
        spot = lax.broadcasted_iota(jnp.int32, (height, lanes.stop - lanes.start), 0)
        spot = (spot + owner * height).astype(jnp.float32)
        chosen = (spot == info_ref[row : row + 1, lanes]).astype(jnp.float32)
        return mm_first(chosen.astype(jnp.bfloat16), incoming_rows[owner])

    sources = SEQ_DEV * SRC
    targets = SEQ_DEV * TGT
    own = pl.ds(0, targets)
    loads[8].wait()
    own_source.wait()
    after_e[...] = slow[0:sources, :].astype(jnp.float32) + spread_rows(
        0, slice(0, sources), src_in, member
    )
    for order in (3, 1, 2):
        source_copy(peer(order), peer(order)).wait_recv()
        after_e[...] = after_e[...] + spread_rows(0, slice(0, sources), src_in, peer(order))
    embedded = after_e[...]

    def allowed(seq):
        return info_ref[2:3, seq * SRC : (seq + 1) * SRC] > 0.0

    entry = normed(embedded, gains_ref[0:1])
    loads[0].wait()
    for block in range(3):
        columns = slice(block * D, (block + 1) * D)
        qkv[:, columns] = mm(entry, attn[0, :, columns]).astype(jnp.bfloat16)
    attend(qkv, qkv, D, 2 * D, SRC, SRC, allowed, mixed)
    state[...] = embedded + mm(mixed[...], attn[0, :, 3 * D :])
    loads[1].wait()
    loads[2].wait()
    for order in range(1, GEN):
        adapter_copy(peer(order), peer(order)).wait_recv()
    unpack_adapters(adapters_in, flat_in, spread, down_ref, up_ref)
    feed(state, gains_ref[1:2], inner.at[0], outer.at[0], act, None, down_ref.at[0], up_ref.at[0],
         SRC, plain_e, low_e, after_e)
    memory[...] = normed(after_e[...], gains_ref[2:3])

    own_target.wait()
    for order in range(1, GEN):
        target_copy(peer(order), peer(order)).wait_recv()
    inputs = slow[sources : sources + targets, :].astype(jnp.float32)
    wanted[...] = slow[sources + targets : sources + 2 * targets, :].astype(jnp.float32)
    for owner in range(GEN):
        inputs = inputs + spread_rows(1, slice(0, targets), tgt_in, owner)
        wanted[...] = wanted[...] + spread_rows(1, slice(targets, 2 * targets), tgt_in, owner)
    entry = normed(inputs, gains_ref[3:4])
    loads[3].wait()
    for block in range(3):
        columns = slice(block * D, (block + 1) * D)
        qkv[own, columns] = mm(entry, attn[1, :, columns]).astype(jnp.bfloat16)
    causal = lax.broadcasted_iota(jnp.int32, (TGT, TGT), 0) >= lax.broadcasted_iota(
        jnp.int32, (TGT, TGT), 1
    )
    attend(qkv, qkv, D, 2 * D, TGT, TGT, lambda seq: causal, mixed)
    y1[...] = inputs + mm(mixed[own, :], attn[1, :, 3 * D :])
    loads[4].wait()
    q_cross[...] = mm(normed(y1[...], gains_ref[4:5]), attn[2, :, :D]).astype(jnp.bfloat16)
    for block in range(2):
        columns = slice(block * D, (block + 1) * D)
        kv_cross[:, columns] = mm(
            memory[...], attn[2, :, (block + 1) * D : (block + 2) * D]
        ).astype(jnp.bfloat16)
    attend(q_cross, kv_cross, 0, D, TGT, SRC, allowed,
           mixed, probs)
    y2[...] = y1[...] + mm(mixed[own, :], attn[2, :, 3 * D :])
    loads[5].wait()
    loads[6].wait()
    feed(y2, gains_ref[5:6], inner.at[1], outer.at[1], act, slope, down_ref.at[1], up_ref.at[1],
         TGT, plain_d, low_d, y3)
    feats[0] = normed(y3[...], gains_ref[6:7])


    def feature_copy(order):
        return pltpu.make_async_remote_copy(
            src_ref=feats.at[0],
            dst_ref=feats.at[order],
            send_sem=feat_send.at[order],
            recv_sem=feat_recv.at[order],
            device_id={"gen": peer(order)},
            device_id_type=MESH,
        )

    def result_copy(order):
        return pltpu.make_async_remote_copy(
            src_ref=results.at[order],
            dst_ref=arrived.at[order],
            send_sem=result_send.at[order],
            recv_sem=result_recv.at[order],
            device_id={"gen": peer(order)},
            device_id_type=MESH,
        )

    def stat_copy(order):
        return pltpu.make_async_remote_copy(
            src_ref=stats.at[order],
            dst_ref=stats_in.at[order],
            send_sem=stat_send.at[order],
            recv_sem=stat_recv.at[order],
            device_id={"gen": peer(order)},
            device_id_type=MESH,
        )

    for order in range(1, GEN):
        feature_copy(order).start()
    loads[7].wait()
    same = lax.broadcasted_iota(jnp.int32, (targets, targets), 0) == lax.broadcasted_iota(
        jnp.int32, (targets, targets), 1
    )

    def as_row(column):
        return jnp.sum(jnp.where(same, column, 0.0), axis=0, keepdims=True)

    def as_column(row):
        return jnp.sum(jnp.where(same, row, 0.0), axis=1, keepdims=True)

    def block_step(order, carry):
        @pl.when(order > 0)
        def _():
            feature_copy(order).wait_recv()

        query = feats[order]
        ends = list(range(0, table.shape[0], VOCAB_TILE)) + [table.shape[0]]
        tiles = [(ends[i], ends[i + 1]) for i in range(len(ends) - 1)]
        peak = scale = None
        scores = mm_last(query, table[tiles[0][0] : tiles[0][1], :])
        for index, (first, last) in enumerate(tiles):
            following = None
            if index + 1 < len(tiles):
                following = mm_last(query, table[tiles[index + 1][0] : tiles[index + 1][1], :])
            top = jnp.max(scores, axis=-1, keepdims=True)
            if index > 0:
                top = jnp.maximum(peak, top)
            weights = jnp.exp2((scores - top) * EXP_SCALE)
            amount = jnp.sum(weights, axis=-1, keepdims=True)
            part = mm(weights.astype(jnp.bfloat16), table[first:last, :])
            if index == 0:
                total[...] = part
                scale = amount
            else:
                shrink = jnp.exp2((peak - top) * EXP_SCALE)
                total[...] = total[...] * shrink + part
                scale = scale * shrink + amount
            peak, scores = top, following
        results[order] = total[...].astype(jnp.bfloat16)
        stats[order] = jnp.concatenate(
            [as_row(peak), as_row(scale), jnp.zeros((6, targets), jnp.float32)], axis=0
        )

        @pl.when(order > 0)
        def _():
            result_copy(order).start()
            stat_copy(order).start()

        return carry

    lax.fori_loop(0, GEN, block_step, 0)
    stats_in[0] = stats[0]
    for order in range(1, GEN):
        stat_copy(order).wait_recv()
    peaks = [as_column(stats_in[order, 0:1, :]) for order in range(GEN)]
    sums = [as_column(stats_in[order, 1:2, :]) for order in range(GEN)]
    top = jnp.maximum(jnp.maximum(peaks[0], peaks[1]), jnp.maximum(peaks[2], peaks[3]))
    parts = [jnp.exp2((peaks[order] - top) * EXP_SCALE) for order in range(GEN)]
    amount = sum(parts[order] * sums[order] for order in range(GEN))
    logsum = top * LOGIT_SCALE + jnp.log(amount)
    inverse = 1.0 / amount
    total[...] = results[0].astype(jnp.float32) * (parts[0] * inverse)
    for order in range(1, GEN):
        result_copy(order).wait_recv()
        total[...] = total[...] + arrived[order].astype(jnp.float32) * (parts[order] * inverse)
    picked = (
        jnp.sum(feats[0].astype(jnp.float32) * wanted[...], axis=-1, keepdims=True) * LOGIT_SCALE
    )
    counted = as_column(info_ref[3:4, 0:targets])
    loss = jnp.sum((logsum - picked) * counted, axis=0, keepdims=True)
    lane = lax.broadcasted_iota(jnp.int32, (8, 128), 1)
    totals = jnp.where(
        lane == 0, loss, jnp.where(lane == 1, info_ref[3:4, targets : targets + 128], 0.0)
    )

    grad[own, :] = norm_back(
        y3[...], gains_ref[6:7], (total[...] - wanted[...]) * (counted * LOGIT_SCALE)
    )
    adapter_back(grad.at[own], low_d, plain_d, down_ref.at[1], up_ref.at[1], TGT,
                 grad_down_ref.at[1], grad_up_ref.at[1], grad_low)

    def grad_copy(layer, owner, target):
        part = SEQ_DEV * FLAT
        begin = pl.multiple_of((layer * GEN + owner) * part, 8)
        return pltpu.make_async_remote_copy(
            src_ref=pack.at[layer, target],
            dst_ref=grads_in.at[pl.ds(begin, part)],
            send_sem=grad_send.at[layer, target],
            recv_sem=grad_recv.at[layer, owner],
            device_id={"gen": target},
            device_id_type=MESH,
        )

    def send_grads(layer):
        pack_grads(grad_down_ref.at[layer], grad_up_ref.at[layer], pack.at[layer])
        for order in range(1, GEN):
            grad_copy(layer, member, peer(order)).start()
        begin = pl.multiple_of((layer * GEN + member) * SEQ_DEV * FLAT, 8)
        grads_in[pl.ds(begin, SEQ_DEV * FLAT), :] = pack[layer, member]

    send_grads(1)
    for block in range(FF // D):
        columns = slice(block * D, (block + 1) * D)
        act[own, columns] = (
            mm_last(grad_low[...], outer[1, columns, :]) * slope[:, columns]
        ).astype(jnp.bfloat16)
    grad_entry = mm_last(act[own, :], inner[1])
    grad_state = grad[own, :] + norm_back(y2[...], gains_ref[5:6], grad_entry)
    mixed[own, :] = mm_last(grad_state.astype(jnp.bfloat16), attn[2, :, 3 * D :]).astype(
        jnp.bfloat16
    )
    attend_back(mixed, q_cross, kv_cross, probs, TGT, SRC, joined)
    grad_memory = mm_last(joined[...], attn[2, :, D : 3 * D])

    grad[...] = norm_back(after_e[...], gains_ref[2:3], grad_memory)
    adapter_back(grad, low_e, plain_e, down_ref.at[0], up_ref.at[0], SRC,
                 grad_down_ref.at[0], grad_up_ref.at[0])
    send_grads(0)
    for layer in range(LAYERS):
        for order in range(1, GEN):
            grad_copy(layer, peer(order), peer(order)).wait_recv()
    pairs = TASKS * LAYERS
    received = jnp.concatenate(
        [grads_in[pl.ds(tile, pairs, stride=FLAT), :] for tile in range(FLAT)], axis=1
    )
    slots = exact(sel_ref[:, 0:pairs], received, ((1,), (0,)))

    for piece in range(count):
        row, column = piece // per_half * 8, piece % per_half * width
        outgoing[piece, :, :width] = slots[row : row + 8, column : column + width]
        outgoing[piece, :, width:] = totals

    def scatter(step, carry):
        target = lax.rem(rank + step, count)
        pltpu.make_async_remote_copy(
            src_ref=outgoing.at[target],
            dst_ref=incoming.at[rank],
            send_sem=scatter_sem.at[0],
            recv_sem=scatter_sem.at[1],
            device_id={"dp": target},
            device_id_type=MESH,
        ).start()
        return carry

    def share(step, carry):
        pltpu.make_async_remote_copy(
            src_ref=shares.at[rank],
            dst_ref=shares.at[rank],
            send_sem=share_sem.at[0],
            recv_sem=share_sem.at[1],
            device_id={"dp": lax.rem(rank + step, count)},
            device_id_type=MESH,
        ).start()
        return carry

    def wait_all(ref, sem):
        others = ref.at[pl.ds(0, count - 1)]
        pltpu.make_async_copy(others, others, sem).wait()

    lax.fori_loop(1, count, scatter, 0)
    incoming[rank] = outgoing[rank]
    wait_all(incoming, scatter_sem.at[1])
    summed = incoming[0]
    for source in range(1, count):
        summed = summed + incoming[source]
    shares[rank] = summed[:, :width]
    lax.fori_loop(1, count, share, 0)
    wait_all(shares, share_sem.at[1])
    for piece in range(count):
        row, column = piece // per_half * 8, piece % per_half * width
        out_ref[row : row + 8, column : column + width] = shares[piece]

    loads[9].wait()
    slots = out_ref[...]
    coded_part = exact(slots, hyper[...], ((1,), (1,)))
    hyper_grad = exact(coded_ref[...], slots, ((0,), (0,)))
    square = jnp.sum(hyper_grad * hyper_grad, axis=0, keepdims=True)
    outgoing_small[0:16, :] = jnp.concatenate(
        [coded_part, jnp.zeros((16, 64), jnp.float32)], axis=1
    )
    outgoing_small[16:24, :] = jnp.broadcast_to(
        jnp.sum(square, axis=1, keepdims=True), (8, 128)
    )
    outgoing_small[24:32, :] = summed[:, width:]
    copies = [
        pltpu.make_async_remote_copy(
            src_ref=outgoing_small,
            dst_ref=incoming_small.at[member],
            send_sem=small_send.at[step],
            recv_sem=small_recv.at[step],
            device_id={"gen": lax.rem(member + step, GEN)},
            device_id_type=MESH,
        )
        for step in range(1, GEN)
    ]
    for copy in copies:
        copy.start()
    incoming_small[member] = outgoing_small[...]
    for order in range(1, GEN):
        source_copy(member, peer(order)).wait_send()
        adapter_copy(member, peer(order)).wait_send()
        target_copy(member, peer(order)).wait_send()
        feature_copy(order).wait_send()
        result_copy(order).wait_send()
        stat_copy(order).wait_send()
        for layer in range(LAYERS):
            grad_copy(layer, member, peer(order)).wait_send()
    wait_all(outgoing, scatter_sem.at[0])
    wait_all(shares, share_sem.at[0])
    for copy in copies:
        copy.wait()
    small_ref[...] = (incoming_small[0] + incoming_small[1]) + (
        incoming_small[2] + incoming_small[3]
    )


def unpack_adapters(entries, flat, spread, down_ref, up_ref):
    lane = lax.broadcasted_iota(jnp.int32, (1, 128), 1)
    kept = lane < ADAPTER
    run = D // 32
    for owner in range(GEN):
        flat[owner] = entries[owner].astype(jnp.float32)
    up_ref[...] = jnp.zeros(up_ref.shape, jnp.bfloat16)
    for layer in range(LAYERS):
        for seq in range(SEQ_DEV):
            base = (seq * LAYERS + layer) * FLAT
            for owner in range(GEN // 2):
                tiles = [flat[owner, pl.ds(base + j, run, stride=3), :] for j in range(3)]
                for step in range(run):
                    tile, shift = divmod(ADAPTER * step, 128)
                    piece = tiles[tile]
                    if shift:
                        piece = pltpu.roll(piece, 128 - shift, axis=1)
                    if shift + ADAPTER > 128:
                        tail = pltpu.roll(tiles[tile + 1], 128 - shift, axis=1)
                        piece = jnp.where(lane < 128 - shift, piece, tail)
                    spread[pl.ds(owner * (D // 2) + step, run, stride=run), 0:128] = jnp.where(
                        kept, piece, 0.0
                    )
            down_ref[layer, seq] = spread[:, 0:128].astype(jnp.bfloat16)
            halves_up = []
            for owner in range(GEN // 2, GEN):
                halves_up.append(
                    jnp.concatenate(
                        [
                            flat[owner, pl.ds(base + k, ADAPTER // 2, stride=4), :]
                            for k in range(4)
                        ],
                        axis=1,
                    )
                )
            joined = jnp.concatenate(halves_up + [jnp.zeros((8, D), jnp.float32)], axis=0)
            up_ref[layer, seq, 0:32, :] = joined.astype(jnp.bfloat16)


def pack_grads(grad_down, grad_up, pack):
    lane = lax.broadcasted_iota(jnp.int32, (1, 128), 1)
    run = D // 32
    for seq in range(SEQ_DEV):
        base = seq * FLAT
        for owner in range(GEN // 2):
            tiles = [jnp.zeros((run, 128), jnp.float32) for _ in range(3)]
            for step in range(run):
                tile, shift = divmod(ADAPTER * step, 128)
                piece = grad_down[seq, pl.ds(owner * (D // 2) + step, run, stride=run), :]
                if shift:
                    piece = pltpu.roll(piece, shift, axis=1)
                if shift + ADAPTER > 128:
                    tiles[tile] = tiles[tile] + jnp.where(lane >= shift, piece, 0.0)
                    tiles[tile + 1] = tiles[tile + 1] + jnp.where(lane < shift, piece, 0.0)
                else:
                    tiles[tile] = tiles[tile] + piece
            for j in range(3):
                pack[owner, pl.ds(base + j, run, stride=3), :] = tiles[j]
        for half in range(GEN // 2):
            rows = slice(half * (ADAPTER // 2), (half + 1) * (ADAPTER // 2))
            for k in range(4):
                pack[GEN // 2 + half, pl.ds(base + k, ADAPTER // 2, stride=4), :] = grad_up[
                    seq, rows, 128 * k : 128 * (k + 1)
                ]


def step(adapters, info, sel, coded, gains, rows, slow, hyper, attn_w, ffn_in, ffn_out, table):
    vmem = pl.BlockSpec(memory_space=pltpu.VMEM)
    whole = pl.BlockSpec(memory_space=pl.ANY)
    low, full = jnp.bfloat16, jnp.float32
    sources, targets = SEQ_DEV * SRC, SEQ_DEV * TGT
    pairs = TASKS * LAYERS
    count = lax.axis_size("dp")
    width = pairs * FLAT * 128 // (8 * count)
    dma = pltpu.SemaphoreType.DMA
    return pl.pallas_call(
        step_kernel,
        out_shape=(
            jax.ShapeDtypeStruct((pairs, FLAT * 128), full),
            jax.ShapeDtypeStruct((32, 128), full),
        ),
        in_specs=[vmem] * 5 + [whole] * 7,
        out_specs=(vmem, vmem),
        scratch_shapes=[
            pltpu.VMEM(attn_w.shape, low),
            pltpu.VMEM(ffn_in.shape, low),
            pltpu.VMEM(ffn_out.shape, low),
            pltpu.VMEM(table.shape, low),
            pltpu.VMEM((sources, D), full),
            pltpu.VMEM((sources, D), full),
            pltpu.VMEM((sources, D), low),
            pltpu.VMEM((sources, LOW), full),
            pltpu.VMEM((sources, 3 * D), low),
            pltpu.VMEM((sources, D), low),
            pltpu.VMEM((sources, FF), low),
            pltpu.VMEM((sources, D), low),
            pltpu.VMEM((targets, D), full),
            pltpu.VMEM((targets, D), full),
            pltpu.VMEM((targets, D), full),
            pltpu.VMEM((targets, D), low),
            pltpu.VMEM((sources, 2 * D), low),
            pltpu.VMEM((SEQ_DEV * HEADS, TGT, SRC), full),
            pltpu.VMEM((targets, FF), full),
            pltpu.VMEM((targets, D), low),
            pltpu.VMEM((targets, LOW), full),
            pltpu.VMEM((GEN, targets, D), low),
            pltpu.VMEM((targets, D), full),
            pltpu.VMEM((GEN, targets, D), low),
            pltpu.VMEM((GEN, targets, D), low),
            pltpu.VMEM((GEN, 8, targets), full),
            pltpu.VMEM((GEN, 8, targets), full),
            pltpu.VMEM((sources, D), full),
            pltpu.VMEM((targets, D), low),
            pltpu.VMEM((sources, 2 * D), low),
            pltpu.VMEM((GEN, SRC_CAP, D), low),
            pltpu.VMEM((GEN, TGT_ROWS, D), low),
            pltpu.VMEM((GEN, SEQ_DEV * LAYERS * FLAT, 128), low),
            pltpu.VMEM((sources + 2 * targets, D), low),
            pltpu.VMEM((GEN, SEQ_DEV * LAYERS * FLAT, 128), full),
            pltpu.VMEM((D, 128), full),
            pltpu.VMEM((LAYERS, SEQ_DEV, D, LOW), low),
            pltpu.VMEM((LAYERS, SEQ_DEV, LOW, D), low),
            pltpu.VMEM((LAYERS, SEQ_DEV, D, LOW), full),
            pltpu.VMEM((LAYERS, SEQ_DEV, ADAPTER, D), full),
            pltpu.VMEM((targets, D), full),
            pltpu.VMEM((LAYERS, GEN, SEQ_DEV * FLAT, 128), full),
            pltpu.VMEM((LAYERS * GEN * SEQ_DEV * FLAT, 128), full),
            pltpu.VMEM(hyper.shape, full),
            pltpu.VMEM((count, 8, width + 128), full),
            pltpu.VMEM((count, 8, width + 128), full),
            pltpu.VMEM((count, 8, width), full),
            pltpu.VMEM((32, 128), full),
            pltpu.VMEM((GEN, 32, 128), full),
            dma((10,)),
            dma((3, GEN)),
            dma((GEN,)),
            dma((GEN,)),
            dma((GEN,)),
            dma((LAYERS, GEN)),
            dma((LAYERS, GEN)),
            dma((2,)),
            dma((2,)),
            dma((GEN,)),
            dma((GEN,)),
            dma((GEN,)),
            dma((GEN,)),
            dma((GEN,)),
            dma((GEN,)),
            dma((GEN,)),
            dma((GEN,)),
        ],
        compiler_params=pltpu.CompilerParams(
            collective_id=1, has_side_effects=True, vmem_limit_bytes=62 * 1024 * 1024
        ),
        name="forward_vocab_backward_sum",
    )(adapters, info, sel, coded, gains, rows, slow, hyper, attn_w, ffn_in, ffn_out, table)


def update_kernel(
    slots_ref,
    small_ref,
    coded_ref,
    embeds,
    embeds_m,
    embeds_v,
    one,
    one_m,
    one_v,
    two,
    two_m,
    two_v,
    hyper,
    hyper_m,
    hyper_v,
    loss_ref,
    tokens_ref,
    norm_ref,
    new_embeds,
    new_embeds_m,
    new_embeds_v,
    new_one,
    new_one_m,
    new_one_v,
    new_two,
    new_two_m,
    new_two_v,
    new_hyper,
    new_hyper_m,
    new_hyper_v,
    shared,
):
    @pl.when(pl.program_id(0) == 0)
    def _():
        coded_grad = small_ref[0:16, 0:64]
        tokens = small_ref[24:25, 1:2]
        loss_ref[...] = small_ref[24:25, 0:1]
        tokens_ref[...] = tokens
        pairs = pair_rows(embeds[...])
        before = exact(pairs, one[...], ((1,), (0,)))
        tanh = gelu_tanh(before)
        active = (0.5 * before) * (1.0 + tanh)
        grad_two = exact(active, coded_grad, ((0,), (0,)))
        grad_before = exact(coded_grad, two[...], ((1,), (1,))) * gelu_slope(before, tanh)
        grad_one = exact(pairs, grad_before, ((0,), (0,)))
        grad_pairs = exact(grad_before, one[...], ((1,), (1,)))
        row = lax.broadcasted_iota(jnp.int32, (16, TASKS * LAYERS), 0)
        column = lax.broadcasted_iota(jnp.int32, (16, TASKS * LAYERS), 1)
        chosen = (row == column // LAYERS) & (row < TASKS) | (row == TASKS + column % LAYERS)
        grad_embeds = exact(chosen.astype(jnp.float32), grad_pairs, ((1,), (0,)))
        grad_embeds = grad_embeds[: TASKS + LAYERS]
        scale = 1.0 / tokens
        grads = [grad * scale for grad in (grad_embeds, grad_one, grad_two)]
        square = small_ref[16:17, 0:1] * scale * scale
        for grad in grads:
            square = square + jnp.sum(
                jnp.sum(grad * grad, axis=1, keepdims=True), axis=0, keepdims=True
            )
        norm = jnp.sqrt(square)
        norm_ref[...] = norm
        factor = jnp.minimum(1.0, clip_limit / (norm + 1e-06))
        shared[...] = jnp.broadcast_to(
            jnp.concatenate([scale, factor] + [jnp.zeros((1, 126), jnp.float32)], axis=1), (8, 128)
        )
        for index, (weight, first, second, outs) in enumerate(
            (
                (embeds, embeds_m, embeds_v, (new_embeds, new_embeds_m, new_embeds_v)),
                (one, one_m, one_v, (new_one, new_one_m, new_one_v)),
                (two, two_m, two_v, (new_two, new_two_m, new_two_v)),
            )
        ):
            for out, value in zip(
                outs,
                adamw(weight[...], first[...], second[...], grads[index] * factor, rates[index]),
            ):
                out[...] = value

    scale = shared[0:1, 0:1]
    factor = shared[0:1, 1:2]
    grad = exact(coded_ref[...], slots_ref[...], ((0,), (0,)))
    for out, value in zip(
        (new_hyper, new_hyper_m, new_hyper_v),
        adamw(hyper[...], hyper_m[...], hyper_v[...], (grad * scale) * factor, rates[3]),
    ):
        out[...] = value


def update(slots, small, coded, *weights):
    full = jnp.float32
    width = slots.shape[1]
    block = width // UPDATE_STEPS

    def kept(array):
        return pl.BlockSpec(array.shape, lambda i: (0, 0))

    def cut(array):
        return pl.BlockSpec((array.shape[0], block), lambda i: (0, i))

    one_value = jax.ShapeDtypeStruct((1, 1), full)
    arrays = list(weights)
    return pl.pallas_call(
        update_kernel,
        grid=(UPDATE_STEPS,),
        out_shape=[one_value] * 3 + [jax.ShapeDtypeStruct(w.shape, full) for w in arrays],
        in_specs=[cut(slots), kept(small), kept(coded)]
        + [kept(w) for w in arrays[:9]]
        + [cut(w) for w in arrays[9:]],
        out_specs=[kept(one_value)] * 3
        + [kept(w) for w in arrays[:9]]
        + [cut(w) for w in arrays[9:]],
        scratch_shapes=[pltpu.VMEM((8, 128), full)],
        compiler_params=pltpu.CompilerParams(vmem_limit_bytes=40 * 1024 * 1024),
        name="update",
    )(slots, small, coded, *arrays)


def per_device(
    src_ids,
    tgt_ids,
    task_ids,
    task_len,
    tgt_count,
    table,
    attn_w,
    ffn_in,
    ffn_out,
    gains,
    embeds,
    embeds_m,
    embeds_v,
    proj_one,
    proj_one_m,
    proj_one_v,
    proj_two,
    proj_two_m,
    proj_two_v,
    hyper,
    hyper_m,
    hyper_v,
):
    rows, adapters, info, sel, coded, crowded = prep(
        task_ids, task_len, tgt_count, src_ids, tgt_ids, embeds, proj_one, proj_two, hyper, table
    )
    slow = lax.cond(
        crowded[0] > 0,
        crowded_rows,
        lambda src_ids, tgt_ids, table: jnp.zeros((SEQ_DEV * (SRC + 2 * TGT), D), table.dtype),
        src_ids,
        tgt_ids,
        table,
    )
    slots, small = step(
        adapters, info, sel, coded, gains, rows, slow, hyper, attn_w, ffn_in, ffn_out, table
    )
    weights = (
        embeds, embeds_m, embeds_v,
        proj_one, proj_one_m, proj_one_v,
        proj_two, proj_two_m, proj_two_v,
        hyper, hyper_m, hyper_v,
    )
    loss_sum, token_count, grad_norm, *updated = update(slots, small, coded, *weights)
    return (loss_sum.reshape(()), token_count.reshape(()), grad_norm.reshape(()), *updated)


def solution(mesh):
    return jax.shard_map(
        per_device,
        mesh=mesh,
        in_specs=(
            P("dp", None),
            P("dp", None),
            P("dp"),
            P(),
            P("dp"),
            P("gen", None),
            P(),
            P(),
            P(),
            P(),
            P(),
            P(),
            P(),
            P(),
            P(),
            P(),
            P(),
            P(),
            P(),
            P(None, "gen"),
            P(None, "gen"),
            P(None, "gen"),
        ),
        out_specs=(
            P(),
            P(),
            P(),
            P(),
            P(),
            P(),
            P(),
            P(),
            P(),
            P(),
            P(),
            P(),
            P(None, "gen"),
            P(None, "gen"),
            P(None, "gen"),
        ),
        check_vma=False,
    )
```

```python
import math
from functools import partial

import jax
import jax.numpy as jnp
from jax import lax
from jax.experimental import pallas as pl
from jax.experimental.pallas import tpu as pltpu
from jax.sharding import PartitionSpec as P

D = 512
HEADS = 8
ADAPTER = 24
TASKS = 8
LAYERS = 2
SRC = 256
TGT = 128
FF = 2048
SEQ_DEV = 2
GEN = 4
LOW = 128
SRC_CAP = 176
TGT_CAP = 128
FLAT = 48
STEP = 5


epsilon = 1e-06
clip_limit = 0.001
beta_one = 0.9
beta_two = 0.999
adam_floor = 1e-08
weight_decay = 0.01
rates = (0.5, 0.1, 0.1, 0.005)
blocked = -1000000000.0
highest = lax.Precision.HIGHEST
LOGIT_SCALE = D ** (-0.5)
EXP_SCALE = LOGIT_SCALE / math.log(2.0)
UPSCALE = math.sqrt(D / ADAPTER)
GELU_A = math.sqrt(2.0 / math.pi)
GELU_B = 0.044715
VOCAB_TILE = 2048
UPDATE_STEPS = 4
WIDE = 5472
VMEM_LIMIT = 62 * 1024 * 1024
MESH = pl.DeviceIdType.MESH


def adamw(weight, first, second, grad, rate):
    first = beta_one * first + (1.0 - beta_one) * grad
    second = beta_two * second + (1.0 - beta_two) * grad * grad
    corrected = first * (1.0 / (1.0 - beta_one**STEP))
    spread = jnp.sqrt(second * (1.0 / (1.0 - beta_two**STEP))) + adam_floor
    return (weight - rate * (corrected / spread + weight_decay * weight), first, second)


def mm(left, right):
    return lax.dot_general(
        left, right, (((1,), (0,)), ((), ())), preferred_element_type=jnp.float32
    )


def mm_last(left, right):
    return lax.dot_general(
        left, right, (((1,), (1,)), ((), ())), preferred_element_type=jnp.float32
    )


def mm_first(left, right):
    return lax.dot_general(
        left, right, (((0,), (0,)), ((), ())), preferred_element_type=jnp.float32
    )


def exact(left, right, dims):
    return lax.dot_general(
        left, right, (dims, ((), ())), precision=highest, preferred_element_type=jnp.float32
    )


def norm_scale(value):
    return lax.rsqrt(jnp.mean(value * value, axis=-1, keepdims=True) + epsilon)


def normed(value, gain):
    return (value * norm_scale(value) * gain).astype(jnp.bfloat16)


def norm_back(value, gain, grad):
    scale = norm_scale(value)
    weighted = grad * gain
    return scale * weighted - value * (
        scale * scale * scale * jnp.mean(weighted * value, axis=-1, keepdims=True)
    )


def gelu_tanh(value):
    return jnp.tanh(value * (GELU_A + (GELU_A * GELU_B) * (value * value)))


def gelu(value):
    return (0.5 * value) * (1.0 + gelu_tanh(value))


def gelu_slope(value, tanh):
    return 0.5 * (1.0 + tanh) + (0.5 * value) * (1.0 - tanh * tanh) * (
        GELU_A + (3.0 * GELU_A * GELU_B) * (value * value)
    )


def halves():
    lane = lax.broadcasted_iota(jnp.int32, (1, 128), 1)
    return [(lane // 64 == half) for half in range(2)]


def attend(q_ref, kv_ref, k_col, v_col, q_len, k_len, allow, out_ref, probs_ref=None):
    sides = halves()
    masks = [side.astype(jnp.float32).astype(jnp.bfloat16) for side in sides]

    def pair_step(pair, carry):
        lanes = pl.multiple_of(pair * 128, 128)
        for seq in range(SEQ_DEV):
            q_rows = pl.ds(seq * q_len, q_len)
            k_rows = pl.ds(seq * k_len, k_len)
            query = q_ref[q_rows, pl.ds(lanes, 128)]
            keys = kv_ref[k_rows, pl.ds(k_col + lanes, 128)]
            values = kv_ref[k_rows, pl.ds(v_col + lanes, 128)]
            outs = []
            for half in range(2):
                scores = mm_last(query * masks[half], keys) * 0.125
                scores = jnp.where(allow(seq), scores, blocked)
                peak = jnp.max(scores, axis=-1, keepdims=True)
                weights = jnp.exp(scores - peak)
                probs = weights * (1.0 / jnp.sum(weights, axis=-1, keepdims=True))
                if probs_ref is not None:
                    begin = pl.multiple_of((pair * SEQ_DEV + seq) * q_len, 8)
                    probs_ref[pl.ds(begin, q_len), half * k_len : (half + 1) * k_len] = probs
                outs.append(mm(probs.astype(jnp.bfloat16), values))
            out_ref[q_rows, pl.ds(lanes, 128)] = jnp.where(sides[0], outs[0], outs[1]).astype(
                jnp.bfloat16
            )
        return carry

    lax.fori_loop(0, HEADS // 2, pair_step, 0)


def attend_back(grad_ref, q_ref, kv_ref, probs_ref, q_len, k_len, joined_ref):
    sides = halves()
    masks = [side.astype(jnp.float32).astype(jnp.bfloat16) for side in sides]

    def pair_step(pair, carry):
        lanes = pl.multiple_of(pair * 128, 128)
        for seq in range(SEQ_DEV):
            q_rows = pl.ds(seq * q_len, q_len)
            k_rows = pl.ds(seq * k_len, k_len)
            grad = grad_ref[q_rows, pl.ds(lanes, 128)]
            query = q_ref[q_rows, pl.ds(lanes, 128)]
            values = kv_ref[k_rows, pl.ds(D + lanes, 128)]
            key_grads, value_grads = [], []
            for half in range(2):
                begin = pl.multiple_of((pair * SEQ_DEV + seq) * q_len, 8)
                probs = probs_ref[pl.ds(begin, q_len), half * k_len : (half + 1) * k_len]
                grad_probs = mm_last(grad * masks[half], values)
                value_grads.append(mm_first(probs.astype(jnp.bfloat16), grad))
                inner = jnp.sum(grad_probs * probs, axis=-1, keepdims=True)
                grad_scores = (probs * (grad_probs - inner)).astype(jnp.bfloat16)
                key_grads.append(mm_first(grad_scores, query))
            joined_ref[k_rows, pl.ds(lanes, 128)] = (
                jnp.where(sides[0], key_grads[0], key_grads[1]) * 0.125
            ).astype(jnp.bfloat16)
            joined_ref[k_rows, pl.ds(D + lanes, 128)] = jnp.where(
                sides[0], value_grads[0], value_grads[1]
            ).astype(jnp.bfloat16)
        return carry

    lax.fori_loop(0, HEADS // 2, pair_step, 0)


def feed(state_ref, gain, inner_ref, outer_ref, act_ref, slope_ref, down_ref, up_ref, length,
         plain_ref, low_ref, after_ref):
    rows = SEQ_DEV * length
    act_rows = pl.ds(0, rows)
    source = normed(state_ref[...], gain)
    for block in range(FF // D):
        columns = slice(block * D, (block + 1) * D)
        hidden = mm(source, inner_ref[:, columns])
        tanh = gelu_tanh(hidden)
        act_ref[act_rows, columns] = ((0.5 * hidden) * (1.0 + tanh)).astype(jnp.bfloat16)
        if slope_ref is not None:
            slope_ref[pl.ds(block * rows, rows), :] = gelu_slope(hidden, tanh)
    branch = mm(act_ref[act_rows, :], outer_ref[...])
    plain_ref[...] = branch.astype(jnp.bfloat16)
    for seq in range(SEQ_DEV):
        span = slice(seq * length, (seq + 1) * length)
        lowered = mm(plain_ref[span, :], down_ref[seq])
        low_ref[span, :] = lowered
        adapted = mm(gelu(lowered).astype(jnp.bfloat16), up_ref[seq]) * UPSCALE
        after_ref[span, :] = state_ref[span, :] + branch[span, :] + adapted


def adapter_back(grad_ref, low_ref, plain_ref, down_ref, up_ref, length, grad_down_ref,
                 grad_up_ref, branch_ref=None):
    for seq in range(SEQ_DEV):
        span = slice(seq * length, (seq + 1) * length)
        grad = grad_ref[span, :]
        grad_low = grad.astype(jnp.bfloat16)
        lowered = low_ref[span, :]
        tanh = gelu_tanh(lowered)
        bottleneck = ((0.5 * lowered) * (1.0 + tanh)).astype(jnp.bfloat16)
        grad_bottle = mm_last(grad_low, up_ref[seq]) * UPSCALE
        grad_up_ref(seq)[...] = mm_first(bottleneck, grad_low)[:ADAPTER] * UPSCALE
        grad_lowered = (grad_bottle * gelu_slope(lowered, tanh)).astype(jnp.bfloat16)
        grad_down_ref(seq)[...] = mm_first(plain_ref[span, :], grad_lowered)
        if branch_ref is not None:
            branch_ref[span, :] = (grad + mm_last(grad_lowered, down_ref[seq])).astype(
                jnp.bfloat16
            )


def pair_rows(embeds):
    return jnp.concatenate(
        [
            embeds[task : task + 1, :] + embeds[TASKS + layer : TASKS + layer + 1, :]
            for task in range(TASKS)
            for layer in range(LAYERS)
        ],
        axis=0,
    )


def place_rows(src_ref, tgt_ref, member, peer, part, done):
    offset = member * part
    wide_tokens = SEQ_DEV * SRC
    order = lax.broadcasted_iota(jnp.int32, (wide_tokens, wide_tokens), 0)
    upto = (
        (order <= lax.broadcasted_iota(jnp.int32, (wide_tokens, wide_tokens), 1))
        .astype(jnp.float32)
        .astype(jnp.bfloat16)
    )
    crowded = jnp.zeros((1, 1), jnp.float32)
    slots, wanted = [], []
    for ids_ref, length, rows in ((src_ref, SRC, SRC_CAP), (tgt_ref, TGT, TGT_CAP)):
        count = SEQ_DEV * length
        ids = jnp.concatenate(
            [
                jnp.concatenate(
                    [ids_ref[pl.ds(SEQ_DEV * peer(k) + s, 1), :] for s in range(SEQ_DEV)], axis=1
                )
                for k in range(GEN)
            ],
            axis=0,
        )
        if length == TGT:
            lane = lax.broadcasted_iota(jnp.int32, (GEN, 128), 1)
            ids = jnp.concatenate([ids, jnp.where(lane == 0, 0, -1)], axis=1)
            count = count + 128
        own = ids[0:1]
        local = ids - offset
        inside = ((local >= 0) & (local < part) & (ids >= 0)).astype(jnp.float32)
        held = [
            ((own >= part * o) & (own < part * (o + 1))).astype(jnp.float32) for o in range(GEN)
        ]
        marks = jnp.concatenate([inside] + held, axis=0)
        ranks = mm(marks.astype(jnp.bfloat16), upto[:count, :count]) - 1.0
        ranks = ranks - (done * count).astype(jnp.float32)
        for o in range(GEN):
            amount = ((ids >= part * o) & (ids < part * (o + 1))).astype(jnp.float32)
            most = jnp.max(jnp.sum(amount, axis=1, keepdims=True), axis=0, keepdims=True)
            crowded = jnp.maximum(crowded, (most > float(rows)).astype(jnp.float32))
        numbers = local.astype(jnp.float32) + 1.0
        spot = lax.broadcasted_iota(jnp.int32, (rows, count), 0).astype(jnp.float32)
        columns = []
        for k in range(GEN):
            position = jnp.where(inside[k : k + 1] > 0.0, ranks[k : k + 1], -1.0)
            columns.append(
                jnp.sum(jnp.where(spot == position, numbers[k : k + 1], 0.0), axis=1, keepdims=True)
                - 1.0
            )
        wanted.append(columns)
        slot = jnp.full((1, count), -1.0, jnp.float32)
        for o in range(GEN):
            rank = ranks[GEN + o : GEN + o + 1]
            now = (held[o] > 0.0) & (rank >= 0.0) & (rank < float(rows))
            slot = jnp.where(now, rank + float(o * rows), slot)
        slots.append(slot)
    targets = SEQ_DEV * TGT
    lane = lax.broadcasted_iota(jnp.int32, (1, targets), 1)
    shifted = jnp.where(
        lax.rem(lane, TGT) == 0,
        slots[1][:, targets : targets + 1],
        pltpu.roll(slots[1][:, :targets], 1, axis=1),
    )
    return wanted, slots[0], shifted, slots[1][:, :targets], crowded


def describe(task_ref, lens_ref, count_ref, member):
    own_first = member * SEQ_DEV
    position = lax.broadcasted_iota(jnp.int32, (1, SRC), 1)
    place = lax.broadcasted_iota(jnp.int32, (1, TGT), 1)
    task = lax.broadcasted_iota(jnp.int32, (1, TASKS), 1)
    allow, valid = [], []
    tokens = jnp.zeros((1, 1), jnp.float32)
    for s in range(SEQ_DEV):
        length = jnp.sum(
            jnp.where(task == task_ref[own_first + s], lens_ref[...], 0).astype(jnp.float32),
            axis=1,
            keepdims=True,
        )
        allow.append((position.astype(jnp.float32) < length).astype(jnp.float32))
        valid.append((place < count_ref[own_first + s]).astype(jnp.float32))
        tokens = tokens + jnp.sum(valid[-1], axis=1, keepdims=True)
    return jnp.concatenate(allow, axis=1), jnp.concatenate(valid, axis=1), tokens


def generate(task_ref, embeds_ref, one_ref, two_ref, hyper_ref, coded_ref, chosen,
             adapters, sel):
    coded = exact(
        gelu(exact(pair_rows(embeds_ref[...]), one_ref[...], ((1,), (0,)))),
        two_ref[...],
        ((1,), (1,)),
    )
    coded_ref[...] = coded
    flat = exact(coded, hyper_ref[...], ((1,), (0,))).astype(jnp.bfloat16)
    pairs = TASKS * LAYERS
    sequences = GEN * SEQ_DEV
    row_of = lax.broadcasted_iota(jnp.int32, (pairs, pairs), 0)
    column_of = lax.broadcasted_iota(jnp.int32, (pairs, pairs), 1)
    picks = jnp.zeros((pairs, pairs), jnp.float32)
    selector = jnp.zeros((pairs, pairs), jnp.float32)
    for seq in range(sequences):
        for layer in range(LAYERS):
            pair = task_ref[seq] * LAYERS + layer
            picks = jnp.where(
                (row_of == seq * LAYERS + layer) & (column_of == pair), 1.0, picks
            )
            selector = jnp.where(
                (row_of == pair) & (column_of == layer * sequences + seq), 1.0, selector
            )
    sel[...] = selector
    taken = mm(picks.astype(jnp.bfloat16), flat)
    for tile in range(FLAT):
        chosen[pl.ds(tile, pairs, stride=FLAT), :] = taken[:, 128 * tile : 128 * (tile + 1)]
    share = SEQ_DEV * LAYERS * FLAT
    for target in range(GEN):
        adapters[target] = chosen[pl.ds(target * share, share), :].astype(jnp.bfloat16)


def step_kernel(
    done_ref,
    task_ref,
    count_ref,
    lens_ref,
    src_ref,
    tgt_ref,
    embeds_ref,
    one_ref,
    two_ref,
    gains_ref,
    known_hbm,
    hyper_hbm,
    attn_hbm,
    inner_hbm,
    outer_hbm,
    table_hbm,
    out_ref,
    small_ref,
    coded_ref,
    missing_ref,
    attn,
    inner,
    outer,
    table,
    wide,
    plain_e,
    qkv,
    mixed,
    act,
    memory,
    q_cross,
    plain_d,
    feats,
    stats,
    stats_in,
    grad_low,
    rows_out,
    known,
    src_in,
    tgt_in,
    generated,
    spread,
    adapters_ref,
    adapters_in,
    sel_ref,
    down_ref,
    up_ref,
    pack,
    grads_in,
    hyper,
    outgoing,
    incoming,
    shares,
    summary,
    summary_in,
    verdict_in,
    load_sem,
    row_send,
    src_recv,
    tgt_recv,
    adapter_recv,
    grad_send,
    grad_recv,
    scatter_sem,
    share_sem,
    small_send,
    small_recv,
    verdict_sem,
    feat_send,
    feat_recv,
    result_send,
    result_recv,
    stat_send,
    stat_recv,
):
    member = lax.axis_index("gen")
    barrier = pltpu.get_barrier_semaphore()
    sources = SEQ_DEV * SRC
    targets = SEQ_DEV * TGT
    own = pl.ds(0, targets)
    part = table.shape[0]

    spans = []

    def view(rows, lanes=None):
        begin = spans[-1] if spans else 0
        if lanes is None:
            spans.append(begin + rows)
            return wide.at[pl.ds(begin, rows)]
        return wide.at[pl.ds(begin, rows), lanes]

    state, after_e, grad = view(sources), view(sources), view(sources)
    y1, y2, y3, total, wanted = (view(targets) for _ in range(5))
    slope = view(targets * (FF // D))
    probs = view(SEQ_DEV * HEADS // 2 * TGT)
    low_e = view(sources, pl.ds(0, LOW))
    low_d = view(targets, pl.ds(LOW, LOW))
    view(sources)
    first_up = spans[-1]
    view(LAYERS * SEQ_DEV * ADAPTER)

    def grad_down_ref(seq):
        return spread.at[pl.ds(seq * D, D)]

    def grad_up_ref(layer, seq):
        begin = first_up + (layer * SEQ_DEV + seq) * ADAPTER
        return wide.at[pl.ds(begin, ADAPTER)]

    def flat_in(owner):
        return generated.at[pl.ds(owner * SEQ_DEV * LAYERS * FLAT, SEQ_DEV * LAYERS * FLAT)]

    kv_cross = attn.at[0, :, pl.ds(0, 2 * D)]
    joined = attn.at[0, :, pl.ds(2 * D, 2 * D)]

    def results(order):
        return outer.at[0, pl.ds(pl.multiple_of(order * targets, targets), targets)]

    def arrived(order):
        begin = pl.multiple_of((GEN + order) * targets, targets)
        return outer.at[0, pl.ds(begin, targets)]

    def peer(order):
        chip = lax.rem(member // 2 + lax.rem((order + 1) // 2, 2), 2)
        return chip * 2 + lax.rem(lax.rem(member, 2) + order // 2, 2)

    rank = lax.axis_index("dp")
    count = outgoing.shape[0]
    width = TASKS * LAYERS * FLAT * 128 // (TASKS * LAYERS * count)
    loads = []

    def load(source, target):
        loads.append(pltpu.make_async_copy(source, target, load_sem.at[len(loads)]))
        loads[-1].start()
        return loads[-1]

    cuts = [0, 2048, 4096, 6144, part]
    table_loads = [
        load(
            table_hbm.at[pl.ds(cuts[i], cuts[i + 1] - cuts[i])],
            table.at[pl.ds(cuts[i], cuts[i + 1] - cuts[i])],
        )
        for i in range(4)
    ]
    hyper_load = load(hyper_hbm, hyper)
    known_load = load(known_hbm.at[pl.ds(0, known.shape[0])], known)
    for order in range(1, GEN):
        pl.semaphore_signal(
            barrier, inc=1, device_id={"gen": peer(order)}, device_id_type=MESH
        )

    def greet(step, carry):
        pl.semaphore_signal(
            barrier, inc=1, device_id={"dp": lax.rem(rank + step, count)}, device_id_type=MESH
        )
        return carry

    lax.fori_loop(1, count, greet, 0)
    weight_loads = [
        load(source, target)
        for source, target in (
            (attn_hbm.at[0], attn.at[0]),
            (inner_hbm.at[0], inner.at[0]),
            (outer_hbm.at[0], outer.at[0]),
            (attn_hbm.at[1], attn.at[1]),
            (attn_hbm.at[2], attn.at[2]),
            (inner_hbm.at[1], inner.at[1]),
            (outer_hbm.at[1], outer.at[1]),
        )
    ]

    (source_rows, target_rows), source_slot, input_slot, target_slot, crowded = place_rows(
        src_ref, tgt_ref, member, peer, part, done_ref[0]
    )

    def gather(columns, begin, orders, first=False):
        numbers = jnp.concatenate([columns[order] for order in orders], axis=0)
        height = numbers.shape[0]
        found = None
        for i in range(len(cuts) - 1):
            if first:
                table_loads[i].wait()
            lane = lax.broadcasted_iota(jnp.int32, (height, cuts[i + 1] - cuts[i]), 1)
            hit = ((lane + cuts[i]).astype(jnp.float32) == numbers).astype(jnp.float32)
            piece = mm(hit.astype(jnp.bfloat16), table[cuts[i] : cuts[i + 1], :])
            found = piece if found is None else found + piece
        size = height // len(orders)
        for place, order in enumerate(orders):
            rows_out[peer(order), pl.ds(begin, size), :] = found[
                place * size : (place + 1) * size
            ].astype(jnp.bfloat16)

    def source_copy(owner, target):
        return pltpu.make_async_remote_copy(
            src_ref=rows_out.at[target, pl.ds(0, SRC_CAP)],
            dst_ref=src_in.at[owner],
            send_sem=row_send.at[0, target],
            recv_sem=src_recv.at[owner],
            device_id={"gen": target},
            device_id_type=MESH,
        )

    def target_copy(owner, target):
        return pltpu.make_async_remote_copy(
            src_ref=rows_out.at[target, pl.ds(SRC_CAP, TGT_CAP)],
            dst_ref=tgt_in.at[owner],
            send_sem=row_send.at[1, target],
            recv_sem=tgt_recv.at[owner],
            device_id={"gen": target},
            device_id_type=MESH,
        )

    def adapter_copy(owner, target):
        return pltpu.make_async_remote_copy(
            src_ref=adapters_ref.at[target],
            dst_ref=adapters_in.at[owner],
            send_sem=row_send.at[2, target],
            recv_sem=adapter_recv.at[owner],
            device_id={"gen": target},
            device_id_type=MESH,
        )

    pl.semaphore_wait(barrier, GEN + count - 2)
    gather(source_rows, 0, (1, 2), True)
    for order in (1, 2):
        source_copy(member, peer(order)).start()
    hyper_load.wait()
    generate(task_ref, embeds_ref, one_ref, two_ref, hyper, coded_ref, generated, adapters_ref,
             sel_ref)
    for order in range(1, GEN):
        adapter_copy(member, peer(order)).start()
    gather(target_rows, SRC_CAP, (1, 2))
    for order in (1, 2):
        target_copy(member, peer(order)).start()
    gather(source_rows, 0, (3, 0))
    source_copy(member, peer(3)).start()
    gather(target_rows, SRC_CAP, (3, 0))
    target_copy(member, peer(3)).start()
    src_in[member] = rows_out[member, 0:SRC_CAP, :]
    tgt_in[member] = rows_out[member, SRC_CAP : SRC_CAP + TGT_CAP, :]
    adapters_in[member] = adapters_ref[member]
    allow, valid, tokens = describe(task_ref, lens_ref, count_ref, member)

    def spread_rows(slot, incoming_rows, owner):
        height = incoming_rows.shape[1]
        spot = lax.broadcasted_iota(jnp.int32, (height, slot.shape[1]), 0)
        spot = (spot + owner * height).astype(jnp.float32)
        chosen = (spot == slot).astype(jnp.float32)
        return mm_first(chosen.astype(jnp.bfloat16), incoming_rows[owner])

    known_load.wait()

    def known_rows(begin, size):
        rows = known[begin : begin + size, :].astype(jnp.float32)
        return jnp.where(done_ref[0] > 0, rows, 0.0)

    after_e[...] = known_rows(0, sources) + spread_rows(
        source_slot, src_in, member
    )
    for order in (3, 1, 2):
        source_copy(peer(order), peer(order)).wait_recv()
        after_e[...] = after_e[...] + spread_rows(source_slot, src_in, peer(order))
    embedded = after_e[...]

    def allowed(seq):
        return allow[:, seq * SRC : (seq + 1) * SRC] > 0.0

    entry = normed(embedded, gains_ref[0:1])
    weight_loads[0].wait()
    for block in range(3):
        columns = slice(block * D, (block + 1) * D)
        qkv[:, columns] = mm(entry, attn[0, :, columns]).astype(jnp.bfloat16)
    attend(qkv, qkv, D, 2 * D, SRC, SRC, allowed, mixed)
    state[...] = embedded + mm(mixed[...], attn[0, :, 3 * D :])
    weight_loads[1].wait()
    weight_loads[2].wait()
    for order in range(1, GEN):
        adapter_copy(peer(order), peer(order)).wait_recv()
    unpack_adapters(adapters_in, flat_in, spread, down_ref, up_ref)
    feed(state, gains_ref[1:2], inner.at[0], outer.at[0], act, None, down_ref.at[0], up_ref.at[0],
         SRC, plain_e, low_e, after_e)
    memory[...] = normed(after_e[...], gains_ref[2:3])

    for order in range(1, GEN):
        target_copy(peer(order), peer(order)).wait_recv()
    inputs = known_rows(sources, targets)
    for owner in range(GEN):
        inputs = inputs + spread_rows(input_slot, tgt_in, owner)
    entry = normed(inputs, gains_ref[3:4])
    weight_loads[3].wait()
    for block in range(3):
        columns = slice(block * D, (block + 1) * D)
        qkv[own, columns] = mm(entry, attn[1, :, columns]).astype(jnp.bfloat16)
    causal = lax.broadcasted_iota(jnp.int32, (TGT, TGT), 0) >= lax.broadcasted_iota(
        jnp.int32, (TGT, TGT), 1
    )
    attend(qkv, qkv, D, 2 * D, TGT, TGT, lambda seq: causal, mixed)
    y1[...] = inputs + mm(mixed[own, :], attn[1, :, 3 * D :])
    weight_loads[4].wait()
    q_cross[...] = mm(normed(y1[...], gains_ref[4:5]), attn[2, :, :D]).astype(jnp.bfloat16)
    for block in range(2):
        columns = slice(block * D, (block + 1) * D)
        kv_cross[:, columns] = mm(
            memory[...], attn[2, :, (block + 1) * D : (block + 2) * D]
        ).astype(jnp.bfloat16)
    attend(q_cross, kv_cross, 0, D, TGT, SRC, allowed,
           mixed, probs)
    y2[...] = y1[...] + mm(mixed[own, :], attn[2, :, 3 * D :])
    weight_loads[5].wait()
    weight_loads[6].wait()
    feed(y2, gains_ref[5:6], inner.at[1], outer.at[1], act, slope, down_ref.at[1], up_ref.at[1],
         TGT, plain_d, low_d, y3)
    feats[0] = normed(y3[...], gains_ref[6:7])


    def feature_copy(order):
        return pltpu.make_async_remote_copy(
            src_ref=feats.at[0],
            dst_ref=feats.at[order],
            send_sem=feat_send.at[order],
            recv_sem=feat_recv.at[order],
            device_id={"gen": peer(order)},
            device_id_type=MESH,
        )

    def result_copy(order):
        return pltpu.make_async_remote_copy(
            src_ref=results(order),
            dst_ref=arrived(order),
            send_sem=result_send.at[order],
            recv_sem=result_recv.at[order],
            device_id={"gen": peer(order)},
            device_id_type=MESH,
        )

    def stat_copy(order):
        return pltpu.make_async_remote_copy(
            src_ref=stats.at[order],
            dst_ref=stats_in.at[order],
            send_sem=stat_send.at[order],
            recv_sem=stat_recv.at[order],
            device_id={"gen": peer(order)},
            device_id_type=MESH,
        )

    for order in range(1, GEN):
        feature_copy(order).start()
    wanted[...] = known_rows(sources + targets, targets)
    for owner in range(GEN):
        wanted[...] = wanted[...] + spread_rows(target_slot, tgt_in, owner)
    same = lax.broadcasted_iota(jnp.int32, (targets, targets), 0) == lax.broadcasted_iota(
        jnp.int32, (targets, targets), 1
    )

    def as_row(column):
        return jnp.sum(jnp.where(same, column, 0.0), axis=0, keepdims=True)

    def as_column(row):
        return jnp.sum(jnp.where(same, row, 0.0), axis=1, keepdims=True)

    def block_step(order, carry):
        @pl.when(order > 0)
        def _():
            feature_copy(order).wait_recv()

        query = feats[order]
        ends = list(range(0, table.shape[0], VOCAB_TILE)) + [table.shape[0]]
        tiles = [(ends[i], ends[i + 1]) for i in range(len(ends) - 1)]
        peak = scale = None
        scores = mm_last(query, table[tiles[0][0] : tiles[0][1], :])
        for index, (first, last) in enumerate(tiles):
            following = None
            if index + 1 < len(tiles):
                following = mm_last(query, table[tiles[index + 1][0] : tiles[index + 1][1], :])
            top = jnp.max(scores, axis=-1, keepdims=True)
            if index > 0:
                top = jnp.maximum(peak, top)
            weights = jnp.exp2((scores - top) * EXP_SCALE)
            amount = jnp.sum(weights, axis=-1, keepdims=True)
            part = mm(weights.astype(jnp.bfloat16), table[first:last, :])
            if index == 0:
                total[...] = part
                scale = amount
            else:
                shrink = jnp.exp2((peak - top) * EXP_SCALE)
                total[...] = total[...] * shrink + part
                scale = scale * shrink + amount
            peak, scores = top, following
        results(order)[...] = total[...].astype(jnp.bfloat16)
        stats[order] = jnp.concatenate(
            [as_row(peak), as_row(scale), jnp.zeros((6, targets), jnp.float32)], axis=0
        )

        @pl.when(order > 0)
        def _():
            result_copy(order).start()
            stat_copy(order).start()

        return carry

    lax.fori_loop(0, GEN, block_step, 0)
    stats_in[0] = stats[0]
    for order in range(1, GEN):
        stat_copy(order).wait_recv()
    peaks = [as_column(stats_in[order, 0:1, :]) for order in range(GEN)]
    sums = [as_column(stats_in[order, 1:2, :]) for order in range(GEN)]
    top = jnp.maximum(jnp.maximum(peaks[0], peaks[1]), jnp.maximum(peaks[2], peaks[3]))
    parts = [jnp.exp2((peaks[order] - top) * EXP_SCALE) for order in range(GEN)]
    amount = sum(parts[order] * sums[order] for order in range(GEN))
    logsum = top * LOGIT_SCALE + jnp.log(amount)
    inverse = 1.0 / amount
    total[...] = results(0)[...].astype(jnp.float32) * (parts[0] * inverse)
    for order in range(1, GEN):
        result_copy(order).wait_recv()
        total[...] = total[...] + arrived(order)[...].astype(jnp.float32) * (parts[order] * inverse)
    picked = (
        jnp.sum(feats[0].astype(jnp.float32) * wanted[...], axis=-1, keepdims=True) * LOGIT_SCALE
    )
    counted = as_column(valid)
    loss = jnp.sum((logsum - picked) * counted, axis=0, keepdims=True)
    lane = lax.broadcasted_iota(jnp.int32, (8, 128), 1)
    totals = jnp.where(
        lane == 0, loss, jnp.where(lane == 1, tokens, jnp.where(lane == 2, crowded, 0.0))
    )

    grad[own, :] = norm_back(
        y3[...], gains_ref[6:7], (total[...] - wanted[...]) * (counted * LOGIT_SCALE)
    )
    adapter_back(grad.at[own], low_d, plain_d, down_ref.at[1], up_ref.at[1], TGT,
                 grad_down_ref, partial(grad_up_ref, 1), grad_low)

    def grad_copy(layer, owner, target):
        part = SEQ_DEV * FLAT
        begin = pl.multiple_of((layer * GEN + owner) * part, 8)
        return pltpu.make_async_remote_copy(
            src_ref=pack.at[layer, target],
            dst_ref=grads_in.at[pl.ds(begin, part)],
            send_sem=grad_send.at[layer, target],
            recv_sem=grad_recv.at[layer, owner],
            device_id={"gen": target},
            device_id_type=MESH,
        )

    def send_grads(layer):
        pack_grads(grad_down_ref, partial(grad_up_ref, layer), pack.at[layer])
        for order in range(1, GEN):
            grad_copy(layer, member, peer(order)).start()
        begin = pl.multiple_of((layer * GEN + member) * SEQ_DEV * FLAT, 8)
        grads_in[pl.ds(begin, SEQ_DEV * FLAT), :] = pack[layer, member]

    send_grads(1)
    for block in range(FF // D):
        columns = slice(block * D, (block + 1) * D)
        act[own, columns] = (
            mm_last(grad_low[...], outer[1, columns, :])
            * slope[pl.ds(block * targets, targets), :]
        ).astype(jnp.bfloat16)
    grad_entry = mm_last(act[own, :], inner[1])
    grad_state = grad[own, :] + norm_back(y2[...], gains_ref[5:6], grad_entry)
    mixed[own, :] = mm_last(grad_state.astype(jnp.bfloat16), attn[2, :, 3 * D :]).astype(
        jnp.bfloat16
    )
    attend_back(mixed, q_cross, kv_cross, probs, TGT, SRC, joined)
    grad_memory = mm_last(joined[...], attn[2, :, D : 3 * D])

    grad[...] = norm_back(after_e[...], gains_ref[2:3], grad_memory)
    adapter_back(grad, low_e, plain_e, down_ref.at[0], up_ref.at[0], SRC,
                 grad_down_ref, partial(grad_up_ref, 0))
    send_grads(0)
    for layer in range(LAYERS):
        for order in range(1, GEN):
            grad_copy(layer, peer(order), peer(order)).wait_recv()
    pairs = TASKS * LAYERS
    received = jnp.concatenate(
        [grads_in[pl.ds(tile, pairs, stride=FLAT), :] for tile in range(FLAT)], axis=1
    )
    slots = exact(sel_ref[...], received, ((1,), (0,)))

    padded = outgoing.shape[2]
    for piece in range(count):
        low_edge = piece * width // 128 * 128
        shift = piece * width - low_edge
        window = slots[:, low_edge : low_edge + padded]
        if shift:
            window = pltpu.roll(window, padded - shift, axis=1)
        outgoing[piece] = window

    def scatter(step, carry):
        target = lax.rem(rank + step, count)
        pltpu.make_async_remote_copy(
            src_ref=outgoing.at[target],
            dst_ref=incoming.at[rank],
            send_sem=scatter_sem.at[0],
            recv_sem=scatter_sem.at[1],
            device_id={"dp": target},
            device_id_type=MESH,
        ).start()
        return carry

    def share(step, carry):
        pltpu.make_async_remote_copy(
            src_ref=shares.at[rank],
            dst_ref=shares.at[rank],
            send_sem=share_sem.at[0],
            recv_sem=share_sem.at[1],
            device_id={"dp": lax.rem(rank + step, count)},
            device_id_type=MESH,
        ).start()
        return carry

    def announce(step, carry):
        pltpu.make_async_remote_copy(
            src_ref=verdict_in.at[rank],
            dst_ref=verdict_in.at[rank],
            send_sem=verdict_sem.at[0],
            recv_sem=verdict_sem.at[1],
            device_id={"dp": lax.rem(rank + step, count)},
            device_id_type=MESH,
        ).start()
        return carry

    def wait_all(ref, sem):
        others = ref.at[pl.ds(0, count - 1)]
        pltpu.make_async_copy(others, others, sem).wait()

    lax.fori_loop(1, count, scatter, 0)
    incoming[rank] = outgoing[rank]
    wait_all(incoming, scatter_sem.at[1])
    summed = incoming[0]
    for source in range(1, count):
        summed = summed + incoming[source]
    shares[rank] = summed

    window_lane = lax.broadcasted_iota(jnp.int32, (1, padded), 1)
    piece_rows = jnp.where(window_lane < width, summed, 0.0)
    shift = lax.rem(rank * width, 128)
    if width % 128:
        piece_rows = jnp.where(
            shift > 0, pltpu.roll(piece_rows, width % 128, axis=1), piece_rows
        )
    low_edge = pl.multiple_of(rank * width // 128 * 128, 128)
    piece_hyper = hyper[:, pl.ds(low_edge, padded)]
    coded_part = exact(piece_rows, piece_hyper, ((1,), (1,)))
    hyper_grad = exact(coded_ref[...], piece_rows, ((0,), (0,)))
    square = jnp.sum(
        jnp.sum(hyper_grad * hyper_grad, axis=0, keepdims=True), axis=1, keepdims=True
    )
    summary[0:16, :] = jnp.concatenate(
        [coded_part, jnp.broadcast_to(square, (16, 64))], axis=1
    )
    summary[16:24, :] = totals
    copies = [
        pltpu.make_async_remote_copy(
            src_ref=summary,
            dst_ref=summary_in.at[member],
            send_sem=small_send.at[step],
            recv_sem=small_recv.at[step],
            device_id={"gen": lax.rem(member + step, GEN)},
            device_id_type=MESH,
        )
        for step in range(1, GEN)
    ]
    for copy in copies:
        copy.start()
    summary_in[member] = summary[...]
    lax.fori_loop(1, count, share, 0)
    for copy in copies:
        copy.wait_recv()
    verdict_in[rank] = (summary_in[0] + summary_in[1]) + (summary_in[2] + summary_in[3])
    lax.fori_loop(1, count, announce, 0)
    for order in range(1, GEN):
        source_copy(member, peer(order)).wait_send()
        adapter_copy(member, peer(order)).wait_send()
        target_copy(member, peer(order)).wait_send()
        feature_copy(order).wait_send()
        result_copy(order).wait_send()
        stat_copy(order).wait_send()
        for layer in range(LAYERS):
            grad_copy(layer, member, peer(order)).wait_send()
    for copy in copies:
        copy.wait_send()
    wait_all(outgoing, scatter_sem.at[0])
    wait_all(shares, share_sem.at[1])
    for piece in range(0, count, 2 if width % 128 else 1):
        first = shares[piece]
        if width % 128:
            second = pltpu.roll(shares[piece + 1], width % 128, axis=1)
            middle = width // 128 * 128
            begin = piece * width
            lane128 = lax.broadcasted_iota(jnp.int32, (1, 128), 1)
            out_ref[:, begin : begin + middle] = first[:, :middle]
            out_ref[:, begin + middle : begin + middle + 128] = jnp.where(
                lane128 < width % 128, first[:, middle : middle + 128], second[:, :128]
            )
            out_ref[:, begin + middle + 128 : begin + 2 * width] = second[
                :, 128 : 2 * width - middle
            ]
        else:
            out_ref[:, piece * width : (piece + 1) * width] = first[:, :width]
    wait_all(verdict_in, verdict_sem.at[1])
    result = verdict_in[0]
    for source in range(1, count):
        result = result + verdict_in[source]
    small_ref[...] = result
    missing_ref[0] = jnp.max(result[16:17, 2:3]).astype(jnp.int32)
    wait_all(shares, share_sem.at[0])
    wait_all(verdict_in, verdict_sem.at[0])


def unpack_adapters(entries, flat, spread, down_ref, up_ref):
    lane = lax.broadcasted_iota(jnp.int32, (1, 128), 1)
    kept = lane < ADAPTER
    run = D // 32
    for owner in range(GEN):
        flat(owner)[...] = entries[owner].astype(jnp.float32)
    up_ref[...] = jnp.zeros(up_ref.shape, jnp.bfloat16)
    for layer in range(LAYERS):
        for seq in range(SEQ_DEV):
            base = (seq * LAYERS + layer) * FLAT
            for owner in range(GEN // 2):
                tiles = [flat(owner)[pl.ds(base + j, run, stride=3), :] for j in range(3)]
                for step in range(run):
                    tile, shift = divmod(ADAPTER * step, 128)
                    piece = tiles[tile]
                    if shift:
                        piece = pltpu.roll(piece, 128 - shift, axis=1)
                    if shift + ADAPTER > 128:
                        tail = pltpu.roll(tiles[tile + 1], 128 - shift, axis=1)
                        piece = jnp.where(lane < 128 - shift, piece, tail)
                    spread[pl.ds(owner * (D // 2) + step, run, stride=run), :] = jnp.where(
                        kept, piece, 0.0
                    )
            down_ref[layer, seq] = spread[pl.ds(0, D), :].astype(jnp.bfloat16)
            halves_up = []
            for owner in range(GEN // 2, GEN):
                halves_up.append(
                    jnp.concatenate(
                        [
                            flat(owner)[pl.ds(base + k, ADAPTER // 2, stride=4), :]
                            for k in range(4)
                        ],
                        axis=1,
                    )
                )
            joined = jnp.concatenate(halves_up + [jnp.zeros((8, D), jnp.float32)], axis=0)
            up_ref[layer, seq, 0:32, :] = joined.astype(jnp.bfloat16)


def pack_grads(grad_down, grad_up, pack):
    lane = lax.broadcasted_iota(jnp.int32, (1, 128), 1)
    run = D // 32
    for seq in range(SEQ_DEV):
        base = seq * FLAT
        for owner in range(GEN // 2):
            tiles = [jnp.zeros((run, 128), jnp.float32) for _ in range(3)]
            for step in range(run):
                tile, shift = divmod(ADAPTER * step, 128)
                piece = grad_down(seq)[pl.ds(owner * (D // 2) + step, run, stride=run), :]
                if shift:
                    piece = pltpu.roll(piece, shift, axis=1)
                if shift + ADAPTER > 128:
                    tiles[tile] = tiles[tile] + jnp.where(lane >= shift, piece, 0.0)
                    tiles[tile + 1] = tiles[tile + 1] + jnp.where(lane < shift, piece, 0.0)
                else:
                    tiles[tile] = tiles[tile] + piece
            for j in range(3):
                pack[owner, pl.ds(base + j, run, stride=3), :] = tiles[j]
        for half in range(GEN // 2):
            rows = slice(half * (ADAPTER // 2), (half + 1) * (ADAPTER // 2))
            for k in range(4):
                pack[GEN // 2 + half, pl.ds(base + k, ADAPTER // 2, stride=4), :] = grad_up(seq)[
                    rows, 128 * k : 128 * (k + 1)
                ]


def step(done, known, task_ids, task_len, tgt_count, src_ids, tgt_ids, embeds, one, two, gains,
         hyper, attn_w, ffn_in, ffn_out, table):
    vmem = pl.BlockSpec(memory_space=pltpu.VMEM)
    smem = pl.BlockSpec(memory_space=pltpu.SMEM)
    whole = pl.BlockSpec(memory_space=pl.ANY)
    low, full = jnp.bfloat16, jnp.float32
    sources, targets = SEQ_DEV * SRC, SEQ_DEV * TGT
    pairs = TASKS * LAYERS
    count = lax.axis_size("dp")
    width = FLAT * 128 // count
    padded = (width + 127) // 128 * 128
    dma = pltpu.SemaphoreType.DMA
    return pl.pallas_call(
        step_kernel,
        out_shape=(
            jax.ShapeDtypeStruct((pairs, FLAT * 128), full),
            jax.ShapeDtypeStruct((24, 128), full),
            jax.ShapeDtypeStruct((pairs, two.shape[0]), full),
            jax.ShapeDtypeStruct((1,), jnp.int32),
        ),
        in_specs=[smem] * 3 + [vmem] * 7 + [whole] * 6,
        out_specs=(vmem, vmem, vmem, smem),
        scratch_shapes=[
            pltpu.VMEM(attn_w.shape, low),
            pltpu.VMEM(ffn_in.shape, low),
            pltpu.VMEM(ffn_out.shape, low),
            pltpu.VMEM(table.shape, low),
            pltpu.VMEM((WIDE, D), full),
            pltpu.VMEM((sources, D), low),
            pltpu.VMEM((sources, 3 * D), low),
            pltpu.VMEM((sources, D), low),
            pltpu.VMEM((sources, FF), low),
            pltpu.VMEM((sources, D), low),
            pltpu.VMEM((targets, D), low),
            pltpu.VMEM((targets, D), low),
            pltpu.VMEM((GEN, targets, D), low),
            pltpu.VMEM((GEN, 8, targets), full),
            pltpu.VMEM((GEN, 8, targets), full),
            pltpu.VMEM((targets, D), low),
            pltpu.VMEM((GEN, SRC_CAP + TGT_CAP, D), low),
            pltpu.VMEM((sources + 2 * targets, D), low),
            pltpu.VMEM((GEN, SRC_CAP, D), low),
            pltpu.VMEM((GEN, TGT_CAP, D), low),
            pltpu.VMEM((pairs * FLAT, 128), full),
            pltpu.VMEM((SEQ_DEV * D, LOW), full),
            pltpu.VMEM((GEN, SEQ_DEV * LAYERS * FLAT, 128), low),
            pltpu.VMEM((GEN, SEQ_DEV * LAYERS * FLAT, 128), low),
            pltpu.VMEM((pairs, pairs), full),
            pltpu.VMEM((LAYERS, SEQ_DEV, D, LOW), low),
            pltpu.VMEM((LAYERS, SEQ_DEV, LOW, D), low),
            pltpu.VMEM((LAYERS, GEN, SEQ_DEV * FLAT, 128), full),
            pltpu.VMEM((LAYERS * GEN * SEQ_DEV * FLAT, 128), full),
            pltpu.VMEM(hyper.shape, full),
            pltpu.VMEM((count, pairs, padded), full),
            pltpu.VMEM((count, pairs, padded), full),
            pltpu.VMEM((count, pairs, padded), full),
            pltpu.VMEM((24, 128), full),
            pltpu.VMEM((GEN, 24, 128), full),
            pltpu.VMEM((count, 24, 128), full),
            dma((14,)),
            dma((3, GEN)),
            dma((GEN,)),
            dma((GEN,)),
            dma((GEN,)),
            dma((LAYERS, GEN)),
            dma((LAYERS, GEN)),
            dma((2,)),
            dma((2,)),
            dma((GEN,)),
            dma((GEN,)),
            dma((2,)),
            dma((GEN,)),
            dma((GEN,)),
            dma((GEN,)),
            dma((GEN,)),
            dma((GEN,)),
            dma((GEN,)),
        ],
        compiler_params=pltpu.CompilerParams(
            collective_id=1, has_side_effects=True, vmem_limit_bytes=VMEM_LIMIT
        ),
        name="rows_forward_vocab_backward_sum",
    )(done, task_ids, tgt_count, task_len.reshape(1, -1), src_ids, tgt_ids, embeds, one, two, gains,
      known, hyper, attn_w, ffn_in, ffn_out, table)


def update_kernel(
    slots_ref,
    small_ref,
    coded_ref,
    embeds,
    embeds_m,
    embeds_v,
    one,
    one_m,
    one_v,
    two,
    two_m,
    two_v,
    hyper,
    hyper_m,
    hyper_v,
    loss_ref,
    tokens_ref,
    norm_ref,
    new_embeds,
    new_embeds_m,
    new_embeds_v,
    new_one,
    new_one_m,
    new_one_v,
    new_two,
    new_two_m,
    new_two_v,
    new_hyper,
    new_hyper_m,
    new_hyper_v,
    held,
    fresh,
    load_sem,
    store_sem,
):
    block = held.shape[3]

    def span(step):
        return pl.ds(step * block, block)

    loads = [
        [
            pltpu.make_async_copy(
                array.at[:, span(step)], held.at[step, index], load_sem.at[step, index]
            )
            for index, array in enumerate((hyper, hyper_m, hyper_v))
        ]
        for step in range(UPDATE_STEPS)
    ]
    for group in loads:
        for load in group:
            load.start()
    coded_grad = small_ref[0:16, 0:64]
    tokens = small_ref[16:17, 1:2]
    loss_ref[...] = small_ref[16:17, 0:1]
    tokens_ref[...] = tokens
    pairs = pair_rows(embeds[...])
    before = exact(pairs, one[...], ((1,), (0,)))
    tanh = gelu_tanh(before)
    active = (0.5 * before) * (1.0 + tanh)
    grad_two = exact(coded_grad, active, ((0,), (0,)))
    grad_before = exact(coded_grad, two[...], ((1,), (0,))) * gelu_slope(before, tanh)
    grad_one = exact(pairs, grad_before, ((0,), (0,)))
    grad_pairs = exact(grad_before, one[...], ((1,), (1,)))
    row = lax.broadcasted_iota(jnp.int32, (16, TASKS * LAYERS), 0)
    column = lax.broadcasted_iota(jnp.int32, (16, TASKS * LAYERS), 1)
    chosen = (row == column // LAYERS) & (row < TASKS) | (row == TASKS + column % LAYERS)
    grad_embeds = exact(chosen.astype(jnp.float32), grad_pairs, ((1,), (0,)))
    grad_embeds = grad_embeds[: TASKS + LAYERS]
    scale = 1.0 / tokens
    grads = [grad * scale for grad in (grad_embeds, grad_one, grad_two)]
    square = small_ref[0:1, 64:65] * scale * scale
    for grad in grads:
        square = square + jnp.sum(
            jnp.sum(grad * grad, axis=1, keepdims=True), axis=0, keepdims=True
        )
    norm = jnp.sqrt(square)
    norm_ref[...] = norm
    factor = jnp.minimum(1.0, clip_limit / (norm + 1e-06))
    for index, (weight, first, second, outs) in enumerate(
        (
            (embeds, embeds_m, embeds_v, (new_embeds, new_embeds_m, new_embeds_v)),
            (one, one_m, one_v, (new_one, new_one_m, new_one_v)),
            (two, two_m, two_v, (new_two, new_two_m, new_two_v)),
        )
    ):
        for out, value in zip(
            outs,
            adamw(weight[...], first[...], second[...], grads[index] * factor, rates[index]),
        ):
            out[...] = value

    stores = []
    clip = scale * factor
    spread = stacked_left(coded_ref[...])
    for step in range(UPDATE_STEPS):
        for load in loads[step]:
            load.wait()
        columns = slice(step * block, (step + 1) * block)
        grad = mm_first(spread, stacked_right(slots_ref[:, columns])) * clip
        values = adamw(held[step, 0], held[step, 1], held[step, 2], grad, rates[3])
        for index, (array, value) in enumerate(zip((new_hyper, new_hyper_m, new_hyper_v), values)):
            fresh[step, index] = value
            stores.append(
                pltpu.make_async_copy(
                    fresh.at[step, index], array.at[:, span(step)], store_sem.at[step, index]
                )
            )
            stores[-1].start()
    for store in stores:
        store.wait()


def split(value):
    high = value.astype(jnp.bfloat16)
    rest = value - high.astype(jnp.float32)
    middle = rest.astype(jnp.bfloat16)
    return high, middle, (rest - middle.astype(jnp.float32)).astype(jnp.bfloat16)


def stacked_left(value):
    high, middle, low = split(value)
    return jnp.concatenate([high, high, middle, high, middle, low], axis=0)


def stacked_right(value):
    high, middle, low = split(value)
    return jnp.concatenate([high, middle, high, low, middle, high], axis=0)


def update(slots, small, coded, *weights):
    full = jnp.float32
    vmem = pl.BlockSpec(memory_space=pltpu.VMEM)
    whole = pl.BlockSpec(memory_space=pl.ANY)
    block = slots.shape[1] // UPDATE_STEPS
    one_value = jax.ShapeDtypeStruct((1, 1), full)
    buffer = pltpu.VMEM((UPDATE_STEPS, 3, weights[9].shape[0], block), full)
    return pl.pallas_call(
        update_kernel,
        out_shape=[one_value] * 3 + [jax.ShapeDtypeStruct(w.shape, full) for w in weights],
        in_specs=[vmem] * 12 + [whole] * 3,
        out_specs=[vmem] * 12 + [whole] * 3,
        scratch_shapes=[
            buffer,
            buffer,
            pltpu.SemaphoreType.DMA((UPDATE_STEPS, 3)),
            pltpu.SemaphoreType.DMA((UPDATE_STEPS, 3)),
        ],
        compiler_params=pltpu.CompilerParams(vmem_limit_bytes=VMEM_LIMIT),
        name="update",
    )(slots, small, coded, *weights)


def ring_rows(src_ids, tgt_ids, table):
    member = lax.axis_index("gen")
    inputs = jnp.concatenate([jnp.zeros_like(tgt_ids[:, :1]), tgt_ids[:, :-1]], axis=1)
    tokens = jnp.concatenate(
        [ids.reshape(GEN, -1) for ids in (src_ids, inputs, tgt_ids)], axis=1
    )
    ring = [(source, (source + 1) % GEN) for source in range(GEN)]

    def held(target):
        token = lax.dynamic_index_in_dim(tokens, target, 0, False) - member * table.shape[0]
        inside = (token >= 0) & (token < table.shape[0])
        rows = jnp.take(table, jnp.clip(token, 0, table.shape[0] - 1), axis=0)
        return jnp.where(inside[:, None], rows, jnp.zeros_like(rows))

    def pass_on(hop, rows):
        rows = lax.ppermute(rows, "gen", ring)
        return rows + held(lax.rem(member - 1 - hop + 2 * GEN, GEN))

    rows = lax.fori_loop(1, GEN, pass_on, held(lax.rem(member - 1 + GEN, GEN)))
    return jnp.pad(rows, ((0, table.shape[0] - rows.shape[0]), (0, 0)))


def per_device(
    src_ids,
    tgt_ids,
    task_ids,
    task_len,
    tgt_count,
    table,
    attn_w,
    ffn_in,
    ffn_out,
    gains,
    embeds,
    embeds_m,
    embeds_v,
    proj_one,
    proj_one_m,
    proj_one_v,
    proj_two,
    proj_two_m,
    proj_two_v,
    hyper,
    hyper_m,
    hyper_v,
):
    weights = (
        embeds, embeds_m, embeds_v,
        proj_one, proj_one_m, proj_one_v,
        proj_two.T, proj_two_m.T, proj_two_v.T,
        hyper, hyper_m, hyper_v,
    )
    inputs = (
        task_ids, task_len, tgt_count, src_ids, tgt_ids, embeds, proj_one, proj_two.T, gains,
        hyper, attn_w, ffn_in, ffn_out, table,
    )
    slots, small, coded, crowded = step(jnp.zeros((1,), jnp.int32), table, *inputs)

    def again(state):
        rows = ring_rows(src_ids, tgt_ids, table)
        slots, small, coded, _ = step(jnp.ones((1,), jnp.int32), rows, *inputs)
        return jnp.zeros((1,), jnp.int32), slots, small, coded

    _, slots, small, coded = lax.while_loop(
        lambda state: state[0][0] > 0, again, (crowded, slots, small, coded)
    )
    loss_sum, token_count, grad_norm, *updated = update(slots, small, coded, *weights)
    updated[6:9] = [value.T for value in updated[6:9]]
    return (loss_sum.reshape(()), token_count.reshape(()), grad_norm.reshape(()), *updated)


def solution(mesh):
    return jax.shard_map(
        per_device,
        mesh=mesh,
        in_specs=(
            P("dp", None),
            P("dp", None),
            P("dp"),
            P(),
            P("dp"),
            P("gen", None),
            P(),
            P(),
            P(),
            P(),
            P(),
            P(),
            P(),
            P(),
            P(),
            P(),
            P(),
            P(),
            P(),
            P(None, "gen"),
            P(None, "gen"),
            P(None, "gen"),
        ),
        out_specs=(
            P(),
            P(),
            P(),
            P(),
            P(),
            P(),
            P(),
            P(),
            P(),
            P(),
            P(),
            P(),
            P(None, "gen"),
            P(None, "gen"),
            P(None, "gen"),
        ),
        check_vma=False,
    )
```

```python
import math
from functools import partial

import jax
import jax.numpy as jnp
from jax import lax
from jax.experimental import pallas as pl
from jax.experimental.pallas import tpu as pltpu
from jax.sharding import PartitionSpec as P

D = 512
HEADS = 8
ADAPTER = 24
TASKS = 8
LAYERS = 2
SRC = 256
TGT = 128
FF = 2048
SEQ_DEV = 2
GEN = 4
LOW = 128
SRC_CAP = 176
TGT_CAP = 128
SRC_SPAN = 256
FLAT = 48
STEP = 5


epsilon = 1e-06
clip_limit = 0.001
beta_one = 0.9
beta_two = 0.999
adam_floor = 1e-08
weight_decay = 0.01
rates = (0.5, 0.1, 0.1, 0.005)
blocked = -1000000000.0
highest = lax.Precision.HIGHEST
LOGIT_SCALE = D ** (-0.5)
EXP_SCALE = LOGIT_SCALE / math.log(2.0)
UPSCALE = math.sqrt(D / ADAPTER)
GELU_A = math.sqrt(2.0 / math.pi)
GELU_B = 0.044715
VOCAB_TILE = 2048
UPDATE_STEPS = 4
VMEM_LIMIT = 62 * 1024 * 1024
MESH = pl.DeviceIdType.MESH


def adamw(weight, first, second, grad, rate):
    first = beta_one * first + (1.0 - beta_one) * grad
    second = beta_two * second + (1.0 - beta_two) * grad * grad
    corrected = first * (1.0 / (1.0 - beta_one**STEP))
    spread = jnp.sqrt(second * (1.0 / (1.0 - beta_two**STEP))) + adam_floor
    return (weight - rate * (corrected / spread + weight_decay * weight), first, second)


def mm(left, right):
    return lax.dot_general(
        left, right, (((1,), (0,)), ((), ())), preferred_element_type=jnp.float32
    )


def mm_last(left, right):
    return lax.dot_general(
        left, right, (((1,), (1,)), ((), ())), preferred_element_type=jnp.float32
    )


def mm_first(left, right):
    return lax.dot_general(
        left, right, (((0,), (0,)), ((), ())), preferred_element_type=jnp.float32
    )


def exact(left, right, dims):
    return lax.dot_general(
        left, right, (dims, ((), ())), precision=highest, preferred_element_type=jnp.float32
    )


def norm_scale(value):
    return lax.rsqrt(jnp.mean(value * value, axis=-1, keepdims=True) + epsilon)


def normed(value, gain):
    return (value * norm_scale(value) * gain).astype(jnp.bfloat16)


def norm_back(value, gain, grad):
    scale = norm_scale(value)
    weighted = grad * gain
    return scale * weighted - value * (
        scale * scale * scale * jnp.mean(weighted * value, axis=-1, keepdims=True)
    )


def gelu_tanh(value):
    return jnp.tanh(value * (GELU_A + (GELU_A * GELU_B) * (value * value)))


def gelu(value):
    return (0.5 * value) * (1.0 + gelu_tanh(value))


def gelu_slope(value, tanh):
    return 0.5 * (1.0 + tanh) + (0.5 * value) * (1.0 - tanh * tanh) * (
        GELU_A + (3.0 * GELU_A * GELU_B) * (value * value)
    )


def halves():
    lane = lax.broadcasted_iota(jnp.int32, (1, 128), 1)
    return [(lane // 64 == half) for half in range(2)]


def attend(q_ref, kv_ref, k_col, v_col, q_len, k_len, allow, out_ref, probs_ref=None):
    sides = halves()
    masks = [side.astype(jnp.float32).astype(jnp.bfloat16) for side in sides]

    def pair_step(pair, carry):
        lanes = pair * 128
        for seq in range(SEQ_DEV):
            q_rows = pl.ds(seq * q_len, q_len)
            k_rows = pl.ds(seq * k_len, k_len)
            query = q_ref[q_rows, pl.ds(lanes, 128)]
            keys = kv_ref[k_rows, pl.ds(k_col + lanes, 128)]
            values = kv_ref[k_rows, pl.ds(v_col + lanes, 128)]
            outs = []
            for half in range(2):
                scores = mm_last(query * masks[half], keys) * 0.125
                scores = jnp.where(allow(seq), scores, blocked)
                peak = jnp.max(scores, axis=-1, keepdims=True)
                weights = jnp.exp(scores - peak)
                probs = weights * (1.0 / jnp.sum(weights, axis=-1, keepdims=True))
                if probs_ref is not None:
                    begin = (pair * SEQ_DEV + seq) * q_len
                    probs_ref[pl.ds(begin, q_len), half * k_len : (half + 1) * k_len] = probs
                outs.append(mm(probs.astype(jnp.bfloat16), values))
            out_ref[q_rows, pl.ds(lanes, 128)] = jnp.where(sides[0], outs[0], outs[1]).astype(
                jnp.bfloat16
            )
        return carry

    for pair in range(HEADS // 2):
        pair_step(pair, 0)


def attend_back(grad_ref, q_ref, kv_ref, probs_ref, q_len, k_len, joined_ref):
    sides = halves()
    masks = [side.astype(jnp.float32).astype(jnp.bfloat16) for side in sides]

    def pair_step(pair, carry):
        lanes = pair * 128
        for seq in range(SEQ_DEV):
            q_rows = pl.ds(seq * q_len, q_len)
            k_rows = pl.ds(seq * k_len, k_len)
            grad = grad_ref[q_rows, pl.ds(lanes, 128)]
            query = q_ref[q_rows, pl.ds(lanes, 128)]
            values = kv_ref[k_rows, pl.ds(D + lanes, 128)]
            key_grads, value_grads = [], []
            for half in range(2):
                begin = (pair * SEQ_DEV + seq) * q_len
                probs = probs_ref[pl.ds(begin, q_len), half * k_len : (half + 1) * k_len]
                grad_probs = mm_last(grad * masks[half], values)
                value_grads.append(mm_first(probs.astype(jnp.bfloat16), grad))
                inner = jnp.sum(grad_probs * probs, axis=-1, keepdims=True)
                grad_scores = (probs * (grad_probs - inner)).astype(jnp.bfloat16)
                key_grads.append(mm_first(grad_scores, query))
            joined_ref[k_rows, pl.ds(lanes, 128)] = (
                jnp.where(sides[0], key_grads[0], key_grads[1]) * 0.125
            ).astype(jnp.bfloat16)
            joined_ref[k_rows, pl.ds(D + lanes, 128)] = jnp.where(
                sides[0], value_grads[0], value_grads[1]
            ).astype(jnp.bfloat16)
        return carry

    for pair in range(HEADS // 2):
        pair_step(pair, 0)


def feed(state_ref, gain, inner_ref, outer_ref, act_ref, slope_ref, down_ref, up_ref, length,
         plain_ref, low_ref, after_ref):
    rows = SEQ_DEV * length
    act_rows = pl.ds(0, rows)
    source = normed(state_ref[...], gain)
    for block in range(FF // D):
        columns = slice(block * D, (block + 1) * D)
        hidden = mm(source, inner_ref[:, columns])
        tanh = gelu_tanh(hidden)
        act_ref[act_rows, columns] = ((0.5 * hidden) * (1.0 + tanh)).astype(jnp.bfloat16)
        if slope_ref is not None:
            slope_ref[pl.ds(block * rows, rows), :] = gelu_slope(hidden, tanh)
    branch = mm(act_ref[act_rows, :], outer_ref[...])
    plain_ref[...] = branch.astype(jnp.bfloat16)
    for seq in range(SEQ_DEV):
        span = slice(seq * length, (seq + 1) * length)
        lowered = mm(plain_ref[span, :], down_ref[seq])
        low_ref[span, :] = lowered
        adapted = mm(gelu(lowered).astype(jnp.bfloat16), up_ref[seq]) * UPSCALE
        after_ref[span, :] = state_ref[span, :] + branch[span, :] + adapted


def adapter_back(grad_ref, low_ref, plain_ref, down_ref, up_ref, length, grad_down_ref,
                 grad_up_ref, branch_ref=None):
    for seq in range(SEQ_DEV):
        span = slice(seq * length, (seq + 1) * length)
        grad = grad_ref[span, :]
        grad_low = grad.astype(jnp.bfloat16)
        lowered = low_ref[span, :]
        tanh = gelu_tanh(lowered)
        bottleneck = ((0.5 * lowered) * (1.0 + tanh)).astype(jnp.bfloat16)
        grad_bottle = mm_last(grad_low, up_ref[seq]) * UPSCALE
        grad_up_ref(seq)[...] = mm_first(bottleneck, grad_low)[:ADAPTER] * UPSCALE
        grad_lowered = (grad_bottle * gelu_slope(lowered, tanh)).astype(jnp.bfloat16)
        grad_down_ref(seq)[...] = mm_first(plain_ref[span, :], grad_lowered)
        if branch_ref is not None:
            branch_ref[span, :] = (grad + mm_last(grad_lowered, down_ref[seq])).astype(
                jnp.bfloat16
            )


def pair_rows(embeds):
    return jnp.concatenate(
        [
            embeds[task : task + 1, :] + embeds[TASKS + layer : TASKS + layer + 1, :]
            for task in range(TASKS)
            for layer in range(LAYERS)
        ],
        axis=0,
    )


def place_rows(src_ref, tgt_ref, member, peer, part, done, index_vmem):
    offset = member * part
    crowded = jnp.zeros((1, 1), jnp.float32)
    slots = []
    for ids_ref, length, rows, begin in (
        (src_ref, SRC, SRC_CAP, 0),
        (tgt_ref, TGT, TGT_CAP, SRC_SPAN),
    ):
        count = SEQ_DEV * length
        ids = jnp.concatenate(
            [
                jnp.concatenate(
                    [ids_ref[pl.ds(SEQ_DEV * peer(k) + s, 1), :] for s in range(SEQ_DEV)], axis=1
                )
                for k in range(GEN)
            ],
            axis=0,
        )
        if length == TGT:
            lane = lax.broadcasted_iota(jnp.int32, (GEN, 128), 1)
            ids = jnp.concatenate([ids, jnp.where(lane == 0, 0, -1)], axis=1)
            count = count + 128
        own = ids[0:1]
        local = ids - offset
        inside = ((local >= 0) & (local < part) & (ids >= 0)).astype(jnp.int32)
        held = [((own >= part * o) & (own < part * (o + 1))).astype(jnp.int32) for o in range(GEN)]
        ranks = jnp.concatenate([inside] + held, axis=0)
        lane = lax.broadcasted_iota(jnp.int32, ranks.shape, 1)
        reach = 1
        while reach < count:
            ranks = ranks + jnp.where(lane >= reach, pltpu.roll(ranks, reach, axis=1), 0)
            reach = 2 * reach
        ranks = ranks - 1 - done * count
        for o in range(GEN):
            amount = ((ids >= part * o) & (ids < part * (o + 1))).astype(jnp.float32)
            most = jnp.max(jnp.sum(amount, axis=1, keepdims=True), axis=0, keepdims=True)
            crowded = jnp.maximum(crowded, (most > float(rows)).astype(jnp.float32))
        spot = lax.broadcasted_iota(jnp.int32, (rows, count), 0)
        span = (rows + 127) // 128 * 128
        same = lax.broadcasted_iota(jnp.int32, (rows, span), 0) == lax.broadcasted_iota(
            jnp.int32, (rows, span), 1
        )
        for k in range(GEN):
            position = jnp.where(inside[k : k + 1] > 0, ranks[k : k + 1], -1)
            numbers = jnp.sum(
                jnp.where(spot == position, local[k : k + 1], 0), axis=1, keepdims=True
            )
            index_vmem[k : k + 1, begin : begin + span] = jnp.sum(
                jnp.where(same, numbers, 0), axis=0, keepdims=True
            )
        slot = jnp.full((1, count), -1.0, jnp.float32)
        for o in range(GEN):
            rank = ranks[GEN + o : GEN + o + 1]
            now = (held[o] > 0) & (rank >= 0) & (rank < rows)
            slot = jnp.where(now, (rank + o * rows).astype(jnp.float32), slot)
        slots.append(slot)
    targets = SEQ_DEV * TGT
    lane = lax.broadcasted_iota(jnp.int32, (1, targets), 1)
    shifted = jnp.where(
        lax.rem(lane, TGT) == 0,
        slots[1][:, targets : targets + 1],
        pltpu.roll(slots[1][:, :targets], 1, axis=1),
    )
    return slots[0], shifted, slots[1][:, :targets], crowded


def describe(task_ref, lens_ref, count_ref, member):
    own_first = member * SEQ_DEV
    position = lax.broadcasted_iota(jnp.int32, (1, SRC), 1)
    place = lax.broadcasted_iota(jnp.int32, (1, TGT), 1)
    task = lax.broadcasted_iota(jnp.int32, (1, TASKS), 1)
    allow, valid = [], []
    tokens = jnp.zeros((1, 1), jnp.float32)
    for s in range(SEQ_DEV):
        length = jnp.sum(
            jnp.where(task == task_ref[own_first + s], lens_ref[...], 0).astype(jnp.float32),
            axis=1,
            keepdims=True,
        )
        allow.append((position.astype(jnp.float32) < length).astype(jnp.float32))
        valid.append((place < count_ref[own_first + s]).astype(jnp.float32))
        tokens = tokens + jnp.sum(valid[-1], axis=1, keepdims=True)
    return jnp.concatenate(allow, axis=1), jnp.concatenate(valid, axis=1), tokens


def generate(task_ref, embeds_ref, one_ref, two_ref, hyper_ref, coded_ref, chosen,
             adapters, sel):
    coded = exact(
        gelu(exact(pair_rows(embeds_ref[...]), one_ref[...], ((1,), (0,)))),
        two_ref[...],
        ((1,), (1,)),
    )
    coded_ref[...] = coded
    flat = mm(stacked_left(coded, 1), stacked_right(hyper_ref[...])).astype(jnp.bfloat16)
    pairs = TASKS * LAYERS
    sequences = GEN * SEQ_DEV
    row_of = lax.broadcasted_iota(jnp.int32, (pairs, pairs), 0)
    column_of = lax.broadcasted_iota(jnp.int32, (pairs, pairs), 1)
    picks = jnp.zeros((pairs, pairs), jnp.float32)
    selector = jnp.zeros((pairs, pairs), jnp.float32)
    for seq in range(sequences):
        for layer in range(LAYERS):
            pair = task_ref[seq] * LAYERS + layer
            picks = jnp.where(
                (row_of == seq * LAYERS + layer) & (column_of == pair), 1.0, picks
            )
            selector = jnp.where(
                (row_of == pair) & (column_of == layer * sequences + seq), 1.0, selector
            )
    sel[...] = selector
    taken = mm(picks.astype(jnp.bfloat16), flat)
    for tile in range(FLAT):
        chosen[pl.ds(tile, pairs, stride=FLAT), :] = taken[:, 128 * tile : 128 * (tile + 1)]
    share = SEQ_DEV * LAYERS * FLAT
    for target in range(GEN):
        adapters[target] = chosen[pl.ds(target * share, share), :].astype(jnp.bfloat16)


def step_kernel(
    done_ref,
    task_ref,
    count_ref,
    lens_ref,
    src_ref,
    tgt_ref,
    embeds_ref,
    one_ref,
    two_ref,
    gains_ref,
    known_hbm,
    hyper_hbm,
    attn_hbm,
    inner_hbm,
    outer_hbm,
    table_hbm,
    out_ref,
    small_ref,
    coded_ref,
    missing_ref,
    attn,
    inner,
    outer,
    table,
    wide,
    plain_e,
    qkv,
    mixed,
    act,
    feats,
    stats,
    stats_in,
    rows_out,
    picked_rows,
    index_vmem,
    index,
    known,
    src_in,
    tgt_in,
    generated,
    spread,
    adapters_ref,
    adapters_in,
    sel_ref,
    down_ref,
    up_ref,
    pack,
    grads_in,
    hyper,
    outgoing,
    incoming,
    shares,
    summary,
    summary_in,
    verdict_in,
    load_sem,
    row_send,
    src_recv,
    tgt_recv,
    adapter_recv,
    grad_send,
    grad_recv,
    scatter_sem,
    share_sem,
    small_send,
    small_recv,
    verdict_sem,
    index_sem,
    feat_send,
    feat_recv,
    result_send,
    result_recv,
    stat_send,
    stat_recv,
):
    member = lax.axis_index("gen")
    barrier = pltpu.get_barrier_semaphore()
    sources = SEQ_DEV * SRC
    targets = SEQ_DEV * TGT
    own = pl.ds(0, targets)
    part = table.shape[0]

    spans = []

    def view(rows, lanes=None):
        begin = spans[-1] if spans else 0
        if lanes is None:
            spans.append(begin + rows)
            return wide.at[pl.ds(begin, rows)]
        return wide.at[pl.ds(begin, rows), lanes]

    state, after_e, grad = view(sources), view(sources), view(sources)
    y1, y2, y3, total, wanted = (view(targets) for _ in range(5))
    slope = view(targets * (FF // D))
    probs = view(SEQ_DEV * HEADS // 2 * TGT)
    low_e = view(sources, pl.ds(0, LOW))
    low_d = view(targets, pl.ds(LOW, LOW))
    view(sources)
    first_up = spans[-1]
    view(LAYERS * SEQ_DEV * ADAPTER)

    def grad_down_ref(seq):
        return spread.at[pl.ds(seq * D, D)]

    def grad_up_ref(layer, seq):
        begin = first_up + (layer * SEQ_DEV + seq) * ADAPTER
        return wide.at[pl.ds(begin, ADAPTER)]

    def flat_in(owner):
        return generated.at[pl.ds(owner * SEQ_DEV * LAYERS * FLAT, SEQ_DEV * LAYERS * FLAT)]

    memory = inner.at[0, :, pl.ds(0, D)]
    q_cross = attn.at[1, pl.ds(0, targets), pl.ds(0, D)]
    plain_d = attn.at[1, pl.ds(targets, targets), pl.ds(0, D)]
    grad_low = attn.at[1, pl.ds(0, targets), pl.ds(D, D)]
    kv_cross = attn.at[0, :, pl.ds(0, 2 * D)]
    joined = attn.at[0, :, pl.ds(2 * D, 2 * D)]

    def results(order):
        return outer.at[0, pl.ds(pl.multiple_of(order * targets, targets), targets)]

    def arrived(order):
        begin = pl.multiple_of((GEN + order) * targets, targets)
        return outer.at[0, pl.ds(begin, targets)]

    def peer(order):
        chip = lax.rem(member // 2 + lax.rem((order + 1) // 2, 2), 2)
        return chip * 2 + lax.rem(lax.rem(member, 2) + order // 2, 2)

    rank = lax.axis_index("dp")
    count = outgoing.shape[0]
    width = TASKS * LAYERS * FLAT * 128 // (TASKS * LAYERS * count)
    loads = []

    def load(source, target):
        loads.append(pltpu.make_async_copy(source, target, load_sem.at[len(loads)]))
        loads[-1].start()
        return loads[-1]

    cuts = [0, 2048, 4096, 6144, part]
    table_loads = [
        load(
            table_hbm.at[pl.ds(cuts[i], cuts[i + 1] - cuts[i])],
            table.at[pl.ds(cuts[i], cuts[i + 1] - cuts[i])],
        )
        for i in range(4)
    ]
    hyper_load = load(hyper_hbm, hyper)
    known_load = load(known_hbm.at[pl.ds(0, known.shape[0])], known)
    for order in range(1, GEN):
        pl.semaphore_signal(
            barrier, inc=1, device_id={"gen": peer(order)}, device_id_type=MESH
        )

    def greet(step, carry):
        pl.semaphore_signal(
            barrier, inc=1, device_id={"dp": lax.rem(rank + step, count)}, device_id_type=MESH
        )
        return carry

    lax.fori_loop(1, count, greet, 0)
    weight_loads = [
        load(source, target)
        for source, target in (
            (attn_hbm.at[0], attn.at[0]),
            (inner_hbm.at[0], inner.at[0]),
            (outer_hbm.at[0], outer.at[0]),
            (attn_hbm.at[1], attn.at[1]),
            (attn_hbm.at[2], attn.at[2]),
            (inner_hbm.at[1], inner.at[1]),
            (outer_hbm.at[1], outer.at[1]),
        )
    ]

    source_slot, input_slot, target_slot, crowded = place_rows(
        src_ref, tgt_ref, member, peer, part, done_ref[0], index_vmem
    )
    index_copy = pltpu.make_async_copy(index_vmem, index, index_sem)
    index_copy.start()
    chunk = 32
    for i in range(len(cuts) - 1):
        table_loads[i].wait()

        def widen(step, carry):
            begin = pl.multiple_of(cuts[i] + step * chunk, chunk)
            wide[pl.ds(begin, chunk), :] = table[pl.ds(begin, chunk), :].astype(jnp.float32)
            return carry

        lax.fori_loop(0, (cuts[i + 1] - cuts[i]) // chunk, widen, 0)
    index_copy.wait()

    def gather(order, begin, first, size):
        def fetch(step, carry):
            place = pl.multiple_of(step * 16, 16)
            for k in range(16):
                picked_rows[pl.ds(place + k, 1), :] = wide[
                    pl.ds(index[order, first + place + k], 1), :
                ]
            return carry

        lax.fori_loop(0, size // 16, fetch, 0)
        rows_out[peer(order), pl.ds(begin, size), :] = picked_rows[pl.ds(0, size), :].astype(
            jnp.bfloat16
        )

    def source_copy(owner, target):
        return pltpu.make_async_remote_copy(
            src_ref=rows_out.at[target, pl.ds(0, SRC_CAP)],
            dst_ref=src_in.at[owner],
            send_sem=row_send.at[0, target],
            recv_sem=src_recv.at[owner],
            device_id={"gen": target},
            device_id_type=MESH,
        )

    def target_copy(owner, target):
        return pltpu.make_async_remote_copy(
            src_ref=rows_out.at[target, pl.ds(SRC_CAP, TGT_CAP)],
            dst_ref=tgt_in.at[owner],
            send_sem=row_send.at[1, target],
            recv_sem=tgt_recv.at[owner],
            device_id={"gen": target},
            device_id_type=MESH,
        )

    def adapter_copy(owner, target):
        return pltpu.make_async_remote_copy(
            src_ref=adapters_ref.at[target],
            dst_ref=adapters_in.at[owner],
            send_sem=row_send.at[2, target],
            recv_sem=adapter_recv.at[owner],
            device_id={"gen": target},
            device_id_type=MESH,
        )

    pl.semaphore_wait(barrier, GEN + count - 2)
    for order in (1, 2):
        gather(order, 0, 0, SRC_CAP)
        source_copy(member, peer(order)).start()
    hyper_load.wait()
    generate(task_ref, embeds_ref, one_ref, two_ref, hyper, coded_ref, generated, adapters_ref,
             sel_ref)
    for order in range(1, GEN):
        adapter_copy(member, peer(order)).start()
    for order in (1, 2):
        gather(order, SRC_CAP, SRC_SPAN, TGT_CAP)
        target_copy(member, peer(order)).start()
    gather(3, 0, 0, SRC_CAP)
    source_copy(member, peer(3)).start()
    gather(3, SRC_CAP, SRC_SPAN, TGT_CAP)
    target_copy(member, peer(3)).start()
    gather(0, 0, 0, SRC_CAP)
    gather(0, SRC_CAP, SRC_SPAN, TGT_CAP)
    src_in[member] = rows_out[member, 0:SRC_CAP, :]
    tgt_in[member] = rows_out[member, SRC_CAP : SRC_CAP + TGT_CAP, :]
    adapters_in[member] = adapters_ref[member]
    allow, valid, tokens = describe(task_ref, lens_ref, count_ref, member)

    def spread_rows(slot, incoming_rows, owner):
        height = incoming_rows.shape[1]
        spot = lax.broadcasted_iota(jnp.int32, (height, slot.shape[1]), 0)
        spot = (spot + owner * height).astype(jnp.float32)
        chosen = (spot == slot).astype(jnp.float32)
        return mm_first(chosen.astype(jnp.bfloat16), incoming_rows[owner])

    known_load.wait()

    def known_rows(begin, size):
        rows = known[begin : begin + size, :].astype(jnp.float32)
        return jnp.where(done_ref[0] > 0, rows, 0.0)

    after_e[...] = known_rows(0, sources) + spread_rows(
        source_slot, src_in, member
    )
    for order in (3, 1, 2):
        source_copy(peer(order), peer(order)).wait_recv()
        after_e[...] = after_e[...] + spread_rows(source_slot, src_in, peer(order))
    embedded = after_e[...]

    def allowed(seq):
        return allow[:, seq * SRC : (seq + 1) * SRC] > 0.0

    entry = normed(embedded, gains_ref[0:1])
    weight_loads[0].wait()
    for block in range(3):
        columns = slice(block * D, (block + 1) * D)
        qkv[:, columns] = mm(entry, attn[0, :, columns]).astype(jnp.bfloat16)
    attend(qkv, qkv, D, 2 * D, SRC, SRC, allowed, mixed)
    state[...] = embedded + mm(mixed[...], attn[0, :, 3 * D :])
    weight_loads[1].wait()
    weight_loads[2].wait()
    for order in range(1, GEN):
        adapter_copy(peer(order), peer(order)).wait_recv()
    unpack_adapters(adapters_in, flat_in, spread, down_ref, up_ref)
    feed(state, gains_ref[1:2], inner.at[0], outer.at[0], act, None, down_ref.at[0], up_ref.at[0],
         SRC, plain_e, low_e, after_e)
    memory[...] = normed(after_e[...], gains_ref[2:3])

    for order in range(1, GEN):
        target_copy(peer(order), peer(order)).wait_recv()
    inputs = known_rows(sources, targets)
    for owner in range(GEN):
        inputs = inputs + spread_rows(input_slot, tgt_in, owner)
    entry = normed(inputs, gains_ref[3:4])
    weight_loads[3].wait()
    for block in range(3):
        columns = slice(block * D, (block + 1) * D)
        qkv[own, columns] = mm(entry, attn[1, :, columns]).astype(jnp.bfloat16)
    causal = lax.broadcasted_iota(jnp.int32, (TGT, TGT), 0) >= lax.broadcasted_iota(
        jnp.int32, (TGT, TGT), 1
    )
    attend(qkv, qkv, D, 2 * D, TGT, TGT, lambda seq: causal, mixed)
    y1[...] = inputs + mm(mixed[own, :], attn[1, :, 3 * D :])
    weight_loads[4].wait()
    q_cross[...] = mm(normed(y1[...], gains_ref[4:5]), attn[2, :, :D]).astype(jnp.bfloat16)
    for block in range(2):
        columns = slice(block * D, (block + 1) * D)
        kv_cross[:, columns] = mm(
            memory[...], attn[2, :, (block + 1) * D : (block + 2) * D]
        ).astype(jnp.bfloat16)
    attend(q_cross, kv_cross, 0, D, TGT, SRC, allowed,
           mixed, probs)
    y2[...] = y1[...] + mm(mixed[own, :], attn[2, :, 3 * D :])
    weight_loads[5].wait()
    weight_loads[6].wait()
    feed(y2, gains_ref[5:6], inner.at[1], outer.at[1], act, slope, down_ref.at[1], up_ref.at[1],
         TGT, plain_d, low_d, y3)
    feats[0] = normed(y3[...], gains_ref[6:7])


    def feature_copy(order):
        return pltpu.make_async_remote_copy(
            src_ref=feats.at[0],
            dst_ref=feats.at[order],
            send_sem=feat_send.at[order],
            recv_sem=feat_recv.at[order],
            device_id={"gen": peer(order)},
            device_id_type=MESH,
        )

    def result_copy(order):
        return pltpu.make_async_remote_copy(
            src_ref=results(order),
            dst_ref=arrived(order),
            send_sem=result_send.at[order],
            recv_sem=result_recv.at[order],
            device_id={"gen": peer(order)},
            device_id_type=MESH,
        )

    def stat_copy(order):
        return pltpu.make_async_remote_copy(
            src_ref=stats.at[order],
            dst_ref=stats_in.at[order],
            send_sem=stat_send.at[order],
            recv_sem=stat_recv.at[order],
            device_id={"gen": peer(order)},
            device_id_type=MESH,
        )

    for order in range(1, GEN):
        feature_copy(order).start()
    wanted[...] = known_rows(sources + targets, targets)
    for owner in range(GEN):
        wanted[...] = wanted[...] + spread_rows(target_slot, tgt_in, owner)
    same = lax.broadcasted_iota(jnp.int32, (targets, targets), 0) == lax.broadcasted_iota(
        jnp.int32, (targets, targets), 1
    )

    def as_row(column):
        return jnp.sum(jnp.where(same, column, 0.0), axis=0, keepdims=True)

    def as_column(row):
        return jnp.sum(jnp.where(same, row, 0.0), axis=1, keepdims=True)

    def block_step(order, carry):
        @pl.when(order > 0)
        def _():
            feature_copy(order).wait_recv()

        query = feats[order]
        ends = list(range(0, table.shape[0], VOCAB_TILE)) + [table.shape[0]]
        tiles = [(ends[i], ends[i + 1]) for i in range(len(ends) - 1)]
        peak = scale = None
        scores = mm_last(query, table[tiles[0][0] : tiles[0][1], :])
        for index, (first, last) in enumerate(tiles):
            following = None
            if index + 1 < len(tiles):
                following = mm_last(query, table[tiles[index + 1][0] : tiles[index + 1][1], :])
            top = jnp.max(scores, axis=-1, keepdims=True)
            if index > 0:
                top = jnp.maximum(peak, top)
            weights = jnp.exp2((scores - top) * EXP_SCALE)
            amount = jnp.sum(weights, axis=-1, keepdims=True)
            part = mm(weights.astype(jnp.bfloat16), table[first:last, :])
            if index == 0:
                total[...] = part
                scale = amount
            else:
                shrink = jnp.exp2((peak - top) * EXP_SCALE)
                total[...] = total[...] * shrink + part
                scale = scale * shrink + amount
            peak, scores = top, following
        results(order)[...] = total[...].astype(jnp.bfloat16)
        stats[order] = jnp.concatenate(
            [as_row(peak), as_row(scale), jnp.zeros((6, targets), jnp.float32)], axis=0
        )

        @pl.when(order > 0)
        def _():
            result_copy(order).start()
            stat_copy(order).start()

        return carry

    lax.fori_loop(0, GEN, block_step, 0)
    stats_in[0] = stats[0]
    for order in range(1, GEN):
        stat_copy(order).wait_recv()
    peaks = [as_column(stats_in[order, 0:1, :]) for order in range(GEN)]
    sums = [as_column(stats_in[order, 1:2, :]) for order in range(GEN)]
    top = jnp.maximum(jnp.maximum(peaks[0], peaks[1]), jnp.maximum(peaks[2], peaks[3]))
    parts = [jnp.exp2((peaks[order] - top) * EXP_SCALE) for order in range(GEN)]
    amount = sum(parts[order] * sums[order] for order in range(GEN))
    logsum = top * LOGIT_SCALE + jnp.log(amount)
    inverse = 1.0 / amount
    total[...] = results(0)[...].astype(jnp.float32) * (parts[0] * inverse)
    for order in range(1, GEN):
        result_copy(order).wait_recv()
        total[...] = total[...] + arrived(order)[...].astype(jnp.float32) * (parts[order] * inverse)
    picked = (
        jnp.sum(feats[0].astype(jnp.float32) * wanted[...], axis=-1, keepdims=True) * LOGIT_SCALE
    )
    counted = as_column(valid)
    loss = jnp.sum((logsum - picked) * counted, axis=0, keepdims=True)
    lane = lax.broadcasted_iota(jnp.int32, (8, 128), 1)
    totals = jnp.where(
        lane == 0, loss, jnp.where(lane == 1, tokens, jnp.where(lane == 2, crowded, 0.0))
    )

    grad[own, :] = norm_back(
        y3[...], gains_ref[6:7], (total[...] - wanted[...]) * (counted * LOGIT_SCALE)
    )
    adapter_back(grad.at[own], low_d, plain_d, down_ref.at[1], up_ref.at[1], TGT,
                 grad_down_ref, partial(grad_up_ref, 1), grad_low)

    def grad_copy(layer, owner, target):
        part = SEQ_DEV * FLAT
        begin = pl.multiple_of((layer * GEN + owner) * part, 8)
        return pltpu.make_async_remote_copy(
            src_ref=pack.at[layer, target],
            dst_ref=grads_in.at[pl.ds(begin, part)],
            send_sem=grad_send.at[layer, target],
            recv_sem=grad_recv.at[layer, owner],
            device_id={"gen": target},
            device_id_type=MESH,
        )

    def send_grads(layer):
        pack_grads(grad_down_ref, partial(grad_up_ref, layer), pack.at[layer])
        for order in range(1, GEN):
            grad_copy(layer, member, peer(order)).start()
        begin = pl.multiple_of((layer * GEN + member) * SEQ_DEV * FLAT, 8)
        grads_in[pl.ds(begin, SEQ_DEV * FLAT), :] = pack[layer, member]

    send_grads(1)
    for block in range(FF // D):
        columns = slice(block * D, (block + 1) * D)
        act[own, columns] = (
            mm_last(grad_low[...], outer[1, columns, :])
            * slope[pl.ds(block * targets, targets), :]
        ).astype(jnp.bfloat16)
    grad_entry = mm_last(act[own, :], inner[1])
    grad_state = grad[own, :] + norm_back(y2[...], gains_ref[5:6], grad_entry)
    mixed[own, :] = mm_last(grad_state.astype(jnp.bfloat16), attn[2, :, 3 * D :]).astype(
        jnp.bfloat16
    )
    attend_back(mixed, q_cross, kv_cross, probs, TGT, SRC, joined)
    grad_memory = mm_last(joined[...], attn[2, :, D : 3 * D])

    grad[...] = norm_back(after_e[...], gains_ref[2:3], grad_memory)
    adapter_back(grad, low_e, plain_e, down_ref.at[0], up_ref.at[0], SRC,
                 grad_down_ref, partial(grad_up_ref, 0))
    send_grads(0)
    for layer in range(LAYERS):
        for order in range(1, GEN):
            grad_copy(layer, peer(order), peer(order)).wait_recv()
    pairs = TASKS * LAYERS
    received = jnp.concatenate(
        [grads_in[pl.ds(tile, pairs, stride=FLAT), :] for tile in range(FLAT)], axis=1
    )
    chosen = sel_ref[...].astype(jnp.bfloat16)
    slots = mm(
        jnp.concatenate([chosen] * 3, axis=1), jnp.concatenate(split(received), axis=0)
    )

    padded = (width + 127) // 128 * 128
    for piece in range(count):
        low_edge = piece * width // 128 * 128
        shift = piece * width - low_edge
        window = slots[:, low_edge : low_edge + padded]
        if shift:
            window = pltpu.roll(window, padded - shift, axis=1)
        outgoing[piece] = packed(window, width)

    def scatter(step, carry):
        target = lax.rem(rank + step, count)
        pltpu.make_async_remote_copy(
            src_ref=outgoing.at[target],
            dst_ref=incoming.at[rank],
            send_sem=scatter_sem.at[0],
            recv_sem=scatter_sem.at[1],
            device_id={"dp": target},
            device_id_type=MESH,
        ).start()
        return carry

    def share(step, carry):
        pltpu.make_async_remote_copy(
            src_ref=shares.at[rank],
            dst_ref=shares.at[rank],
            send_sem=share_sem.at[0],
            recv_sem=share_sem.at[1],
            device_id={"dp": lax.rem(rank + step, count)},
            device_id_type=MESH,
        ).start()
        return carry

    def announce(step, carry):
        pltpu.make_async_remote_copy(
            src_ref=verdict_in.at[rank],
            dst_ref=verdict_in.at[rank],
            send_sem=verdict_sem.at[0],
            recv_sem=verdict_sem.at[1],
            device_id={"dp": lax.rem(rank + step, count)},
            device_id_type=MESH,
        ).start()
        return carry

    def wait_all(ref, sem):
        others = ref.at[pl.ds(0, count - 1)]
        pltpu.make_async_copy(others, others, sem).wait()

    lax.fori_loop(1, count, scatter, 0)
    incoming[rank] = outgoing[rank]
    wait_all(incoming, scatter_sem.at[1])
    summed = incoming[0]
    for source in range(1, count):
        summed = summed + incoming[source]
    shares[rank] = summed

    piece_rows = unpacked(summed, width)
    shift = lax.rem(rank * width, 128)
    if width % 128:
        piece_rows = jnp.where(
            shift > 0, pltpu.roll(piece_rows, width % 128, axis=1), piece_rows
        )
    low_edge = pl.multiple_of(rank * width // 128 * 128, 128)
    piece_hyper = hyper[:, pl.ds(low_edge, padded)]
    coded_part = exact(piece_rows, piece_hyper, ((1,), (1,)))
    hyper_grad = exact(coded_ref[...], piece_rows, ((0,), (0,)))
    square = jnp.sum(
        jnp.sum(hyper_grad * hyper_grad, axis=0, keepdims=True), axis=1, keepdims=True
    )
    summary[0:16, :] = jnp.concatenate(
        [coded_part, jnp.broadcast_to(square, (16, 64))], axis=1
    )
    summary[16:24, :] = totals
    copies = [
        pltpu.make_async_remote_copy(
            src_ref=summary,
            dst_ref=summary_in.at[member],
            send_sem=small_send.at[step],
            recv_sem=small_recv.at[step],
            device_id={"gen": lax.rem(member + step, GEN)},
            device_id_type=MESH,
        )
        for step in range(1, GEN)
    ]
    for copy in copies:
        copy.start()
    summary_in[member] = summary[...]
    lax.fori_loop(1, count, share, 0)
    for copy in copies:
        copy.wait_recv()
    verdict_in[rank] = (summary_in[0] + summary_in[1]) + (summary_in[2] + summary_in[3])
    lax.fori_loop(1, count, announce, 0)
    for order in range(1, GEN):
        source_copy(member, peer(order)).wait_send()
        adapter_copy(member, peer(order)).wait_send()
        target_copy(member, peer(order)).wait_send()
        feature_copy(order).wait_send()
        result_copy(order).wait_send()
        stat_copy(order).wait_send()
        for layer in range(LAYERS):
            grad_copy(layer, member, peer(order)).wait_send()
    for copy in copies:
        copy.wait_send()
    wait_all(outgoing, scatter_sem.at[0])
    wait_all(shares, share_sem.at[1])
    for piece in range(0, count, 2 if width % 128 else 1):
        first = unpacked(shares[piece], width)
        if width % 128:
            second = pltpu.roll(unpacked(shares[piece + 1], width), width % 128, axis=1)
            middle = width // 128 * 128
            begin = piece * width
            lane128 = lax.broadcasted_iota(jnp.int32, (1, 128), 1)
            out_ref[:, begin : begin + middle] = first[:, :middle]
            out_ref[:, begin + middle : begin + middle + 128] = jnp.where(
                lane128 < width % 128, first[:, middle : middle + 128], second[:, :128]
            )
            out_ref[:, begin + middle + 128 : begin + 2 * width] = second[
                :, 128 : 2 * width - middle
            ]
        else:
            out_ref[:, piece * width : (piece + 1) * width] = first[:, :width]
    wait_all(verdict_in, verdict_sem.at[1])
    result = verdict_in[0]
    for source in range(1, count):
        result = result + verdict_in[source]
    small_ref[...] = result
    missing_ref[0] = jnp.max(result[16:17, 2:3]).astype(jnp.int32)
    wait_all(shares, share_sem.at[0])
    wait_all(verdict_in, verdict_sem.at[0])


def packed(window, width):
    tiles = [window[:, 128 * i : 128 * (i + 1)] for i in range(width // 128)]
    if width % 128:
        rest = window[:, width // 128 * 128 :]
        rows = rest.shape[0] // 2
        lane = lax.broadcasted_iota(jnp.int32, (1, 128), 1)
        tiles.append(jnp.where(lane < 64, rest[:rows], pltpu.roll(rest[rows:], 64, axis=1)))
    return jnp.concatenate(tiles, axis=0)


def unpacked(rows, width):
    pairs = TASKS * LAYERS
    tiles = [rows[pairs * i : pairs * (i + 1)] for i in range(width // 128)]
    if width % 128:
        rest = rows[width // 128 * pairs :]
        lane = lax.broadcasted_iota(jnp.int32, (1, 128), 1)
        both = jnp.concatenate([rest, pltpu.roll(rest, 64, axis=1)], axis=0)
        tiles.append(jnp.where(lane < 64, both, 0.0))
    return jnp.concatenate(tiles, axis=1)


def unpack_adapters(entries, flat, spread, down_ref, up_ref):
    lane = lax.broadcasted_iota(jnp.int32, (1, 128), 1)
    kept = lane < ADAPTER
    run = D // 32
    for owner in range(GEN):
        flat(owner)[...] = entries[owner].astype(jnp.float32)
    up_ref[...] = jnp.zeros(up_ref.shape, jnp.bfloat16)
    for layer in range(LAYERS):
        for seq in range(SEQ_DEV):
            base = (seq * LAYERS + layer) * FLAT
            for owner in range(GEN // 2):
                tiles = [flat(owner)[pl.ds(base + j, run, stride=3), :] for j in range(3)]
                for step in range(run):
                    tile, shift = divmod(ADAPTER * step, 128)
                    piece = tiles[tile]
                    if shift:
                        piece = pltpu.roll(piece, 128 - shift, axis=1)
                    if shift + ADAPTER > 128:
                        tail = pltpu.roll(tiles[tile + 1], 128 - shift, axis=1)
                        piece = jnp.where(lane < 128 - shift, piece, tail)
                    spread[pl.ds(owner * (D // 2) + step, run, stride=run), :] = jnp.where(
                        kept, piece, 0.0
                    )
            down_ref[layer, seq] = spread[pl.ds(0, D), :].astype(jnp.bfloat16)
            halves_up = []
            for owner in range(GEN // 2, GEN):
                halves_up.append(
                    jnp.concatenate(
                        [
                            flat(owner)[pl.ds(base + k, ADAPTER // 2, stride=4), :]
                            for k in range(4)
                        ],
                        axis=1,
                    )
                )
            joined = jnp.concatenate(halves_up + [jnp.zeros((8, D), jnp.float32)], axis=0)
            up_ref[layer, seq, 0:32, :] = joined.astype(jnp.bfloat16)


def pack_grads(grad_down, grad_up, pack):
    lane = lax.broadcasted_iota(jnp.int32, (1, 128), 1)
    run = D // 32
    for seq in range(SEQ_DEV):
        base = seq * FLAT
        for owner in range(GEN // 2):
            tiles = [jnp.zeros((run, 128), jnp.float32) for _ in range(3)]
            for step in range(run):
                tile, shift = divmod(ADAPTER * step, 128)
                piece = grad_down(seq)[pl.ds(owner * (D // 2) + step, run, stride=run), :]
                if shift:
                    piece = pltpu.roll(piece, shift, axis=1)
                if shift + ADAPTER > 128:
                    tiles[tile] = tiles[tile] + jnp.where(lane >= shift, piece, 0.0)
                    tiles[tile + 1] = tiles[tile + 1] + jnp.where(lane < shift, piece, 0.0)
                else:
                    tiles[tile] = tiles[tile] + piece
            for j in range(3):
                pack[owner, pl.ds(base + j, run, stride=3), :] = tiles[j]
        for half in range(GEN // 2):
            rows = slice(half * (ADAPTER // 2), (half + 1) * (ADAPTER // 2))
            for k in range(4):
                pack[GEN // 2 + half, pl.ds(base + k, ADAPTER // 2, stride=4), :] = grad_up(seq)[
                    rows, 128 * k : 128 * (k + 1)
                ]


def step(done, known, task_ids, task_len, tgt_count, src_ids, tgt_ids, embeds, one, two, gains,
         hyper, attn_w, ffn_in, ffn_out, table):
    vmem = pl.BlockSpec(memory_space=pltpu.VMEM)
    smem = pl.BlockSpec(memory_space=pltpu.SMEM)
    whole = pl.BlockSpec(memory_space=pl.ANY)
    low, full = jnp.bfloat16, jnp.float32
    sources, targets = SEQ_DEV * SRC, SEQ_DEV * TGT
    pairs = TASKS * LAYERS
    count = lax.axis_size("dp")
    width = FLAT * 128 // count
    dma = pltpu.SemaphoreType.DMA
    return pl.pallas_call(
        step_kernel,
        out_shape=(
            jax.ShapeDtypeStruct((pairs, FLAT * 128), full),
            jax.ShapeDtypeStruct((24, 128), full),
            jax.ShapeDtypeStruct((pairs, two.shape[0]), full),
            jax.ShapeDtypeStruct((1,), jnp.int32),
        ),
        in_specs=[smem] * 3 + [vmem] * 7 + [whole] * 6,
        out_specs=(vmem, vmem, vmem, smem),
        scratch_shapes=[
            pltpu.VMEM(attn_w.shape, low),
            pltpu.VMEM(ffn_in.shape, low),
            pltpu.VMEM(ffn_out.shape, low),
            pltpu.VMEM(table.shape, low),
            pltpu.VMEM(table.shape, full),
            pltpu.VMEM((sources, D), low),
            pltpu.VMEM((sources, 3 * D), low),
            pltpu.VMEM((sources, D), low),
            pltpu.VMEM((sources, FF), low),
            pltpu.VMEM((GEN, targets, D), low),
            pltpu.VMEM((GEN, 8, targets), full),
            pltpu.VMEM((GEN, 8, targets), full),
            pltpu.VMEM((GEN, SRC_CAP + TGT_CAP, D), low),
            pltpu.VMEM((SRC_CAP, D), full),
            pltpu.VMEM((8, 384), jnp.int32),
            pltpu.SMEM((8, 384), jnp.int32),
            pltpu.VMEM((sources + 2 * targets, D), low),
            pltpu.VMEM((GEN, SRC_CAP, D), low),
            pltpu.VMEM((GEN, TGT_CAP, D), low),
            pltpu.VMEM((pairs * FLAT, 128), full),
            pltpu.VMEM((SEQ_DEV * D, LOW), full),
            pltpu.VMEM((GEN, SEQ_DEV * LAYERS * FLAT, 128), low),
            pltpu.VMEM((GEN, SEQ_DEV * LAYERS * FLAT, 128), low),
            pltpu.VMEM((pairs, pairs), full),
            pltpu.VMEM((LAYERS, SEQ_DEV, D, LOW), low),
            pltpu.VMEM((LAYERS, SEQ_DEV, LOW, D), low),
            pltpu.VMEM((LAYERS, GEN, SEQ_DEV * FLAT, 128), full),
            pltpu.VMEM((LAYERS * GEN * SEQ_DEV * FLAT, 128), full),
            pltpu.VMEM(hyper.shape, full),
            pltpu.VMEM((count, pairs * width // 128, 128), full),
            pltpu.VMEM((count, pairs * width // 128, 128), full),
            pltpu.VMEM((count, pairs * width // 128, 128), full),
            pltpu.VMEM((24, 128), full),
            pltpu.VMEM((GEN, 24, 128), full),
            pltpu.VMEM((count, 24, 128), full),
            dma((14,)),
            dma((3, GEN)),
            dma((GEN,)),
            dma((GEN,)),
            dma((GEN,)),
            dma((LAYERS, GEN)),
            dma((LAYERS, GEN)),
            dma((2,)),
            dma((2,)),
            dma((GEN,)),
            dma((GEN,)),
            dma((2,)),
            dma,
            dma((GEN,)),
            dma((GEN,)),
            dma((GEN,)),
            dma((GEN,)),
            dma((GEN,)),
            dma((GEN,)),
        ],
        compiler_params=pltpu.CompilerParams(
            collective_id=1, has_side_effects=True, vmem_limit_bytes=VMEM_LIMIT
        ),
        name="rows_forward_vocab_backward_sum",
    )(done, task_ids, tgt_count, task_len.reshape(1, -1), src_ids, tgt_ids, embeds, one, two, gains,
      known, hyper, attn_w, ffn_in, ffn_out, table)


def update_kernel(
    slots_ref,
    small_ref,
    coded_ref,
    embeds,
    embeds_m,
    embeds_v,
    one,
    one_m,
    one_v,
    two,
    two_m,
    two_v,
    hyper,
    hyper_m,
    hyper_v,
    loss_ref,
    tokens_ref,
    norm_ref,
    new_embeds,
    new_embeds_m,
    new_embeds_v,
    new_one,
    new_one_m,
    new_one_v,
    new_two,
    new_two_m,
    new_two_v,
    new_hyper,
    new_hyper_m,
    new_hyper_v,
    held,
    fresh,
    load_sem,
    store_sem,
):
    block = held.shape[3]

    def span(step):
        return pl.ds(step * block, block)

    loads = [
        [
            pltpu.make_async_copy(
                array.at[:, span(step)], held.at[step, index], load_sem.at[step, index]
            )
            for index, array in enumerate((hyper, hyper_m, hyper_v))
        ]
        for step in range(UPDATE_STEPS)
    ]
    for group in loads:
        for load in group:
            load.start()
    coded_grad = small_ref[0:16, 0:64]
    tokens = small_ref[16:17, 1:2]
    loss_ref[...] = small_ref[16:17, 0:1]
    tokens_ref[...] = tokens
    spread = stacked_left(coded_ref[...])
    for step in range(UPDATE_STEPS):
        columns = slice(step * block, (step + 1) * block)
        fresh[step, 0] = mm_first(spread, stacked_right(slots_ref[:, columns]))
    pairs = pair_rows(embeds[...])
    before = exact(pairs, one[...], ((1,), (0,)))
    tanh = gelu_tanh(before)
    active = (0.5 * before) * (1.0 + tanh)
    grad_two = exact(coded_grad, active, ((0,), (0,)))
    grad_before = exact(coded_grad, two[...], ((1,), (0,))) * gelu_slope(before, tanh)
    grad_one = exact(pairs, grad_before, ((0,), (0,)))
    grad_pairs = exact(grad_before, one[...], ((1,), (1,)))
    row = lax.broadcasted_iota(jnp.int32, (16, TASKS * LAYERS), 0)
    column = lax.broadcasted_iota(jnp.int32, (16, TASKS * LAYERS), 1)
    chosen = (row == column // LAYERS) & (row < TASKS) | (row == TASKS + column % LAYERS)
    grad_embeds = exact(chosen.astype(jnp.float32), grad_pairs, ((1,), (0,)))
    grad_embeds = grad_embeds[: TASKS + LAYERS]
    scale = 1.0 / tokens
    grads = [grad * scale for grad in (grad_embeds, grad_one, grad_two)]
    square = small_ref[0:1, 64:65] * scale * scale
    for grad in grads:
        square = square + jnp.sum(
            jnp.sum(grad * grad, axis=1, keepdims=True), axis=0, keepdims=True
        )
    norm = jnp.sqrt(square)
    norm_ref[...] = norm
    factor = jnp.minimum(1.0, clip_limit / (norm + 1e-06))
    for index, (weight, first, second, outs) in enumerate(
        (
            (embeds, embeds_m, embeds_v, (new_embeds, new_embeds_m, new_embeds_v)),
            (one, one_m, one_v, (new_one, new_one_m, new_one_v)),
            (two, two_m, two_v, (new_two, new_two_m, new_two_v)),
        )
    ):
        for out, value in zip(
            outs,
            adamw(weight[...], first[...], second[...], grads[index] * factor, rates[index]),
        ):
            out[...] = value

    stores = []
    clip = scale * factor
    for step in range(UPDATE_STEPS):
        for load in loads[step]:
            load.wait()
        grad = fresh[step, 0] * clip
        values = adamw(held[step, 0], held[step, 1], held[step, 2], grad, rates[3])
        for index, (array, value) in enumerate(zip((new_hyper, new_hyper_m, new_hyper_v), values)):
            fresh[step, index] = value
            stores.append(
                pltpu.make_async_copy(
                    fresh.at[step, index], array.at[:, span(step)], store_sem.at[step, index]
                )
            )
            stores[-1].start()
    for store in stores:
        store.wait()


def split(value):
    high = value.astype(jnp.bfloat16)
    rest = value - high.astype(jnp.float32)
    middle = rest.astype(jnp.bfloat16)
    return high, middle, (rest - middle.astype(jnp.float32)).astype(jnp.bfloat16)


def stacked_left(value, axis=0):
    high, middle, low = split(value)
    return jnp.concatenate([high, high, middle, high, middle, low], axis=axis)


def stacked_right(value):
    high, middle, low = split(value)
    return jnp.concatenate([high, middle, high, low, middle, high], axis=0)


def update(slots, small, coded, *weights):
    full = jnp.float32
    vmem = pl.BlockSpec(memory_space=pltpu.VMEM)
    whole = pl.BlockSpec(memory_space=pl.ANY)
    block = slots.shape[1] // UPDATE_STEPS
    one_value = jax.ShapeDtypeStruct((1, 1), full)
    buffer = pltpu.VMEM((UPDATE_STEPS, 3, weights[9].shape[0], block), full)
    return pl.pallas_call(
        update_kernel,
        out_shape=[one_value] * 3 + [jax.ShapeDtypeStruct(w.shape, full) for w in weights],
        in_specs=[vmem] * 12 + [whole] * 3,
        out_specs=[vmem] * 12 + [whole] * 3,
        scratch_shapes=[
            buffer,
            buffer,
            pltpu.SemaphoreType.DMA((UPDATE_STEPS, 3)),
            pltpu.SemaphoreType.DMA((UPDATE_STEPS, 3)),
        ],
        compiler_params=pltpu.CompilerParams(vmem_limit_bytes=VMEM_LIMIT),
        name="update",
    )(slots, small, coded, *weights)


def ring_rows(src_ids, tgt_ids, table):
    member = lax.axis_index("gen")
    inputs = jnp.concatenate([jnp.zeros_like(tgt_ids[:, :1]), tgt_ids[:, :-1]], axis=1)
    tokens = jnp.concatenate(
        [ids.reshape(GEN, -1) for ids in (src_ids, inputs, tgt_ids)], axis=1
    )
    ring = [(source, (source + 1) % GEN) for source in range(GEN)]

    def held(target):
        token = lax.dynamic_index_in_dim(tokens, target, 0, False) - member * table.shape[0]
        inside = (token >= 0) & (token < table.shape[0])
        rows = jnp.take(table, jnp.clip(token, 0, table.shape[0] - 1), axis=0)
        return jnp.where(inside[:, None], rows, jnp.zeros_like(rows))

    def pass_on(hop, rows):
        rows = lax.ppermute(rows, "gen", ring)
        return rows + held(lax.rem(member - 1 - hop + 2 * GEN, GEN))

    rows = lax.fori_loop(1, GEN, pass_on, held(lax.rem(member - 1 + GEN, GEN)))
    return jnp.pad(rows, ((0, table.shape[0] - rows.shape[0]), (0, 0)))


def per_device(
    src_ids,
    tgt_ids,
    task_ids,
    task_len,
    tgt_count,
    table,
    attn_w,
    ffn_in,
    ffn_out,
    gains,
    embeds,
    embeds_m,
    embeds_v,
    proj_one,
    proj_one_m,
    proj_one_v,
    proj_two,
    proj_two_m,
    proj_two_v,
    hyper,
    hyper_m,
    hyper_v,
):
    weights = (
        embeds, embeds_m, embeds_v,
        proj_one, proj_one_m, proj_one_v,
        proj_two.T, proj_two_m.T, proj_two_v.T,
        hyper, hyper_m, hyper_v,
    )
    inputs = (
        task_ids, task_len, tgt_count, src_ids, tgt_ids, embeds, proj_one, proj_two.T, gains,
        hyper, attn_w, ffn_in, ffn_out, table,
    )
    slots, small, coded, crowded = step(jnp.zeros((1,), jnp.int32), table, *inputs)

    def again(state):
        rows = ring_rows(src_ids, tgt_ids, table)
        slots, small, coded, _ = step(jnp.ones((1,), jnp.int32), rows, *inputs)
        return jnp.zeros((1,), jnp.int32), slots, small, coded

    _, slots, small, coded = lax.while_loop(
        lambda state: state[0][0] > 0, again, (crowded, slots, small, coded)
    )
    loss_sum, token_count, grad_norm, *updated = update(slots, small, coded, *weights)
    updated[6:9] = [value.T for value in updated[6:9]]
    return (loss_sum.reshape(()), token_count.reshape(()), grad_norm.reshape(()), *updated)


def solution(mesh):
    return jax.shard_map(
        per_device,
        mesh=mesh,
        in_specs=(
            P("dp", None),
            P("dp", None),
            P("dp"),
            P(),
            P("dp"),
            P("gen", None),
            P(),
            P(),
            P(),
            P(),
            P(),
            P(),
            P(),
            P(),
            P(),
            P(),
            P(),
            P(),
            P(),
            P(None, "gen"),
            P(None, "gen"),
            P(None, "gen"),
        ),
        out_specs=(
            P(),
            P(),
            P(),
            P(),
            P(),
            P(),
            P(),
            P(),
            P(),
            P(),
            P(),
            P(),
            P(None, "gen"),
            P(None, "gen"),
            P(None, "gen"),
        ),
        check_vma=False,
    )
```

```python
import math
from functools import partial

import jax
import jax.numpy as jnp
from jax import lax
from jax.experimental import pallas as pl
from jax.experimental.pallas import tpu as pltpu
from jax.sharding import PartitionSpec as P

D = 512
HEADS = 8
ADAPTER = 24
TASKS = 8
LAYERS = 2
SRC = 256
TGT = 128
FF = 2048
SEQ_DEV = 2
GEN = 4
LOW = 128
SRC_CAP = 176
TGT_CAP = 64
SRC_SPAN = 256
FLAT = 48
STEP = 5


epsilon = 1e-06
clip_limit = 0.001
beta_one = 0.9
beta_two = 0.999
adam_floor = 1e-08
weight_decay = 0.01
rates = (0.5, 0.1, 0.1, 0.005)
blocked = -1000000000.0
highest = lax.Precision.HIGHEST
LOGIT_SCALE = D ** (-0.5)
EXP_SCALE = LOGIT_SCALE / math.log(2.0)
UPSCALE = math.sqrt(D / ADAPTER)
GELU_A = math.sqrt(2.0 / math.pi)
GELU_B = 0.044715
VOCAB_TILE = 2048
UPDATE_STEPS = 4
VMEM_LIMIT = 63 * 1024 * 1024
MESH = pl.DeviceIdType.MESH


def adamw(weight, first, second, grad, rate):
    first = beta_one * first + (1.0 - beta_one) * grad
    second = beta_two * second + (1.0 - beta_two) * grad * grad
    corrected = first * (1.0 / (1.0 - beta_one**STEP))
    spread = jnp.sqrt(second * (1.0 / (1.0 - beta_two**STEP))) + adam_floor
    return (weight - rate * (corrected / spread + weight_decay * weight), first, second)


def mm(left, right):
    return lax.dot_general(
        left, right, (((1,), (0,)), ((), ())), preferred_element_type=jnp.float32
    )


def mm_last(left, right):
    return lax.dot_general(
        left, right, (((1,), (1,)), ((), ())), preferred_element_type=jnp.float32
    )


def mm_first(left, right):
    return lax.dot_general(
        left, right, (((0,), (0,)), ((), ())), preferred_element_type=jnp.float32
    )


def exact(left, right, dims):
    return lax.dot_general(
        left, right, (dims, ((), ())), precision=highest, preferred_element_type=jnp.float32
    )


def norm_scale(value):
    return lax.rsqrt(jnp.mean(value * value, axis=-1, keepdims=True) + epsilon)


def normed(value, gain):
    return (value * norm_scale(value) * gain).astype(jnp.bfloat16)


def norm_back(value, gain, grad):
    scale = norm_scale(value)
    weighted = grad * gain
    return scale * weighted - value * (
        scale * scale * scale * jnp.mean(weighted * value, axis=-1, keepdims=True)
    )


def gelu_tanh(value):
    return jnp.tanh(value * (GELU_A + (GELU_A * GELU_B) * (value * value)))


def gelu(value):
    return (0.5 * value) * (1.0 + gelu_tanh(value))


def gelu_slope(value, tanh):
    return 0.5 * (1.0 + tanh) + (0.5 * value) * (1.0 - tanh * tanh) * (
        GELU_A + (3.0 * GELU_A * GELU_B) * (value * value)
    )


def halves():
    lane = lax.broadcasted_iota(jnp.int32, (1, 128), 1)
    return [(lane // 64 == half) for half in range(2)]


def attend(q_ref, kv_ref, k_col, v_col, q_len, k_len, allow, out_ref, probs_ref=None):
    sides = halves()
    masks = [side.astype(jnp.float32).astype(jnp.bfloat16) for side in sides]

    def pair_step(pair, carry):
        lanes = pair * 128
        for seq in range(SEQ_DEV):
            q_rows = pl.ds(seq * q_len, q_len)
            k_rows = pl.ds(seq * k_len, k_len)
            query = q_ref[q_rows, pl.ds(lanes, 128)]
            keys = kv_ref[k_rows, pl.ds(k_col + lanes, 128)]
            values = kv_ref[k_rows, pl.ds(v_col + lanes, 128)]
            outs = []
            for half in range(2):
                scores = mm_last(query * masks[half], keys) * 0.125
                scores = jnp.where(allow(seq), scores, blocked)
                peak = jnp.max(scores, axis=-1, keepdims=True)
                weights = jnp.exp(scores - peak)
                probs = weights * (1.0 / jnp.sum(weights, axis=-1, keepdims=True))
                if probs_ref is not None:
                    begin = (pair * SEQ_DEV + seq) * q_len
                    probs_ref[pl.ds(begin, q_len), half * k_len : (half + 1) * k_len] = probs
                outs.append(mm(probs.astype(jnp.bfloat16), values))
            out_ref[q_rows, pl.ds(lanes, 128)] = jnp.where(sides[0], outs[0], outs[1]).astype(
                jnp.bfloat16
            )
        return carry

    for pair in range(HEADS // 2):
        pair_step(pair, 0)


def attend_back(grad_ref, q_ref, kv_ref, probs_ref, q_len, k_len, joined_ref):
    sides = halves()
    masks = [side.astype(jnp.float32).astype(jnp.bfloat16) for side in sides]

    def pair_step(pair, carry):
        lanes = pair * 128
        for seq in range(SEQ_DEV):
            q_rows = pl.ds(seq * q_len, q_len)
            k_rows = pl.ds(seq * k_len, k_len)
            grad = grad_ref[q_rows, pl.ds(lanes, 128)]
            query = q_ref[q_rows, pl.ds(lanes, 128)]
            values = kv_ref[k_rows, pl.ds(D + lanes, 128)]
            key_grads, value_grads = [], []
            for half in range(2):
                begin = (pair * SEQ_DEV + seq) * q_len
                probs = probs_ref[pl.ds(begin, q_len), half * k_len : (half + 1) * k_len]
                grad_probs = mm_last(grad * masks[half], values)
                value_grads.append(mm_first(probs.astype(jnp.bfloat16), grad))
                inner = jnp.sum(grad_probs * probs, axis=-1, keepdims=True)
                grad_scores = (probs * (grad_probs - inner)).astype(jnp.bfloat16)
                key_grads.append(mm_first(grad_scores, query))
            joined_ref[k_rows, pl.ds(lanes, 128)] = (
                jnp.where(sides[0], key_grads[0], key_grads[1]) * 0.125
            ).astype(jnp.bfloat16)
            joined_ref[k_rows, pl.ds(D + lanes, 128)] = jnp.where(
                sides[0], value_grads[0], value_grads[1]
            ).astype(jnp.bfloat16)
        return carry

    for pair in range(HEADS // 2):
        pair_step(pair, 0)


def feed(state_ref, gain, inner_ref, outer_ref, act_ref, slope_ref, down_ref, up_ref, length,
         plain_ref, low_ref, after_ref):
    rows = SEQ_DEV * length
    act_rows = pl.ds(0, rows)
    source = normed(state_ref[...], gain)
    for block in range(FF // D):
        columns = slice(block * D, (block + 1) * D)
        hidden = mm(source, inner_ref[:, columns])
        tanh = gelu_tanh(hidden)
        act_ref[act_rows, columns] = ((0.5 * hidden) * (1.0 + tanh)).astype(jnp.bfloat16)
        if slope_ref is not None:
            slope_ref[pl.ds(block * rows, rows), :] = gelu_slope(hidden, tanh)
    branch = mm(act_ref[act_rows, :], outer_ref[...])
    plain_ref[...] = branch.astype(jnp.bfloat16)
    for seq in range(SEQ_DEV):
        span = slice(seq * length, (seq + 1) * length)
        lowered = mm(plain_ref[span, :], down_ref[seq])
        low_ref[span, :] = lowered
        adapted = mm(gelu(lowered).astype(jnp.bfloat16), up_ref[seq]) * UPSCALE
        after_ref[span, :] = state_ref[span, :] + branch[span, :] + adapted


def adapter_back(grad_ref, low_ref, plain_ref, down_ref, up_ref, length, grad_down_ref,
                 grad_up_ref, branch_ref=None):
    for seq in range(SEQ_DEV):
        span = slice(seq * length, (seq + 1) * length)
        grad = grad_ref[span, :]
        grad_low = grad.astype(jnp.bfloat16)
        lowered = low_ref[span, :]
        tanh = gelu_tanh(lowered)
        bottleneck = ((0.5 * lowered) * (1.0 + tanh)).astype(jnp.bfloat16)
        grad_bottle = mm_last(grad_low, up_ref[seq]) * UPSCALE
        grad_up_ref(seq)[...] = mm_first(bottleneck, grad_low)[:ADAPTER] * UPSCALE
        grad_lowered = (grad_bottle * gelu_slope(lowered, tanh)).astype(jnp.bfloat16)
        grad_down_ref(seq)[...] = mm_first(plain_ref[span, :], grad_lowered)
        if branch_ref is not None:
            branch_ref[span, :] = (grad + mm_last(grad_lowered, down_ref[seq])).astype(
                jnp.bfloat16
            )


def pair_rows(embeds):
    return jnp.concatenate(
        [
            embeds[task : task + 1, :] + embeds[TASKS + layer : TASKS + layer + 1, :]
            for task in range(TASKS)
            for layer in range(LAYERS)
        ],
        axis=0,
    )


def rank_tokens(ids_ref, peer, member, part, done):
    length = ids_ref.shape[1]
    ids = jnp.concatenate(
        [
            jnp.concatenate(
                [ids_ref[pl.ds(SEQ_DEV * peer(k) + s, 1), :] for s in range(SEQ_DEV)], axis=1
            )
            for k in range(GEN)
        ],
        axis=0,
    )
    if length == TGT:
        lane = lax.broadcasted_iota(jnp.int32, (GEN, 128), 1)
        ids = jnp.concatenate([ids, jnp.where(lane == 0, 0, -1)], axis=1)
    count = ids.shape[1]
    own = ids[0:1]
    local = ids - member * part
    inside = ((local >= 0) & (local < part) & (ids >= 0)).astype(jnp.int32)
    held = [((own >= part * o) & (own < part * (o + 1))).astype(jnp.int32) for o in range(GEN)]
    lane = lax.broadcasted_iota(jnp.int32, ids.shape, 1)
    fresh = ((lax.rem(lane, length) == 0) | (ids != pltpu.roll(ids, 1, axis=1))).astype(jnp.int32)
    inside = inside * fresh
    ranks = jnp.concatenate([inside] + [mark * fresh[0:1] for mark in held], axis=0)
    lane = lax.broadcasted_iota(jnp.int32, ranks.shape, 1)
    reach = 1
    while reach < count:
        ranks = ranks + jnp.where(lane >= reach, pltpu.roll(ranks, reach, axis=1), 0)
        reach = 2 * reach
    return ids, local, inside, held, ranks - 1 - done * count, fresh


def row_numbers(ranked, peer_order, rows):
    _, local, inside, _, ranks, _ = ranked
    k = peer_order
    spot = lax.broadcasted_iota(jnp.int32, (rows, local.shape[1]), 0)
    position = jnp.where(inside[k : k + 1] > 0, ranks[k : k + 1], -1)
    return jnp.sum(jnp.where(spot == position, local[k : k + 1], 0), axis=1, keepdims=True)


def list_rows(ranked, rows, begin, index_vmem):
    span = (rows + 127) // 128 * 128
    same = lax.broadcasted_iota(jnp.int32, (rows, span), 0) == lax.broadcasted_iota(
        jnp.int32, (rows, span), 1
    )
    for k in range(GEN):
        index_vmem[k : k + 1, begin : begin + span] = jnp.sum(
            jnp.where(same, row_numbers(ranked, k, rows), 0), axis=0, keepdims=True
        )


def token_places(ranked, rows, part):
    ids, _, _, held, ranks, fresh = ranked
    slot = jnp.full((1, ids.shape[1]), -1.0, jnp.float32)
    crowded = jnp.zeros((1, 1), jnp.float32)
    for o in range(GEN):
        amount = ((ids >= part * o) & (ids < part * (o + 1)) & (fresh > 0)).astype(jnp.float32)
        most = jnp.max(jnp.sum(amount, axis=1, keepdims=True), axis=0, keepdims=True)
        crowded = jnp.maximum(crowded, (most > float(rows)).astype(jnp.float32))
        rank = ranks[GEN + o : GEN + o + 1]
        now = (held[o] > 0) & (rank >= 0) & (rank < rows)
        slot = jnp.where(now, (rank + o * rows).astype(jnp.float32), slot)
    return slot, crowded


def after_zero(slot):
    targets = SEQ_DEV * TGT
    lane = lax.broadcasted_iota(jnp.int32, (1, targets), 1)
    return jnp.where(
        lax.rem(lane, TGT) == 0,
        slot[:, targets : targets + 1],
        pltpu.roll(slot[:, :targets], 1, axis=1),
    )


def describe(task_ref, lens_ref, count_ref, member):
    own_first = member * SEQ_DEV
    position = lax.broadcasted_iota(jnp.int32, (1, SRC), 1)
    place = lax.broadcasted_iota(jnp.int32, (1, TGT), 1)
    task = lax.broadcasted_iota(jnp.int32, (1, TASKS), 1)
    allow, valid = [], []
    tokens = jnp.zeros((1, 1), jnp.float32)
    for s in range(SEQ_DEV):
        length = jnp.sum(
            jnp.where(task == task_ref[own_first + s], lens_ref[...], 0).astype(jnp.float32),
            axis=1,
            keepdims=True,
        )
        allow.append((position.astype(jnp.float32) < length).astype(jnp.float32))
        valid.append((place < count_ref[own_first + s]).astype(jnp.float32))
        tokens = tokens + jnp.sum(valid[-1], axis=1, keepdims=True)
    return jnp.concatenate(allow, axis=1), jnp.concatenate(valid, axis=1), tokens


def generate(task_ref, embeds_ref, one_ref, two_ref, hyper_ref, coded_ref, chosen,
             adapters, sel):
    coded = exact(
        gelu(exact(pair_rows(embeds_ref[...]), one_ref[...], ((1,), (0,)))),
        two_ref[...],
        ((1,), (1,)),
    )
    coded_ref[...] = coded
    flat = mm(stacked_left(coded, 1), stacked_right(hyper_ref[...])).astype(jnp.bfloat16)
    pairs = TASKS * LAYERS
    sequences = GEN * SEQ_DEV
    row_of = lax.broadcasted_iota(jnp.int32, (pairs, pairs), 0)
    column_of = lax.broadcasted_iota(jnp.int32, (pairs, pairs), 1)
    picks = jnp.zeros((pairs, pairs), jnp.float32)
    selector = jnp.zeros((pairs, pairs), jnp.float32)
    for seq in range(sequences):
        for layer in range(LAYERS):
            pair = task_ref[seq] * LAYERS + layer
            picks = jnp.where(
                (row_of == seq * LAYERS + layer) & (column_of == pair), 1.0, picks
            )
            selector = jnp.where(
                (row_of == pair) & (column_of == layer * sequences + seq), 1.0, selector
            )
    sel[...] = selector
    taken = mm(picks.astype(jnp.bfloat16), flat)
    for tile in range(FLAT):
        chosen[pl.ds(tile, pairs, stride=FLAT), :] = taken[:, 128 * tile : 128 * (tile + 1)]
    share = SEQ_DEV * LAYERS * FLAT
    for target in range(GEN):
        adapters[target] = chosen[pl.ds(target * share, share), :].astype(jnp.bfloat16)


def step_kernel(
    done_ref,
    task_ref,
    count_ref,
    lens_ref,
    src_ref,
    tgt_ref,
    embeds_ref,
    one_ref,
    two_ref,
    gains_ref,
    known_hbm,
    hyper_hbm,
    attn_hbm,
    inner_hbm,
    outer_hbm,
    table_hbm,
    out_ref,
    small_ref,
    coded_ref,
    missing_ref,
    attn,
    inner,
    outer,
    table,
    wide,
    plain_e,
    qkv,
    mixed,
    act,
    feats,
    stats,
    stats_in,
    rows_out,
    picked_rows,
    index_vmem,
    index,
    known,
    src_in,
    tgt_in,
    generated,
    spread,
    adapters_ref,
    adapters_in,
    sel_ref,
    down_ref,
    up_ref,
    pack,
    pack_low,
    grads_low_in,
    grads_in,
    hyper,
    outgoing,
    incoming,
    shares,
    summary,
    summary_in,
    verdict_in,
    load_sem,
    row_send,
    src_recv,
    tgt_recv,
    adapter_recv,
    grad_send,
    grad_recv,
    scatter_sem,
    share_sem,
    small_send,
    small_recv,
    verdict_sem,
    index_sem,
    feat_send,
    feat_recv,
    result_send,
    result_recv,
    stat_send,
    stat_recv,
):
    member = lax.axis_index("gen")
    barrier = pltpu.get_barrier_semaphore()
    sources = SEQ_DEV * SRC
    targets = SEQ_DEV * TGT
    own = pl.ds(0, targets)
    part = table.shape[0]

    spans = []

    def view(rows, lanes=None):
        begin = spans[-1] if spans else 0
        if lanes is None:
            spans.append(begin + rows)
            return wide.at[pl.ds(begin, rows)]
        return wide.at[pl.ds(begin, rows), lanes]

    state, after_e, grad = view(sources), view(sources), view(sources)
    y1, y2, y3, total, wanted = (view(targets) for _ in range(5))
    slope = view(targets * (FF // D))
    probs = view(SEQ_DEV * HEADS // 2 * TGT)
    low_e = view(sources, pl.ds(0, LOW))
    low_d = view(targets, pl.ds(LOW, LOW))
    view(sources)
    first_up = spans[-1]
    view(LAYERS * SEQ_DEV * ADAPTER)

    def grad_down_ref(seq):
        return spread.at[pl.ds(seq * D, D)]

    def grad_up_ref(layer, seq):
        begin = first_up + (layer * SEQ_DEV + seq) * ADAPTER
        return wide.at[pl.ds(begin, ADAPTER)]

    def flat_in(owner):
        return generated.at[pl.ds(owner * SEQ_DEV * LAYERS * FLAT, SEQ_DEV * LAYERS * FLAT)]

    memory = inner.at[0, :, pl.ds(0, D)]
    q_cross = attn.at[1, pl.ds(0, targets), pl.ds(0, D)]
    plain_d = attn.at[1, pl.ds(targets, targets), pl.ds(0, D)]
    grad_low = attn.at[1, pl.ds(0, targets), pl.ds(D, D)]
    kv_cross = attn.at[0, :, pl.ds(0, 2 * D)]
    joined = attn.at[0, :, pl.ds(2 * D, 2 * D)]

    def results(order):
        return outer.at[0, pl.ds(pl.multiple_of(order * targets, targets), targets)]

    def arrived(order):
        begin = pl.multiple_of((GEN + order) * targets, targets)
        return outer.at[0, pl.ds(begin, targets)]

    def peer(order):
        chip = lax.rem(member // 2 + lax.rem((order + 1) // 2, 2), 2)
        return chip * 2 + lax.rem(lax.rem(member, 2) + order // 2, 2)

    rank = lax.axis_index("dp")
    count = outgoing.shape[0]
    width = TASKS * LAYERS * FLAT * 128 // (TASKS * LAYERS * count)
    loads = []

    def load(source, target):
        loads.append(pltpu.make_async_copy(source, target, load_sem.at[len(loads)]))
        loads[-1].start()
        return loads[-1]

    cuts = [0, 2048, 4096, 6144, part]
    table_loads = [
        load(
            table_hbm.at[pl.ds(cuts[i], cuts[i + 1] - cuts[i])],
            table.at[pl.ds(cuts[i], cuts[i + 1] - cuts[i])],
        )
        for i in range(4)
    ]
    hyper_load = load(hyper_hbm, hyper)
    known_load = load(known_hbm.at[pl.ds(0, known.shape[0])], known)
    for order in range(1, GEN):
        pl.semaphore_signal(
            barrier, inc=1, device_id={"gen": peer(order)}, device_id_type=MESH
        )

    for step in range(1, count):
        pl.semaphore_signal(
            barrier, inc=1, device_id={"dp": lax.rem(rank + step, count)}, device_id_type=MESH
        )
    weight_loads = [
        load(source, target)
        for source, target in (
            (attn_hbm.at[0], attn.at[0]),
            (inner_hbm.at[0], inner.at[0]),
            (outer_hbm.at[0], outer.at[0]),
            (attn_hbm.at[1], attn.at[1]),
            (attn_hbm.at[2], attn.at[2]),
            (inner_hbm.at[1], inner.at[1]),
            (outer_hbm.at[1], outer.at[1]),
        )
    ]

    def source_copy(owner, target):
        return pltpu.make_async_remote_copy(
            src_ref=rows_out.at[target, pl.ds(0, SRC_CAP)],
            dst_ref=src_in.at[owner],
            send_sem=row_send.at[0, target],
            recv_sem=src_recv.at[owner],
            device_id={"gen": target},
            device_id_type=MESH,
        )

    def target_copy(owner, target):
        return pltpu.make_async_remote_copy(
            src_ref=rows_out.at[target, pl.ds(SRC_CAP, TGT_CAP)],
            dst_ref=tgt_in.at[owner],
            send_sem=row_send.at[1, target],
            recv_sem=tgt_recv.at[owner],
            device_id={"gen": target},
            device_id_type=MESH,
        )

    def adapter_copy(owner, target):
        return pltpu.make_async_remote_copy(
            src_ref=adapters_ref.at[target],
            dst_ref=adapters_in.at[owner],
            send_sem=row_send.at[2, target],
            recv_sem=adapter_recv.at[owner],
            device_id={"gen": target},
            device_id_type=MESH,
        )

    sources_ranked = rank_tokens(src_ref, peer, member, part, done_ref[0])
    numbers = row_numbers(sources_ranked, 1, SRC_CAP)
    found = None
    for i in range(len(cuts) - 1):
        lane = lax.broadcasted_iota(jnp.int32, (SRC_CAP, cuts[i + 1] - cuts[i]), 1)
        hit = (lane + cuts[i] == numbers).astype(jnp.float32).astype(jnp.bfloat16)
        table_loads[i].wait()
        piece = mm(hit, table[cuts[i] : cuts[i + 1], :])
        found = piece if found is None else found + piece
    rows_out[peer(1), pl.ds(0, SRC_CAP), :] = found.astype(jnp.bfloat16)
    pl.semaphore_wait(barrier, GEN + count - 2)
    source_copy(member, peer(1)).start()

    targets_ranked = rank_tokens(tgt_ref, peer, member, part, done_ref[0])
    list_rows(sources_ranked, SRC_CAP, 0, index_vmem)
    list_rows(targets_ranked, TGT_CAP, SRC_SPAN, index_vmem)
    index_copy = pltpu.make_async_copy(index_vmem, index, index_sem)
    index_copy.start()
    chunk = 32
    for i in range(len(cuts) - 1):

        def widen(step, carry):
            begin = pl.multiple_of(cuts[i] + step * chunk, chunk)
            wide[pl.ds(begin, chunk), :] = table[pl.ds(begin, chunk), :].astype(jnp.float32)
            return carry

        lax.fori_loop(0, (cuts[i + 1] - cuts[i]) // chunk, widen, 0)
    index_copy.wait()

    def gather(order, begin, first, size):
        def fetch(step, carry):
            place = pl.multiple_of(step * 16, 16)
            for k in range(16):
                picked_rows[pl.ds(place + k, 1), :] = wide[
                    pl.ds(index[order, first + place + k], 1), :
                ]
            return carry

        lax.fori_loop(0, size // 16, fetch, 0)
        rows_out[peer(order), pl.ds(begin, size), :] = picked_rows[pl.ds(0, size), :].astype(
            jnp.bfloat16
        )

    gather(2, 0, 0, SRC_CAP)
    source_copy(member, peer(2)).start()
    hyper_load.wait()
    generate(task_ref, embeds_ref, one_ref, two_ref, hyper, coded_ref, generated, adapters_ref,
             sel_ref)
    for order in range(1, GEN):
        adapter_copy(member, peer(order)).start()
    for order in (1, 2):
        gather(order, SRC_CAP, SRC_SPAN, TGT_CAP)
        target_copy(member, peer(order)).start()
    gather(3, 0, 0, SRC_CAP)
    source_copy(member, peer(3)).start()
    gather(3, SRC_CAP, SRC_SPAN, TGT_CAP)
    target_copy(member, peer(3)).start()
    gather(0, 0, 0, SRC_CAP)
    gather(0, SRC_CAP, SRC_SPAN, TGT_CAP)
    src_in[member] = rows_out[member, 0:SRC_CAP, :]
    tgt_in[member] = rows_out[member, SRC_CAP : SRC_CAP + TGT_CAP, :]
    adapters_in[member] = adapters_ref[member]
    source_slot, crowded_sources = token_places(sources_ranked, SRC_CAP, part)
    target_slot, crowded_targets = token_places(targets_ranked, TGT_CAP, part)
    input_slot, target_slot = after_zero(target_slot), target_slot[:, :targets]
    crowded = jnp.maximum(crowded_sources, crowded_targets)
    allow, valid, tokens = describe(task_ref, lens_ref, count_ref, member)

    def spread_rows(slot, incoming_rows, first, owners):
        height = incoming_rows.shape[1]
        spot = lax.broadcasted_iota(jnp.int32, (owners * height, slot.shape[1]), 0)
        spot = (spot + first * height).astype(jnp.float32)
        chosen = (spot == slot).astype(jnp.float32).astype(jnp.bfloat16)
        rows = jnp.concatenate([incoming_rows[first + k] for k in range(owners)], axis=0)
        return mm_first(chosen, rows)

    known_load.wait()

    def known_rows(begin, size):
        rows = known[begin : begin + size, :].astype(jnp.float32)
        return jnp.where(done_ref[0] > 0, rows, 0.0)

    near = member // 2 * 2
    source_copy(peer(3), peer(3)).wait_recv()
    after_e[...] = known_rows(0, sources) + spread_rows(source_slot, src_in, near, 2)
    for order in (1, 2):
        source_copy(peer(order), peer(order)).wait_recv()
    after_e[...] = after_e[...] + spread_rows(source_slot, src_in, 2 - near, 2)
    embedded = after_e[...]

    def allowed(seq):
        return allow[:, seq * SRC : (seq + 1) * SRC] > 0.0

    entry = normed(embedded, gains_ref[0:1])
    weight_loads[0].wait()
    for block in range(3):
        columns = slice(block * D, (block + 1) * D)
        qkv[:, columns] = mm(entry, attn[0, :, columns]).astype(jnp.bfloat16)
    attend(qkv, qkv, D, 2 * D, SRC, SRC, allowed, mixed)
    state[...] = embedded + mm(mixed[...], attn[0, :, 3 * D :])
    weight_loads[1].wait()
    weight_loads[2].wait()
    for order in range(1, GEN):
        adapter_copy(peer(order), peer(order)).wait_recv()
    unpack_adapters(adapters_in, flat_in, spread, down_ref, up_ref)
    feed(state, gains_ref[1:2], inner.at[0], outer.at[0], act, None, down_ref.at[0], up_ref.at[0],
         SRC, plain_e, low_e, after_e)
    memory[...] = normed(after_e[...], gains_ref[2:3])

    for order in range(1, GEN):
        target_copy(peer(order), peer(order)).wait_recv()
    inputs = known_rows(sources, targets) + spread_rows(input_slot, tgt_in, 0, GEN)
    entry = normed(inputs, gains_ref[3:4])
    weight_loads[3].wait()
    for block in range(3):
        columns = slice(block * D, (block + 1) * D)
        qkv[own, columns] = mm(entry, attn[1, :, columns]).astype(jnp.bfloat16)
    causal = lax.broadcasted_iota(jnp.int32, (TGT, TGT), 0) >= lax.broadcasted_iota(
        jnp.int32, (TGT, TGT), 1
    )
    attend(qkv, qkv, D, 2 * D, TGT, TGT, lambda seq: causal, mixed)
    y1[...] = inputs + mm(mixed[own, :], attn[1, :, 3 * D :])
    weight_loads[4].wait()
    q_cross[...] = mm(normed(y1[...], gains_ref[4:5]), attn[2, :, :D]).astype(jnp.bfloat16)
    for block in range(2):
        columns = slice(block * D, (block + 1) * D)
        kv_cross[:, columns] = mm(
            memory[...], attn[2, :, (block + 1) * D : (block + 2) * D]
        ).astype(jnp.bfloat16)
    attend(q_cross, kv_cross, 0, D, TGT, SRC, allowed,
           mixed, probs)
    y2[...] = y1[...] + mm(mixed[own, :], attn[2, :, 3 * D :])
    weight_loads[5].wait()
    weight_loads[6].wait()
    feed(y2, gains_ref[5:6], inner.at[1], outer.at[1], act, slope, down_ref.at[1], up_ref.at[1],
         TGT, plain_d, low_d, y3)
    feats[0] = normed(y3[...], gains_ref[6:7])


    def feature_copy(order):
        return pltpu.make_async_remote_copy(
            src_ref=feats.at[0],
            dst_ref=feats.at[order],
            send_sem=feat_send.at[order],
            recv_sem=feat_recv.at[order],
            device_id={"gen": peer(order)},
            device_id_type=MESH,
        )

    def result_copy(order):
        return pltpu.make_async_remote_copy(
            src_ref=results(order),
            dst_ref=arrived(order),
            send_sem=result_send.at[order],
            recv_sem=result_recv.at[order],
            device_id={"gen": peer(order)},
            device_id_type=MESH,
        )

    def stat_copy(order):
        return pltpu.make_async_remote_copy(
            src_ref=stats.at[order],
            dst_ref=stats_in.at[order],
            send_sem=stat_send.at[order],
            recv_sem=stat_recv.at[order],
            device_id={"gen": peer(order)},
            device_id_type=MESH,
        )

    for order in range(1, GEN):
        feature_copy(order).start()
    wanted[...] = known_rows(sources + targets, targets) + spread_rows(
        target_slot, tgt_in, 0, GEN
    )
    same = lax.broadcasted_iota(jnp.int32, (targets, targets), 0) == lax.broadcasted_iota(
        jnp.int32, (targets, targets), 1
    )

    def as_row(column):
        return jnp.sum(jnp.where(same, column, 0.0), axis=0, keepdims=True)

    def as_column(row):
        return jnp.sum(jnp.where(same, row, 0.0), axis=1, keepdims=True)

    def block_step(order, carry):
        @pl.when(order > 0)
        def _():
            feature_copy(order).wait_recv()

        query = feats[order]
        ends = list(range(0, table.shape[0], VOCAB_TILE)) + [table.shape[0]]
        tiles = [(ends[i], ends[i + 1]) for i in range(len(ends) - 1)]
        peak = scale = None
        scores = mm_last(query, table[tiles[0][0] : tiles[0][1], :])
        for index, (first, last) in enumerate(tiles):
            following = None
            if index + 1 < len(tiles):
                following = mm_last(query, table[tiles[index + 1][0] : tiles[index + 1][1], :])
            top = jnp.max(scores, axis=-1, keepdims=True)
            if index > 0:
                top = jnp.maximum(peak, top)
            weights = jnp.exp2((scores - top) * EXP_SCALE)
            amount = jnp.sum(weights, axis=-1, keepdims=True)
            part = mm(weights.astype(jnp.bfloat16), table[first:last, :])
            if index == 0:
                total[...] = part
                scale = amount
            else:
                shrink = jnp.exp2((peak - top) * EXP_SCALE)
                total[...] = total[...] * shrink + part
                scale = scale * shrink + amount
            peak, scores = top, following
        results(order)[...] = total[...].astype(jnp.bfloat16)
        stats[order] = jnp.concatenate(
            [as_row(peak), as_row(scale), jnp.zeros((6, targets), jnp.float32)], axis=0
        )

        @pl.when(order > 0)
        def _():
            result_copy(order).start()
            stat_copy(order).start()

        return carry

    lax.fori_loop(0, GEN, block_step, 0)
    stats_in[0] = stats[0]
    for order in range(1, GEN):
        stat_copy(order).wait_recv()
    peaks = [as_column(stats_in[order, 0:1, :]) for order in range(GEN)]
    sums = [as_column(stats_in[order, 1:2, :]) for order in range(GEN)]
    top = jnp.maximum(jnp.maximum(peaks[0], peaks[1]), jnp.maximum(peaks[2], peaks[3]))
    parts = [jnp.exp2((peaks[order] - top) * EXP_SCALE) for order in range(GEN)]
    amount = sum(parts[order] * sums[order] for order in range(GEN))
    logsum = top * LOGIT_SCALE + jnp.log(amount)
    inverse = 1.0 / amount
    total[...] = results(0)[...].astype(jnp.float32) * (parts[0] * inverse)
    for order in range(1, GEN):
        result_copy(order).wait_recv()
        total[...] = total[...] + arrived(order)[...].astype(jnp.float32) * (parts[order] * inverse)
    picked = (
        jnp.sum(feats[0].astype(jnp.float32) * wanted[...], axis=-1, keepdims=True) * LOGIT_SCALE
    )
    counted = as_column(valid)
    loss = jnp.sum((logsum - picked) * counted, axis=0, keepdims=True)
    lane = lax.broadcasted_iota(jnp.int32, (8, 128), 1)
    totals = jnp.where(
        lane == 0, loss, jnp.where(lane == 1, tokens, jnp.where(lane == 2, crowded, 0.0))
    )

    grad[own, :] = norm_back(
        y3[...], gains_ref[6:7], (total[...] - wanted[...]) * (counted * LOGIT_SCALE)
    )
    adapter_back(grad.at[own], low_d, plain_d, down_ref.at[1], up_ref.at[1], TGT,
                 grad_down_ref, partial(grad_up_ref, 1), grad_low)

    def grad_copy(layer, owner, target):
        part = SEQ_DEV * FLAT
        begin = pl.multiple_of((layer * GEN + owner) * part, 8)
        return pltpu.make_async_remote_copy(
            src_ref=pack.at[layer, target] if layer else pack_low.at[target],
            dst_ref=grads_in.at[pl.ds(begin, part)] if layer else grads_low_in.at[owner],
            send_sem=grad_send.at[layer, target],
            recv_sem=grad_recv.at[layer, owner],
            device_id={"gen": target},
            device_id_type=MESH,
        )

    def send_grads(layer):
        pack_grads(grad_down_ref, partial(grad_up_ref, layer), pack.at[layer])
        if layer == 0:
            pack_low[...] = pack[0].astype(jnp.bfloat16)
        for order in range(1, GEN):
            grad_copy(layer, member, peer(order)).start()
        if layer == 0:
            grads_low_in[member] = pack_low[member]
        else:
            begin = pl.multiple_of((layer * GEN + member) * SEQ_DEV * FLAT, 8)
            grads_in[pl.ds(begin, SEQ_DEV * FLAT), :] = pack[layer, member]

    send_grads(1)
    for block in range(FF // D):
        columns = slice(block * D, (block + 1) * D)
        act[own, columns] = (
            mm_last(grad_low[...], outer[1, columns, :])
            * slope[pl.ds(block * targets, targets), :]
        ).astype(jnp.bfloat16)
    grad_entry = mm_last(act[own, :], inner[1])
    grad_state = grad[own, :] + norm_back(y2[...], gains_ref[5:6], grad_entry)
    mixed[own, :] = mm_last(grad_state.astype(jnp.bfloat16), attn[2, :, 3 * D :]).astype(
        jnp.bfloat16
    )
    attend_back(mixed, q_cross, kv_cross, probs, TGT, SRC, joined)
    grad_memory = mm_last(joined[...], attn[2, :, D : 3 * D])

    grad[...] = norm_back(after_e[...], gains_ref[2:3], grad_memory)
    adapter_back(grad, low_e, plain_e, down_ref.at[0], up_ref.at[0], SRC,
                 grad_down_ref, partial(grad_up_ref, 0))
    send_grads(0)
    for layer in range(LAYERS):
        for order in range(1, GEN):
            grad_copy(layer, peer(order), peer(order)).wait_recv()
    for owner in range(GEN):
        grads_in[pl.ds(owner * SEQ_DEV * FLAT, SEQ_DEV * FLAT), :] = grads_low_in[owner].astype(
            jnp.float32
        )
    pairs = TASKS * LAYERS
    received = jnp.concatenate(
        [grads_in[pl.ds(tile, pairs, stride=FLAT), :] for tile in range(FLAT)], axis=1
    )
    chosen = sel_ref[...].astype(jnp.bfloat16)
    slots = mm(
        jnp.concatenate([chosen] * 3, axis=1), jnp.concatenate(split(received), axis=0)
    )

    padded = (width + 127) // 128 * 128
    for piece in range(count):
        low_edge = piece * width // 128 * 128
        shift = piece * width - low_edge
        window = slots[:, low_edge : low_edge + padded]
        if shift:
            window = pltpu.roll(window, padded - shift, axis=1)
        outgoing[piece] = packed(window, width)

    def scatter(step, carry):
        target = lax.rem(rank + step, count)
        pltpu.make_async_remote_copy(
            src_ref=outgoing.at[target],
            dst_ref=incoming.at[rank],
            send_sem=scatter_sem.at[0],
            recv_sem=scatter_sem.at[1],
            device_id={"dp": target},
            device_id_type=MESH,
        ).start()
        return carry

    def share(step, carry):
        pltpu.make_async_remote_copy(
            src_ref=shares.at[rank],
            dst_ref=shares.at[rank],
            send_sem=share_sem.at[0],
            recv_sem=share_sem.at[1],
            device_id={"dp": lax.rem(rank + step, count)},
            device_id_type=MESH,
        ).start()
        return carry

    def announce(step, carry):
        pltpu.make_async_remote_copy(
            src_ref=verdict_in.at[rank],
            dst_ref=verdict_in.at[rank],
            send_sem=verdict_sem.at[0],
            recv_sem=verdict_sem.at[1],
            device_id={"dp": lax.rem(rank + step, count)},
            device_id_type=MESH,
        ).start()
        return carry

    def wait_all(ref, sem):
        others = ref.at[pl.ds(0, count - 1)]
        pltpu.make_async_copy(others, others, sem).wait()

    lax.fori_loop(1, count, scatter, 0)
    incoming[rank] = outgoing[rank]
    wait_all(incoming, scatter_sem.at[1])
    summed = incoming[0]
    for source in range(1, count):
        summed = summed + incoming[source]
    shares[rank] = summed

    piece_rows = unpacked(summed, width)
    shift = lax.rem(rank * width, 128)
    if width % 128:
        piece_rows = jnp.where(
            shift > 0, pltpu.roll(piece_rows, width % 128, axis=1), piece_rows
        )
    low_edge = pl.multiple_of(rank * width // 128 * 128, 128)
    piece_hyper = hyper[:, pl.ds(low_edge, padded)]
    coded_part = exact(piece_rows, piece_hyper, ((1,), (1,)))
    hyper_grad = exact(coded_ref[...], piece_rows, ((0,), (0,)))
    square = jnp.sum(
        jnp.sum(hyper_grad * hyper_grad, axis=0, keepdims=True), axis=1, keepdims=True
    )
    summary[0:16, :] = jnp.concatenate(
        [coded_part, jnp.broadcast_to(square, (16, 64))], axis=1
    )
    summary[16:24, :] = totals
    copies = [
        pltpu.make_async_remote_copy(
            src_ref=summary,
            dst_ref=summary_in.at[member],
            send_sem=small_send.at[step],
            recv_sem=small_recv.at[step],
            device_id={"gen": lax.rem(member + step, GEN)},
            device_id_type=MESH,
        )
        for step in range(1, GEN)
    ]
    for copy in copies:
        copy.start()
    summary_in[member] = summary[...]
    lax.fori_loop(1, count, share, 0)
    for copy in copies:
        copy.wait_recv()
    verdict_in[rank] = (summary_in[0] + summary_in[1]) + (summary_in[2] + summary_in[3])
    lax.fori_loop(1, count, announce, 0)
    for order in range(1, GEN):
        source_copy(member, peer(order)).wait_send()
        adapter_copy(member, peer(order)).wait_send()
        target_copy(member, peer(order)).wait_send()
        feature_copy(order).wait_send()
        result_copy(order).wait_send()
        stat_copy(order).wait_send()
        for layer in range(LAYERS):
            grad_copy(layer, member, peer(order)).wait_send()
    for copy in copies:
        copy.wait_send()
    wait_all(outgoing, scatter_sem.at[0])
    wait_all(shares, share_sem.at[1])
    for piece in range(0, count, 2 if width % 128 else 1):
        first = unpacked(shares[piece], width)
        if width % 128:
            second = pltpu.roll(unpacked(shares[piece + 1], width), width % 128, axis=1)
            middle = width // 128 * 128
            begin = piece * width
            lane128 = lax.broadcasted_iota(jnp.int32, (1, 128), 1)
            out_ref[:, begin : begin + middle] = first[:, :middle]
            out_ref[:, begin + middle : begin + middle + 128] = jnp.where(
                lane128 < width % 128, first[:, middle : middle + 128], second[:, :128]
            )
            out_ref[:, begin + middle + 128 : begin + 2 * width] = second[
                :, 128 : 2 * width - middle
            ]
        else:
            out_ref[:, piece * width : (piece + 1) * width] = first[:, :width]
    wait_all(verdict_in, verdict_sem.at[1])
    result = verdict_in[0]
    for source in range(1, count):
        result = result + verdict_in[source]
    small_ref[...] = result
    missing_ref[0] = jnp.max(result[16:17, 2:3]).astype(jnp.int32)
    wait_all(shares, share_sem.at[0])
    wait_all(verdict_in, verdict_sem.at[0])


def packed(window, width):
    tiles = [window[:, 128 * i : 128 * (i + 1)] for i in range(width // 128)]
    if width % 128:
        rest = window[:, width // 128 * 128 :]
        rows = rest.shape[0] // 2
        lane = lax.broadcasted_iota(jnp.int32, (1, 128), 1)
        tiles.append(jnp.where(lane < 64, rest[:rows], pltpu.roll(rest[rows:], 64, axis=1)))
    return jnp.concatenate(tiles, axis=0)


def unpacked(rows, width):
    pairs = TASKS * LAYERS
    tiles = [rows[pairs * i : pairs * (i + 1)] for i in range(width // 128)]
    if width % 128:
        rest = rows[width // 128 * pairs :]
        lane = lax.broadcasted_iota(jnp.int32, (1, 128), 1)
        both = jnp.concatenate([rest, pltpu.roll(rest, 64, axis=1)], axis=0)
        tiles.append(jnp.where(lane < 64, both, 0.0))
    return jnp.concatenate(tiles, axis=1)


def unpack_adapters(entries, flat, spread, down_ref, up_ref):
    lane = lax.broadcasted_iota(jnp.int32, (1, 128), 1)
    kept = lane < ADAPTER
    run = D // 32
    for owner in range(GEN):
        flat(owner)[...] = entries[owner].astype(jnp.float32)
    up_ref[...] = jnp.zeros(up_ref.shape, jnp.bfloat16)
    for layer in range(LAYERS):
        for seq in range(SEQ_DEV):
            base = (seq * LAYERS + layer) * FLAT
            for owner in range(GEN // 2):
                tiles = [flat(owner)[pl.ds(base + j, run, stride=3), :] for j in range(3)]
                for step in range(run):
                    tile, shift = divmod(ADAPTER * step, 128)
                    piece = tiles[tile]
                    if shift:
                        piece = pltpu.roll(piece, 128 - shift, axis=1)
                    if shift + ADAPTER > 128:
                        tail = pltpu.roll(tiles[tile + 1], 128 - shift, axis=1)
                        piece = jnp.where(lane < 128 - shift, piece, tail)
                    spread[pl.ds(owner * (D // 2) + step, run, stride=run), :] = jnp.where(
                        kept, piece, 0.0
                    )
            down_ref[layer, seq] = spread[pl.ds(0, D), :].astype(jnp.bfloat16)
            halves_up = []
            for owner in range(GEN // 2, GEN):
                halves_up.append(
                    jnp.concatenate(
                        [
                            flat(owner)[pl.ds(base + k, ADAPTER // 2, stride=4), :]
                            for k in range(4)
                        ],
                        axis=1,
                    )
                )
            joined = jnp.concatenate(halves_up + [jnp.zeros((8, D), jnp.float32)], axis=0)
            up_ref[layer, seq, 0:32, :] = joined.astype(jnp.bfloat16)


def pack_grads(grad_down, grad_up, pack):
    lane = lax.broadcasted_iota(jnp.int32, (1, 128), 1)
    run = D // 32
    for seq in range(SEQ_DEV):
        base = seq * FLAT
        for owner in range(GEN // 2):
            tiles = [jnp.zeros((run, 128), jnp.float32) for _ in range(3)]
            for step in range(run):
                tile, shift = divmod(ADAPTER * step, 128)
                piece = grad_down(seq)[pl.ds(owner * (D // 2) + step, run, stride=run), :]
                if shift:
                    piece = pltpu.roll(piece, shift, axis=1)
                if shift + ADAPTER > 128:
                    tiles[tile] = tiles[tile] + jnp.where(lane >= shift, piece, 0.0)
                    tiles[tile + 1] = tiles[tile + 1] + jnp.where(lane < shift, piece, 0.0)
                else:
                    tiles[tile] = tiles[tile] + piece
            for j in range(3):
                pack[owner, pl.ds(base + j, run, stride=3), :] = tiles[j]
        for half in range(GEN // 2):
            rows = slice(half * (ADAPTER // 2), (half + 1) * (ADAPTER // 2))
            for k in range(4):
                pack[GEN // 2 + half, pl.ds(base + k, ADAPTER // 2, stride=4), :] = grad_up(seq)[
                    rows, 128 * k : 128 * (k + 1)
                ]


def step(done, known, task_ids, task_len, tgt_count, src_ids, tgt_ids, embeds, one, two, gains,
         hyper, attn_w, ffn_in, ffn_out, table):
    vmem = pl.BlockSpec(memory_space=pltpu.VMEM)
    smem = pl.BlockSpec(memory_space=pltpu.SMEM)
    whole = pl.BlockSpec(memory_space=pl.ANY)
    low, full = jnp.bfloat16, jnp.float32
    sources, targets = SEQ_DEV * SRC, SEQ_DEV * TGT
    pairs = TASKS * LAYERS
    count = lax.axis_size("dp")
    width = FLAT * 128 // count
    dma = pltpu.SemaphoreType.DMA
    return pl.pallas_call(
        step_kernel,
        out_shape=(
            jax.ShapeDtypeStruct((pairs, FLAT * 128), full),
            jax.ShapeDtypeStruct((24, 128), full),
            jax.ShapeDtypeStruct((pairs, two.shape[0]), full),
            jax.ShapeDtypeStruct((1,), jnp.int32),
        ),
        in_specs=[smem] * 3 + [vmem] * 7 + [whole] * 6,
        out_specs=(vmem, vmem, vmem, smem),
        scratch_shapes=[
            pltpu.VMEM(attn_w.shape, low),
            pltpu.VMEM(ffn_in.shape, low),
            pltpu.VMEM(ffn_out.shape, low),
            pltpu.VMEM(table.shape, low),
            pltpu.VMEM(table.shape, full),
            pltpu.VMEM((sources, D), low),
            pltpu.VMEM((sources, 3 * D), low),
            pltpu.VMEM((sources, D), low),
            pltpu.VMEM((sources, FF), low),
            pltpu.VMEM((GEN, targets, D), low),
            pltpu.VMEM((GEN, 8, targets), full),
            pltpu.VMEM((GEN, 8, targets), full),
            pltpu.VMEM((GEN, SRC_CAP + TGT_CAP, D), low),
            pltpu.VMEM((SRC_CAP, D), full),
            pltpu.VMEM((8, 384), jnp.int32),
            pltpu.SMEM((8, 384), jnp.int32),
            pltpu.VMEM((sources + 2 * targets, D), low),
            pltpu.VMEM((GEN, SRC_CAP, D), low),
            pltpu.VMEM((GEN, TGT_CAP, D), low),
            pltpu.VMEM((pairs * FLAT, 128), full),
            pltpu.VMEM((SEQ_DEV * D, LOW), full),
            pltpu.VMEM((GEN, SEQ_DEV * LAYERS * FLAT, 128), low),
            pltpu.VMEM((GEN, SEQ_DEV * LAYERS * FLAT, 128), low),
            pltpu.VMEM((pairs, pairs), full),
            pltpu.VMEM((LAYERS, SEQ_DEV, D, LOW), low),
            pltpu.VMEM((LAYERS, SEQ_DEV, LOW, D), low),
            pltpu.VMEM((LAYERS, GEN, SEQ_DEV * FLAT, 128), full),
            pltpu.VMEM((GEN, SEQ_DEV * FLAT, 128), low),
            pltpu.VMEM((GEN, SEQ_DEV * FLAT, 128), low),
            pltpu.VMEM((LAYERS * GEN * SEQ_DEV * FLAT, 128), full),
            pltpu.VMEM(hyper.shape, full),
            pltpu.VMEM((count, pairs * width // 128, 128), full),
            pltpu.VMEM((count, pairs * width // 128, 128), full),
            pltpu.VMEM((count, pairs * width // 128, 128), full),
            pltpu.VMEM((24, 128), full),
            pltpu.VMEM((GEN, 24, 128), full),
            pltpu.VMEM((count, 24, 128), full),
            dma((14,)),
            dma((3, GEN)),
            dma((GEN,)),
            dma((GEN,)),
            dma((GEN,)),
            dma((LAYERS, GEN)),
            dma((LAYERS, GEN)),
            dma((2,)),
            dma((2,)),
            dma((GEN,)),
            dma((GEN,)),
            dma((2,)),
            dma,
            dma((GEN,)),
            dma((GEN,)),
            dma((GEN,)),
            dma((GEN,)),
            dma((GEN,)),
            dma((GEN,)),
        ],
        compiler_params=pltpu.CompilerParams(
            collective_id=1, has_side_effects=True, vmem_limit_bytes=VMEM_LIMIT
        ),
        name="rows_forward_vocab_backward_sum",
    )(done, task_ids, tgt_count, task_len.reshape(1, -1), src_ids, tgt_ids, embeds, one, two, gains,
      known, hyper, attn_w, ffn_in, ffn_out, table)


def update_kernel(
    slots_ref,
    small_ref,
    coded_ref,
    embeds,
    embeds_m,
    embeds_v,
    one,
    one_m,
    one_v,
    two,
    two_m,
    two_v,
    hyper,
    hyper_m,
    hyper_v,
    loss_ref,
    tokens_ref,
    norm_ref,
    new_embeds,
    new_embeds_m,
    new_embeds_v,
    new_one,
    new_one_m,
    new_one_v,
    new_two,
    new_two_m,
    new_two_v,
    new_hyper,
    new_hyper_m,
    new_hyper_v,
    held,
    fresh,
    load_sem,
    store_sem,
):
    block = held.shape[3]

    def span(step):
        return pl.ds(step * block, block)

    loads = [
        [
            pltpu.make_async_copy(
                array.at[:, span(step)], held.at[step, index], load_sem.at[step, index]
            )
            for index, array in enumerate((hyper, hyper_m, hyper_v))
        ]
        for step in range(UPDATE_STEPS)
    ]
    for group in loads:
        for load in group:
            load.start()
    coded_grad = small_ref[0:16, 0:64]
    tokens = small_ref[16:17, 1:2]
    loss_ref[...] = small_ref[16:17, 0:1]
    tokens_ref[...] = tokens
    spread = stacked_left(coded_ref[...])
    for step in range(UPDATE_STEPS):
        columns = slice(step * block, (step + 1) * block)
        fresh[step, 0] = mm_first(spread, stacked_right(slots_ref[:, columns]))
    pairs = pair_rows(embeds[...])
    before = exact(pairs, one[...], ((1,), (0,)))
    tanh = gelu_tanh(before)
    active = (0.5 * before) * (1.0 + tanh)
    grad_two = exact(coded_grad, active, ((0,), (0,)))
    grad_before = exact(coded_grad, two[...], ((1,), (0,))) * gelu_slope(before, tanh)
    grad_one = exact(pairs, grad_before, ((0,), (0,)))
    grad_pairs = exact(grad_before, one[...], ((1,), (1,)))
    row = lax.broadcasted_iota(jnp.int32, (16, TASKS * LAYERS), 0)
    column = lax.broadcasted_iota(jnp.int32, (16, TASKS * LAYERS), 1)
    chosen = (row == column // LAYERS) & (row < TASKS) | (row == TASKS + column % LAYERS)
    grad_embeds = exact(chosen.astype(jnp.float32), grad_pairs, ((1,), (0,)))
    grad_embeds = grad_embeds[: TASKS + LAYERS]
    scale = 1.0 / tokens
    grads = [grad * scale for grad in (grad_embeds, grad_one, grad_two)]
    square = small_ref[0:1, 64:65] * scale * scale
    for grad in grads:
        square = square + jnp.sum(
            jnp.sum(grad * grad, axis=1, keepdims=True), axis=0, keepdims=True
        )
    norm = jnp.sqrt(square)
    norm_ref[...] = norm
    factor = jnp.minimum(1.0, clip_limit / (norm + 1e-06))
    for index, (weight, first, second, outs) in enumerate(
        (
            (embeds, embeds_m, embeds_v, (new_embeds, new_embeds_m, new_embeds_v)),
            (one, one_m, one_v, (new_one, new_one_m, new_one_v)),
            (two, two_m, two_v, (new_two, new_two_m, new_two_v)),
        )
    ):
        for out, value in zip(
            outs,
            adamw(weight[...], first[...], second[...], grads[index] * factor, rates[index]),
        ):
            out[...] = value

    stores = []
    clip = scale * factor
    for step in range(UPDATE_STEPS):
        for load in loads[step]:
            load.wait()
        grad = fresh[step, 0] * clip
        values = adamw(held[step, 0], held[step, 1], held[step, 2], grad, rates[3])
        for index, (array, value) in enumerate(zip((new_hyper, new_hyper_m, new_hyper_v), values)):
            fresh[step, index] = value
            stores.append(
                pltpu.make_async_copy(
                    fresh.at[step, index], array.at[:, span(step)], store_sem.at[step, index]
                )
            )
            stores[-1].start()
    for store in stores:
        store.wait()


def split(value):
    high = value.astype(jnp.bfloat16)
    rest = value - high.astype(jnp.float32)
    middle = rest.astype(jnp.bfloat16)
    return high, middle, (rest - middle.astype(jnp.float32)).astype(jnp.bfloat16)


def stacked_left(value, axis=0):
    high, middle, low = split(value)
    return jnp.concatenate([high, high, middle, high, middle, low], axis=axis)


def stacked_right(value):
    high, middle, low = split(value)
    return jnp.concatenate([high, middle, high, low, middle, high], axis=0)


def update(slots, small, coded, *weights):
    full = jnp.float32
    vmem = pl.BlockSpec(memory_space=pltpu.VMEM)
    whole = pl.BlockSpec(memory_space=pl.ANY)
    block = slots.shape[1] // UPDATE_STEPS
    one_value = jax.ShapeDtypeStruct((1, 1), full)
    buffer = pltpu.VMEM((UPDATE_STEPS, 3, weights[9].shape[0], block), full)
    return pl.pallas_call(
        update_kernel,
        out_shape=[one_value] * 3 + [jax.ShapeDtypeStruct(w.shape, full) for w in weights],
        in_specs=[vmem] * 12 + [whole] * 3,
        out_specs=[vmem] * 12 + [whole] * 3,
        scratch_shapes=[
            buffer,
            buffer,
            pltpu.SemaphoreType.DMA((UPDATE_STEPS, 3)),
            pltpu.SemaphoreType.DMA((UPDATE_STEPS, 3)),
        ],
        compiler_params=pltpu.CompilerParams(vmem_limit_bytes=VMEM_LIMIT),
        name="update",
    )(slots, small, coded, *weights)


def ring_rows(src_ids, tgt_ids, table):
    member = lax.axis_index("gen")
    inputs = jnp.concatenate([jnp.zeros_like(tgt_ids[:, :1]), tgt_ids[:, :-1]], axis=1)
    tokens = jnp.concatenate(
        [ids.reshape(GEN, -1) for ids in (src_ids, inputs, tgt_ids)], axis=1
    )
    ring = [(source, (source + 1) % GEN) for source in range(GEN)]

    def held(target):
        token = lax.dynamic_index_in_dim(tokens, target, 0, False) - member * table.shape[0]
        inside = (token >= 0) & (token < table.shape[0])
        rows = jnp.take(table, jnp.clip(token, 0, table.shape[0] - 1), axis=0)
        return jnp.where(inside[:, None], rows, jnp.zeros_like(rows))

    def pass_on(hop, rows):
        rows = lax.ppermute(rows, "gen", ring)
        return rows + held(lax.rem(member - 1 - hop + 2 * GEN, GEN))

    rows = lax.fori_loop(1, GEN, pass_on, held(lax.rem(member - 1 + GEN, GEN)))
    return jnp.pad(rows, ((0, table.shape[0] - rows.shape[0]), (0, 0)))


def per_device(
    src_ids,
    tgt_ids,
    task_ids,
    task_len,
    tgt_count,
    table,
    attn_w,
    ffn_in,
    ffn_out,
    gains,
    embeds,
    embeds_m,
    embeds_v,
    proj_one,
    proj_one_m,
    proj_one_v,
    proj_two,
    proj_two_m,
    proj_two_v,
    hyper,
    hyper_m,
    hyper_v,
):
    weights = (
        embeds, embeds_m, embeds_v,
        proj_one, proj_one_m, proj_one_v,
        proj_two.T, proj_two_m.T, proj_two_v.T,
        hyper, hyper_m, hyper_v,
    )
    inputs = (
        task_ids, task_len, tgt_count, src_ids, tgt_ids, embeds, proj_one, proj_two.T, gains,
        hyper, attn_w, ffn_in, ffn_out, table,
    )
    slots, small, coded, crowded = step(jnp.zeros((1,), jnp.int32), table, *inputs)

    def again(state):
        rows = ring_rows(src_ids, tgt_ids, table)
        slots, small, coded, _ = step(jnp.ones((1,), jnp.int32), rows, *inputs)
        return jnp.zeros((1,), jnp.int32), slots, small, coded

    _, slots, small, coded = lax.while_loop(
        lambda state: state[0][0] > 0, again, (crowded, slots, small, coded)
    )
    loss_sum, token_count, grad_norm, *updated = update(slots, small, coded, *weights)
    updated[6:9] = [value.T for value in updated[6:9]]
    return (loss_sum.reshape(()), token_count.reshape(()), grad_norm.reshape(()), *updated)


def solution(mesh):
    return jax.shard_map(
        per_device,
        mesh=mesh,
        in_specs=(
            P("dp", None),
            P("dp", None),
            P("dp"),
            P(),
            P("dp"),
            P("gen", None),
            P(),
            P(),
            P(),
            P(),
            P(),
            P(),
            P(),
            P(),
            P(),
            P(),
            P(),
            P(),
            P(),
            P(None, "gen"),
            P(None, "gen"),
            P(None, "gen"),
        ),
        out_specs=(
            P(),
            P(),
            P(),
            P(),
            P(),
            P(),
            P(),
            P(),
            P(),
            P(),
            P(),
            P(),
            P(None, "gen"),
            P(None, "gen"),
            P(None, "gen"),
        ),
        check_vma=False,
    )
```

```python
import math
from functools import partial

import jax
import jax.numpy as jnp
from jax import lax
from jax.experimental import pallas as pl
from jax.experimental.pallas import tpu as pltpu
from jax.sharding import PartitionSpec as P

D = 512
HEADS = 8
ADAPTER = 24
TASKS = 8
LAYERS = 2
SRC = 256
TGT = 128
FF = 2048
SEQ_DEV = 2
GEN = 4
LOW = 128
SRC_CAP = 176
TGT_CAP = 64
SRC_SPAN = 256
FLAT = 48
STEP = 5


epsilon = 1e-06
clip_limit = 0.001
beta_one = 0.9
beta_two = 0.999
adam_floor = 1e-08
weight_decay = 0.01
rates = (0.5, 0.1, 0.1, 0.005)
blocked = -1000000000.0
highest = lax.Precision.HIGHEST
LOGIT_SCALE = D ** (-0.5)
EXP_SCALE = LOGIT_SCALE / math.log(2.0)
UPSCALE = math.sqrt(D / ADAPTER)
GELU_A = math.sqrt(2.0 / math.pi)
GELU_B = 0.044715
VOCAB_TILE = 2048
UPDATE_STEPS = 8
VMEM_LIMIT = 63 * 1024 * 1024
MESH = pl.DeviceIdType.MESH


def adamw(weight, first, second, grad, rate):
    first = beta_one * first + (1.0 - beta_one) * grad
    second = beta_two * second + (1.0 - beta_two) * grad * grad
    corrected = first * (1.0 / (1.0 - beta_one**STEP))
    spread = jnp.sqrt(second * (1.0 / (1.0 - beta_two**STEP))) + adam_floor
    return (weight - rate * (corrected / spread + weight_decay * weight), first, second)


def mm(left, right):
    return lax.dot_general(
        left, right, (((1,), (0,)), ((), ())), preferred_element_type=jnp.float32
    )


def mm_last(left, right):
    return lax.dot_general(
        left, right, (((1,), (1,)), ((), ())), preferred_element_type=jnp.float32
    )


def mm_first(left, right):
    return lax.dot_general(
        left, right, (((0,), (0,)), ((), ())), preferred_element_type=jnp.float32
    )


def exact(left, right, dims):
    return lax.dot_general(
        left, right, (dims, ((), ())), precision=highest, preferred_element_type=jnp.float32
    )


def norm_scale(value):
    return lax.rsqrt(jnp.mean(value * value, axis=-1, keepdims=True) + epsilon)


def normed(value, gain):
    return (value * norm_scale(value) * gain).astype(jnp.bfloat16)


def norm_back(value, gain, grad):
    scale = norm_scale(value)
    weighted = grad * gain
    return scale * weighted - value * (
        scale * scale * scale * jnp.mean(weighted * value, axis=-1, keepdims=True)
    )


def gelu_tanh(value):
    return jnp.tanh(value * (GELU_A + (GELU_A * GELU_B) * (value * value)))


def gelu(value):
    return (0.5 * value) * (1.0 + gelu_tanh(value))


def gelu_slope(value, tanh):
    return 0.5 * (1.0 + tanh) + (0.5 * value) * (1.0 - tanh * tanh) * (
        GELU_A + (3.0 * GELU_A * GELU_B) * (value * value)
    )


def halves():
    lane = lax.broadcasted_iota(jnp.int32, (1, 128), 1)
    return [(lane // 64 == half) for half in range(2)]


def attend(q_ref, kv_ref, k_col, v_col, q_len, k_len, allow, out_ref, probs_ref=None):
    sides = halves()
    masks = [side.astype(jnp.float32).astype(jnp.bfloat16) for side in sides]

    def pair_step(pair, carry):
        lanes = pair * 128
        for seq in range(SEQ_DEV):
            q_rows = pl.ds(seq * q_len, q_len)
            k_rows = pl.ds(seq * k_len, k_len)
            query = q_ref[q_rows, pl.ds(lanes, 128)]
            keys = kv_ref[k_rows, pl.ds(k_col + lanes, 128)]
            values = kv_ref[k_rows, pl.ds(v_col + lanes, 128)]
            outs = []
            for half in range(2):
                scores = mm_last(query * masks[half], keys) * 0.125
                scores = jnp.where(allow(seq), scores, blocked)
                peak = jnp.max(scores, axis=-1, keepdims=True)
                weights = jnp.exp(scores - peak)
                probs = weights * (1.0 / jnp.sum(weights, axis=-1, keepdims=True))
                if probs_ref is not None:
                    begin = (pair * SEQ_DEV + seq) * q_len
                    probs_ref[pl.ds(begin, q_len), half * k_len : (half + 1) * k_len] = probs
                outs.append(mm(probs.astype(jnp.bfloat16), values))
            out_ref[q_rows, pl.ds(lanes, 128)] = jnp.where(sides[0], outs[0], outs[1]).astype(
                jnp.bfloat16
            )
        return carry

    for pair in range(HEADS // 2):
        pair_step(pair, 0)


def attend_back(grad_ref, q_ref, kv_ref, probs_ref, q_len, k_len, joined_ref):
    sides = halves()
    masks = [side.astype(jnp.float32).astype(jnp.bfloat16) for side in sides]

    def pair_step(pair, carry):
        lanes = pair * 128
        for seq in range(SEQ_DEV):
            q_rows = pl.ds(seq * q_len, q_len)
            k_rows = pl.ds(seq * k_len, k_len)
            grad = grad_ref[q_rows, pl.ds(lanes, 128)]
            query = q_ref[q_rows, pl.ds(lanes, 128)]
            values = kv_ref[k_rows, pl.ds(D + lanes, 128)]
            key_grads, value_grads = [], []
            for half in range(2):
                begin = (pair * SEQ_DEV + seq) * q_len
                probs = probs_ref[pl.ds(begin, q_len), half * k_len : (half + 1) * k_len]
                grad_probs = mm_last(grad * masks[half], values)
                value_grads.append(mm_first(probs.astype(jnp.bfloat16), grad))
                inner = jnp.sum(grad_probs * probs, axis=-1, keepdims=True)
                grad_scores = (probs * (grad_probs - inner)).astype(jnp.bfloat16)
                key_grads.append(mm_first(grad_scores, query))
            joined_ref[k_rows, pl.ds(lanes, 128)] = (
                jnp.where(sides[0], key_grads[0], key_grads[1]) * 0.125
            ).astype(jnp.bfloat16)
            joined_ref[k_rows, pl.ds(D + lanes, 128)] = jnp.where(
                sides[0], value_grads[0], value_grads[1]
            ).astype(jnp.bfloat16)
        return carry

    for pair in range(HEADS // 2):
        pair_step(pair, 0)


def feed(state_ref, gain, inner_ref, outer_ref, act_ref, slope_ref, down_ref, up_ref, length,
         plain_ref, low_ref, after_ref):
    rows = SEQ_DEV * length
    act_rows = pl.ds(0, rows)
    source = normed(state_ref[...], gain)
    for block in range(FF // D):
        columns = slice(block * D, (block + 1) * D)
        hidden = mm(source, inner_ref[:, columns])
        tanh = gelu_tanh(hidden)
        act_ref[act_rows, columns] = ((0.5 * hidden) * (1.0 + tanh)).astype(jnp.bfloat16)
        if slope_ref is not None:
            slope_ref[pl.ds(block * rows, rows), :] = gelu_slope(hidden, tanh)
    branch = mm(act_ref[act_rows, :], outer_ref[...])
    plain_ref[...] = branch.astype(jnp.bfloat16)
    for seq in range(SEQ_DEV):
        span = slice(seq * length, (seq + 1) * length)
        lowered = mm(plain_ref[span, :], down_ref[seq])
        low_ref[span, :] = lowered
        adapted = mm(gelu(lowered).astype(jnp.bfloat16), up_ref[seq]) * UPSCALE
        after_ref[span, :] = state_ref[span, :] + branch[span, :] + adapted


def adapter_back(grad_ref, low_ref, plain_ref, down_ref, up_ref, length, grad_down_ref,
                 grad_up_ref, branch_ref=None):
    for seq in range(SEQ_DEV):
        span = slice(seq * length, (seq + 1) * length)
        grad = grad_ref[span, :]
        grad_low = grad.astype(jnp.bfloat16)
        lowered = low_ref[span, :]
        tanh = gelu_tanh(lowered)
        bottleneck = ((0.5 * lowered) * (1.0 + tanh)).astype(jnp.bfloat16)
        grad_bottle = mm_last(grad_low, up_ref[seq]) * UPSCALE
        grad_up_ref(seq)[...] = mm_first(bottleneck, grad_low)[:ADAPTER] * UPSCALE
        grad_lowered = (grad_bottle * gelu_slope(lowered, tanh)).astype(jnp.bfloat16)
        grad_down_ref(seq)[...] = mm_first(plain_ref[span, :], grad_lowered)
        if branch_ref is not None:
            branch_ref[span, :] = (grad + mm_last(grad_lowered, down_ref[seq])).astype(
                jnp.bfloat16
            )


def pair_rows(embeds):
    return jnp.concatenate(
        [
            embeds[task : task + 1, :] + embeds[TASKS + layer : TASKS + layer + 1, :]
            for task in range(TASKS)
            for layer in range(LAYERS)
        ],
        axis=0,
    )


def rank_tokens(ids_ref, peer, member, part, done):
    length = ids_ref.shape[1]
    ids = jnp.concatenate(
        [
            jnp.concatenate(
                [ids_ref[pl.ds(SEQ_DEV * peer(k) + s, 1), :] for s in range(SEQ_DEV)], axis=1
            )
            for k in range(GEN)
        ],
        axis=0,
    )
    if length == TGT:
        lane = lax.broadcasted_iota(jnp.int32, (GEN, 128), 1)
        ids = jnp.concatenate([ids, jnp.where(lane == 0, 0, -1)], axis=1)
    count = ids.shape[1]
    own = ids[0:1]
    local = ids - member * part
    inside = ((local >= 0) & (local < part) & (ids >= 0)).astype(jnp.int32)
    held = [((own >= part * o) & (own < part * (o + 1))).astype(jnp.int32) for o in range(GEN)]
    lane = lax.broadcasted_iota(jnp.int32, ids.shape, 1)
    fresh = ((lax.rem(lane, length) == 0) | (ids != pltpu.roll(ids, 1, axis=1))).astype(jnp.int32)
    inside = inside * fresh
    ranks = jnp.concatenate([inside] + [mark * fresh[0:1] for mark in held], axis=0)
    lane = lax.broadcasted_iota(jnp.int32, ranks.shape, 1)
    reach = 1
    while reach < count:
        ranks = ranks + jnp.where(lane >= reach, pltpu.roll(ranks, reach, axis=1), 0)
        reach = 2 * reach
    return ids, local, inside, held, ranks - 1 - done * count, fresh


def row_numbers(ranked, peer_order, rows):
    _, local, inside, _, ranks, _ = ranked
    k = peer_order
    spot = lax.broadcasted_iota(jnp.int32, (rows, local.shape[1]), 0)
    position = jnp.where(inside[k : k + 1] > 0, ranks[k : k + 1], -1)
    return jnp.sum(jnp.where(spot == position, local[k : k + 1], 0), axis=1, keepdims=True)


def list_rows(ranked, rows, begin, index_vmem):
    span = (rows + 127) // 128 * 128
    same = lax.broadcasted_iota(jnp.int32, (rows, span), 0) == lax.broadcasted_iota(
        jnp.int32, (rows, span), 1
    )
    for k in range(GEN):
        index_vmem[k : k + 1, begin : begin + span] = jnp.sum(
            jnp.where(same, row_numbers(ranked, k, rows), 0), axis=0, keepdims=True
        )


def token_places(ranked, rows, part):
    ids, _, _, held, ranks, fresh = ranked
    slot = jnp.full((1, ids.shape[1]), -1.0, jnp.float32)
    crowded = jnp.zeros((1, 1), jnp.float32)
    for o in range(GEN):
        amount = ((ids >= part * o) & (ids < part * (o + 1)) & (fresh > 0)).astype(jnp.float32)
        most = jnp.max(jnp.sum(amount, axis=1, keepdims=True), axis=0, keepdims=True)
        crowded = jnp.maximum(crowded, (most > float(rows)).astype(jnp.float32))
        rank = ranks[GEN + o : GEN + o + 1]
        now = (held[o] > 0) & (rank >= 0) & (rank < rows)
        slot = jnp.where(now, (rank + o * rows).astype(jnp.float32), slot)
    return slot, crowded


def after_zero(slot):
    targets = SEQ_DEV * TGT
    lane = lax.broadcasted_iota(jnp.int32, (1, targets), 1)
    return jnp.where(
        lax.rem(lane, TGT) == 0,
        slot[:, targets : targets + 1],
        pltpu.roll(slot[:, :targets], 1, axis=1),
    )


def describe(task_ref, lens_ref, count_ref, member):
    own_first = member * SEQ_DEV
    position = lax.broadcasted_iota(jnp.int32, (1, SRC), 1)
    place = lax.broadcasted_iota(jnp.int32, (1, TGT), 1)
    task = lax.broadcasted_iota(jnp.int32, (1, TASKS), 1)
    allow, valid = [], []
    tokens = jnp.zeros((1, 1), jnp.float32)
    for s in range(SEQ_DEV):
        length = jnp.sum(
            jnp.where(task == task_ref[own_first + s], lens_ref[...], 0).astype(jnp.float32),
            axis=1,
            keepdims=True,
        )
        allow.append((position.astype(jnp.float32) < length).astype(jnp.float32))
        valid.append((place < count_ref[own_first + s]).astype(jnp.float32))
        tokens = tokens + jnp.sum(valid[-1], axis=1, keepdims=True)
    return jnp.concatenate(allow, axis=1), jnp.concatenate(valid, axis=1), tokens


def generate(task_ref, embeds_ref, one_ref, two_ref, hyper_ref, coded_ref, chosen,
             adapters, sel):
    coded = exact(
        gelu(exact(pair_rows(embeds_ref[...]), one_ref[...], ((1,), (0,)))),
        two_ref[...],
        ((1,), (1,)),
    )
    coded_ref[...] = coded
    flat = mm(stacked_left(coded, 1), stacked_right(hyper_ref[...])).astype(jnp.bfloat16)
    pairs = TASKS * LAYERS
    sequences = GEN * SEQ_DEV
    row_of = lax.broadcasted_iota(jnp.int32, (pairs, pairs), 0)
    column_of = lax.broadcasted_iota(jnp.int32, (pairs, pairs), 1)
    picks = jnp.zeros((pairs, pairs), jnp.float32)
    selector = jnp.zeros((pairs, pairs), jnp.float32)
    for seq in range(sequences):
        for layer in range(LAYERS):
            pair = task_ref[seq] * LAYERS + layer
            picks = jnp.where(
                (row_of == seq * LAYERS + layer) & (column_of == pair), 1.0, picks
            )
            selector = jnp.where(
                (row_of == pair) & (column_of == layer * sequences + seq), 1.0, selector
            )
    sel[...] = selector
    taken = mm(picks.astype(jnp.bfloat16), flat)
    for tile in range(FLAT):
        chosen[pl.ds(tile, pairs, stride=FLAT), :] = taken[:, 128 * tile : 128 * (tile + 1)]
    share = SEQ_DEV * LAYERS * FLAT
    for target in range(GEN):
        adapters[target] = chosen[pl.ds(target * share, share), :].astype(jnp.bfloat16)


def step_kernel(
    done_ref,
    task_ref,
    count_ref,
    lens_ref,
    src_ref,
    tgt_ref,
    embeds_ref,
    one_ref,
    two_ref,
    gains_ref,
    known_hbm,
    hyper_hbm,
    attn_hbm,
    inner_hbm,
    outer_hbm,
    table_hbm,
    out_ref,
    small_ref,
    coded_ref,
    missing_ref,
    attn,
    inner,
    outer,
    table,
    wide,
    plain_e,
    qkv,
    mixed,
    act,
    feats,
    stats,
    stats_in,
    rows_out,
    picked_rows,
    index_vmem,
    index,
    known,
    src_in,
    tgt_in,
    generated,
    spread,
    adapters_ref,
    adapters_in,
    sel_ref,
    down_ref,
    up_ref,
    pack,
    pack_low,
    grads_low_in,
    grads_in,
    hyper,
    outgoing,
    incoming,
    shares,
    summary,
    summary_in,
    verdict_in,
    load_sem,
    row_send,
    src_recv,
    tgt_recv,
    adapter_recv,
    grad_send,
    grad_recv,
    scatter_sem,
    share_sem,
    small_send,
    small_recv,
    verdict_sem,
    index_sem,
    feat_send,
    feat_recv,
    result_send,
    result_recv,
    stat_send,
    stat_recv,
):
    member = lax.axis_index("gen")
    barrier = pltpu.get_barrier_semaphore()
    sources = SEQ_DEV * SRC
    targets = SEQ_DEV * TGT
    own = pl.ds(0, targets)
    part = table.shape[0]

    spans = []

    def view(rows, lanes=None):
        begin = spans[-1] if spans else 0
        if lanes is None:
            spans.append(begin + rows)
            return wide.at[pl.ds(begin, rows)]
        return wide.at[pl.ds(begin, rows), lanes]

    state, after_e, grad = view(sources), view(sources), view(sources)
    y1, y2, y3, total, wanted = (view(targets) for _ in range(5))
    slope = view(targets * (FF // D))
    probs = view(SEQ_DEV * HEADS // 2 * TGT)
    low_e = view(sources, pl.ds(0, LOW))
    low_d = view(targets, pl.ds(LOW, LOW))
    view(sources)
    first_up = spans[-1]
    view(LAYERS * SEQ_DEV * ADAPTER)

    def grad_down_ref(seq):
        return spread.at[pl.ds(seq * D, D)]

    def grad_up_ref(layer, seq):
        begin = first_up + (layer * SEQ_DEV + seq) * ADAPTER
        return wide.at[pl.ds(begin, ADAPTER)]

    def flat_in(owner):
        return generated.at[pl.ds(owner * SEQ_DEV * LAYERS * FLAT, SEQ_DEV * LAYERS * FLAT)]

    memory = inner.at[0, :, pl.ds(0, D)]
    q_cross = attn.at[1, pl.ds(0, targets), pl.ds(0, D)]
    plain_d = attn.at[1, pl.ds(targets, targets), pl.ds(0, D)]
    grad_low = attn.at[1, pl.ds(0, targets), pl.ds(D, D)]
    kv_cross = attn.at[0, :, pl.ds(0, 2 * D)]
    joined = attn.at[0, :, pl.ds(2 * D, 2 * D)]

    def results(order):
        return outer.at[0, pl.ds(pl.multiple_of(order * targets, targets), targets)]

    def arrived(order):
        begin = pl.multiple_of((GEN + order) * targets, targets)
        return outer.at[0, pl.ds(begin, targets)]

    def peer(order):
        chip = lax.rem(member // 2 + lax.rem((order + 1) // 2, 2), 2)
        return chip * 2 + lax.rem(lax.rem(member, 2) + order // 2, 2)

    rank = lax.axis_index("dp")
    count = outgoing.shape[0]
    width = TASKS * LAYERS * FLAT * 128 // (TASKS * LAYERS * count)
    loads = []

    def load(source, target):
        loads.append(pltpu.make_async_copy(source, target, load_sem.at[len(loads)]))
        loads[-1].start()
        return loads[-1]

    cuts = [0, 2048, 4096, 6144, part]
    table_loads = [
        load(
            table_hbm.at[pl.ds(cuts[i], cuts[i + 1] - cuts[i])],
            table.at[pl.ds(cuts[i], cuts[i + 1] - cuts[i])],
        )
        for i in range(4)
    ]
    hyper_load = load(hyper_hbm, hyper)
    known_load = load(known_hbm.at[pl.ds(0, known.shape[0])], known)
    for order in range(1, GEN):
        pl.semaphore_signal(
            barrier, inc=1, device_id={"gen": peer(order)}, device_id_type=MESH
        )

    for step in range(1, count):
        pl.semaphore_signal(
            barrier, inc=1, device_id={"dp": lax.rem(rank + step, count)}, device_id_type=MESH
        )
    weight_loads = [
        load(source, target)
        for source, target in (
            (attn_hbm.at[0], attn.at[0]),
            (inner_hbm.at[0], inner.at[0]),
            (outer_hbm.at[0], outer.at[0]),
            (attn_hbm.at[1], attn.at[1]),
            (attn_hbm.at[2], attn.at[2]),
            (inner_hbm.at[1], inner.at[1]),
            (outer_hbm.at[1], outer.at[1]),
        )
    ]

    def source_copy(owner, target):
        return pltpu.make_async_remote_copy(
            src_ref=rows_out.at[target, pl.ds(0, SRC_CAP)],
            dst_ref=src_in.at[owner],
            send_sem=row_send.at[0, target],
            recv_sem=src_recv.at[owner],
            device_id={"gen": target},
            device_id_type=MESH,
        )

    def target_copy(owner, target):
        return pltpu.make_async_remote_copy(
            src_ref=rows_out.at[target, pl.ds(SRC_CAP, TGT_CAP)],
            dst_ref=tgt_in.at[owner],
            send_sem=row_send.at[1, target],
            recv_sem=tgt_recv.at[owner],
            device_id={"gen": target},
            device_id_type=MESH,
        )

    def adapter_copy(owner, target):
        return pltpu.make_async_remote_copy(
            src_ref=adapters_ref.at[target],
            dst_ref=adapters_in.at[owner],
            send_sem=row_send.at[2, target],
            recv_sem=adapter_recv.at[owner],
            device_id={"gen": target},
            device_id_type=MESH,
        )

    sources_ranked = rank_tokens(src_ref, peer, member, part, done_ref[0])
    numbers = row_numbers(sources_ranked, 1, SRC_CAP)
    found = None
    for i in range(len(cuts) - 1):
        lane = lax.broadcasted_iota(jnp.int32, (SRC_CAP, cuts[i + 1] - cuts[i]), 1)
        hit = (lane + cuts[i] == numbers).astype(jnp.float32).astype(jnp.bfloat16)
        table_loads[i].wait()
        piece = mm(hit, table[cuts[i] : cuts[i + 1], :])
        found = piece if found is None else found + piece
    rows_out[peer(1), pl.ds(0, SRC_CAP), :] = found.astype(jnp.bfloat16)
    pl.semaphore_wait(barrier, GEN + count - 2)
    source_copy(member, peer(1)).start()

    targets_ranked = rank_tokens(tgt_ref, peer, member, part, done_ref[0])
    list_rows(sources_ranked, SRC_CAP, 0, index_vmem)
    list_rows(targets_ranked, TGT_CAP, SRC_SPAN, index_vmem)
    index_copy = pltpu.make_async_copy(index_vmem, index, index_sem)
    index_copy.start()
    chunk = 32
    for i in range(len(cuts) - 1):

        def widen(step, carry):
            begin = pl.multiple_of(cuts[i] + step * chunk, chunk)
            wide[pl.ds(begin, chunk), :] = table[pl.ds(begin, chunk), :].astype(jnp.float32)
            return carry

        lax.fori_loop(0, (cuts[i + 1] - cuts[i]) // chunk, widen, 0)
    index_copy.wait()

    def gather(order, begin, first, size):
        def fetch(step, carry):
            place = pl.multiple_of(step * 16, 16)
            for k in range(16):
                picked_rows[pl.ds(place + k, 1), :] = wide[
                    pl.ds(index[order, first + place + k], 1), :
                ]
            return carry

        lax.fori_loop(0, size // 16, fetch, 0)
        rows_out[peer(order), pl.ds(begin, size), :] = picked_rows[pl.ds(0, size), :].astype(
            jnp.bfloat16
        )

    gather(2, 0, 0, SRC_CAP)
    source_copy(member, peer(2)).start()
    hyper_load.wait()
    generate(task_ref, embeds_ref, one_ref, two_ref, hyper, coded_ref, generated, adapters_ref,
             sel_ref)
    for order in range(1, GEN):
        adapter_copy(member, peer(order)).start()
    for order in (1, 2):
        gather(order, SRC_CAP, SRC_SPAN, TGT_CAP)
        target_copy(member, peer(order)).start()
    gather(3, 0, 0, SRC_CAP)
    source_copy(member, peer(3)).start()
    gather(3, SRC_CAP, SRC_SPAN, TGT_CAP)
    target_copy(member, peer(3)).start()
    gather(0, 0, 0, SRC_CAP)
    gather(0, SRC_CAP, SRC_SPAN, TGT_CAP)
    src_in[member] = rows_out[member, 0:SRC_CAP, :]
    tgt_in[member] = rows_out[member, SRC_CAP : SRC_CAP + TGT_CAP, :]
    adapters_in[member] = adapters_ref[member]
    source_slot, crowded_sources = token_places(sources_ranked, SRC_CAP, part)
    target_slot, crowded_targets = token_places(targets_ranked, TGT_CAP, part)
    input_slot, target_slot = after_zero(target_slot), target_slot[:, :targets]
    crowded = jnp.maximum(crowded_sources, crowded_targets)
    allow, valid, tokens = describe(task_ref, lens_ref, count_ref, member)

    def spread_rows(slot, incoming_rows, first, owners):
        height = incoming_rows.shape[1]
        spot = lax.broadcasted_iota(jnp.int32, (owners * height, slot.shape[1]), 0)
        spot = (spot + first * height).astype(jnp.float32)
        chosen = (spot == slot).astype(jnp.float32).astype(jnp.bfloat16)
        rows = jnp.concatenate([incoming_rows[first + k] for k in range(owners)], axis=0)
        return mm_first(chosen, rows)

    known_load.wait()

    def known_rows(begin, size):
        rows = known[begin : begin + size, :].astype(jnp.float32)
        return jnp.where(done_ref[0] > 0, rows, 0.0)

    near = member // 2 * 2
    source_copy(peer(3), peer(3)).wait_recv()
    after_e[...] = known_rows(0, sources) + spread_rows(source_slot, src_in, near, 2)
    for order in (1, 2):
        source_copy(peer(order), peer(order)).wait_recv()
    after_e[...] = after_e[...] + spread_rows(source_slot, src_in, 2 - near, 2)
    embedded = after_e[...]

    def allowed(seq):
        return allow[:, seq * SRC : (seq + 1) * SRC] > 0.0

    entry = normed(embedded, gains_ref[0:1])
    weight_loads[0].wait()
    for block in range(3):
        columns = slice(block * D, (block + 1) * D)
        qkv[:, columns] = mm(entry, attn[0, :, columns]).astype(jnp.bfloat16)
    attend(qkv, qkv, D, 2 * D, SRC, SRC, allowed, mixed)
    state[...] = embedded + mm(mixed[...], attn[0, :, 3 * D :])
    weight_loads[1].wait()
    weight_loads[2].wait()
    for order in range(1, GEN):
        adapter_copy(peer(order), peer(order)).wait_recv()
    unpack_adapters(adapters_in, flat_in, spread, down_ref, up_ref)
    feed(state, gains_ref[1:2], inner.at[0], outer.at[0], act, None, down_ref.at[0], up_ref.at[0],
         SRC, plain_e, low_e, after_e)
    memory[...] = normed(after_e[...], gains_ref[2:3])

    for order in range(1, GEN):
        target_copy(peer(order), peer(order)).wait_recv()
    inputs = known_rows(sources, targets) + spread_rows(input_slot, tgt_in, 0, GEN)
    entry = normed(inputs, gains_ref[3:4])
    weight_loads[3].wait()
    for block in range(3):
        columns = slice(block * D, (block + 1) * D)
        qkv[own, columns] = mm(entry, attn[1, :, columns]).astype(jnp.bfloat16)
    causal = lax.broadcasted_iota(jnp.int32, (TGT, TGT), 0) >= lax.broadcasted_iota(
        jnp.int32, (TGT, TGT), 1
    )
    attend(qkv, qkv, D, 2 * D, TGT, TGT, lambda seq: causal, mixed)
    y1[...] = inputs + mm(mixed[own, :], attn[1, :, 3 * D :])
    weight_loads[4].wait()
    q_cross[...] = mm(normed(y1[...], gains_ref[4:5]), attn[2, :, :D]).astype(jnp.bfloat16)
    for block in range(2):
        columns = slice(block * D, (block + 1) * D)
        kv_cross[:, columns] = mm(
            memory[...], attn[2, :, (block + 1) * D : (block + 2) * D]
        ).astype(jnp.bfloat16)
    attend(q_cross, kv_cross, 0, D, TGT, SRC, allowed,
           mixed, probs)
    y2[...] = y1[...] + mm(mixed[own, :], attn[2, :, 3 * D :])
    weight_loads[5].wait()
    weight_loads[6].wait()
    feed(y2, gains_ref[5:6], inner.at[1], outer.at[1], act, slope, down_ref.at[1], up_ref.at[1],
         TGT, plain_d, low_d, y3)
    feats[0] = normed(y3[...], gains_ref[6:7])


    def feature_copy(order):
        return pltpu.make_async_remote_copy(
            src_ref=feats.at[0],
            dst_ref=feats.at[order],
            send_sem=feat_send.at[order],
            recv_sem=feat_recv.at[order],
            device_id={"gen": peer(order)},
            device_id_type=MESH,
        )

    def result_copy(order):
        return pltpu.make_async_remote_copy(
            src_ref=results(order),
            dst_ref=arrived(order),
            send_sem=result_send.at[order],
            recv_sem=result_recv.at[order],
            device_id={"gen": peer(order)},
            device_id_type=MESH,
        )

    def stat_copy(order):
        return pltpu.make_async_remote_copy(
            src_ref=stats.at[order],
            dst_ref=stats_in.at[order],
            send_sem=stat_send.at[order],
            recv_sem=stat_recv.at[order],
            device_id={"gen": peer(order)},
            device_id_type=MESH,
        )

    for order in range(1, GEN):
        feature_copy(order).start()
    wanted[...] = known_rows(sources + targets, targets) + spread_rows(
        target_slot, tgt_in, 0, GEN
    )
    same = lax.broadcasted_iota(jnp.int32, (targets, targets), 0) == lax.broadcasted_iota(
        jnp.int32, (targets, targets), 1
    )

    def as_row(column):
        return jnp.sum(jnp.where(same, column, 0.0), axis=0, keepdims=True)

    def as_column(row):
        return jnp.sum(jnp.where(same, row, 0.0), axis=1, keepdims=True)

    def block_step(order, carry):
        @pl.when(order > 0)
        def _():
            feature_copy(order).wait_recv()

        query = feats[order]
        ends = list(range(0, table.shape[0], VOCAB_TILE)) + [table.shape[0]]
        tiles = [(ends[i], ends[i + 1]) for i in range(len(ends) - 1)]
        peak = scale = None
        scores = mm_last(query, table[tiles[0][0] : tiles[0][1], :])
        for index, (first, last) in enumerate(tiles):
            following = None
            if index + 1 < len(tiles):
                following = mm_last(query, table[tiles[index + 1][0] : tiles[index + 1][1], :])
            top = jnp.max(scores, axis=-1, keepdims=True)
            if index > 0:
                top = jnp.maximum(peak, top)
            weights = jnp.exp2((scores - top) * EXP_SCALE)
            amount = jnp.sum(weights, axis=-1, keepdims=True)
            part = mm(weights.astype(jnp.bfloat16), table[first:last, :])
            if index == 0:
                total[...] = part
                scale = amount
            else:
                shrink = jnp.exp2((peak - top) * EXP_SCALE)
                total[...] = total[...] * shrink + part
                scale = scale * shrink + amount
            peak, scores = top, following
        results(order)[...] = total[...].astype(jnp.bfloat16)
        stats[order] = jnp.concatenate(
            [as_row(peak), as_row(scale), jnp.zeros((6, targets), jnp.float32)], axis=0
        )

        @pl.when(order > 0)
        def _():
            result_copy(order).start()
            stat_copy(order).start()

        return carry

    lax.fori_loop(0, GEN, block_step, 0)
    stats_in[0] = stats[0]
    for order in range(1, GEN):
        stat_copy(order).wait_recv()
    peaks = [as_column(stats_in[order, 0:1, :]) for order in range(GEN)]
    sums = [as_column(stats_in[order, 1:2, :]) for order in range(GEN)]
    top = jnp.maximum(jnp.maximum(peaks[0], peaks[1]), jnp.maximum(peaks[2], peaks[3]))
    parts = [jnp.exp2((peaks[order] - top) * EXP_SCALE) for order in range(GEN)]
    amount = sum(parts[order] * sums[order] for order in range(GEN))
    logsum = top * LOGIT_SCALE + jnp.log(amount)
    inverse = 1.0 / amount
    total[...] = results(0)[...].astype(jnp.float32) * (parts[0] * inverse)
    for order in range(1, GEN):
        result_copy(order).wait_recv()
        total[...] = total[...] + arrived(order)[...].astype(jnp.float32) * (parts[order] * inverse)
    picked = (
        jnp.sum(feats[0].astype(jnp.float32) * wanted[...], axis=-1, keepdims=True) * LOGIT_SCALE
    )
    counted = as_column(valid)
    loss = jnp.sum((logsum - picked) * counted, axis=0, keepdims=True)
    lane = lax.broadcasted_iota(jnp.int32, (8, 128), 1)
    totals = jnp.where(
        lane == 0, loss, jnp.where(lane == 1, tokens, jnp.where(lane == 2, crowded, 0.0))
    )

    grad[own, :] = norm_back(
        y3[...], gains_ref[6:7], (total[...] - wanted[...]) * (counted * LOGIT_SCALE)
    )
    adapter_back(grad.at[own], low_d, plain_d, down_ref.at[1], up_ref.at[1], TGT,
                 grad_down_ref, partial(grad_up_ref, 1), grad_low)

    def grad_copy(layer, owner, target):
        part = SEQ_DEV * FLAT
        begin = pl.multiple_of((layer * GEN + owner) * part, 8)
        return pltpu.make_async_remote_copy(
            src_ref=pack.at[layer, target] if layer else pack_low.at[target],
            dst_ref=grads_in.at[pl.ds(begin, part)] if layer else grads_low_in.at[owner],
            send_sem=grad_send.at[layer, target],
            recv_sem=grad_recv.at[layer, owner],
            device_id={"gen": target},
            device_id_type=MESH,
        )

    def send_grads(layer):
        pack_grads(grad_down_ref, partial(grad_up_ref, layer), pack.at[layer])
        if layer == 0:
            pack_low[...] = pack[0].astype(jnp.bfloat16)
        for order in range(1, GEN):
            grad_copy(layer, member, peer(order)).start()
        if layer == 0:
            grads_low_in[member] = pack_low[member]
        else:
            begin = pl.multiple_of((layer * GEN + member) * SEQ_DEV * FLAT, 8)
            grads_in[pl.ds(begin, SEQ_DEV * FLAT), :] = pack[layer, member]

    send_grads(1)
    for block in range(FF // D):
        columns = slice(block * D, (block + 1) * D)
        act[own, columns] = (
            mm_last(grad_low[...], outer[1, columns, :])
            * slope[pl.ds(block * targets, targets), :]
        ).astype(jnp.bfloat16)
    grad_entry = mm_last(act[own, :], inner[1])
    grad_state = grad[own, :] + norm_back(y2[...], gains_ref[5:6], grad_entry)
    mixed[own, :] = mm_last(grad_state.astype(jnp.bfloat16), attn[2, :, 3 * D :]).astype(
        jnp.bfloat16
    )
    attend_back(mixed, q_cross, kv_cross, probs, TGT, SRC, joined)
    grad_memory = mm_last(joined[...], attn[2, :, D : 3 * D])

    grad[...] = norm_back(after_e[...], gains_ref[2:3], grad_memory)
    adapter_back(grad, low_e, plain_e, down_ref.at[0], up_ref.at[0], SRC,
                 grad_down_ref, partial(grad_up_ref, 0))
    send_grads(0)
    for layer in range(LAYERS):
        for order in range(1, GEN):
            grad_copy(layer, peer(order), peer(order)).wait_recv()
    for owner in range(GEN):
        grads_in[pl.ds(owner * SEQ_DEV * FLAT, SEQ_DEV * FLAT), :] = grads_low_in[owner].astype(
            jnp.float32
        )
    pairs = TASKS * LAYERS
    received = jnp.concatenate(
        [grads_in[pl.ds(tile, pairs, stride=FLAT), :] for tile in range(FLAT)], axis=1
    )
    chosen = sel_ref[...].astype(jnp.bfloat16)
    slots = mm(
        jnp.concatenate([chosen] * 3, axis=1), jnp.concatenate(split(received), axis=0)
    )

    padded = (width + 127) // 128 * 128
    for piece in range(count):
        low_edge = piece * width // 128 * 128
        shift = piece * width - low_edge
        window = slots[:, low_edge : low_edge + padded]
        if shift:
            window = pltpu.roll(window, padded - shift, axis=1)
        outgoing[piece] = packed(window, width)

    def scatter(step, carry):
        target = lax.rem(rank + step, count)
        pltpu.make_async_remote_copy(
            src_ref=outgoing.at[target],
            dst_ref=incoming.at[rank],
            send_sem=scatter_sem.at[0],
            recv_sem=scatter_sem.at[1],
            device_id={"dp": target},
            device_id_type=MESH,
        ).start()
        return carry

    def share(step, carry):
        pltpu.make_async_remote_copy(
            src_ref=shares.at[rank],
            dst_ref=shares.at[rank],
            send_sem=share_sem.at[0],
            recv_sem=share_sem.at[1],
            device_id={"dp": lax.rem(rank + step, count)},
            device_id_type=MESH,
        ).start()
        return carry

    def announce(step, carry):
        pltpu.make_async_remote_copy(
            src_ref=verdict_in.at[rank],
            dst_ref=verdict_in.at[rank],
            send_sem=verdict_sem.at[0],
            recv_sem=verdict_sem.at[1],
            device_id={"dp": lax.rem(rank + step, count)},
            device_id_type=MESH,
        ).start()
        return carry

    def wait_all(ref, sem):
        others = ref.at[pl.ds(0, count - 1)]
        pltpu.make_async_copy(others, others, sem).wait()

    lax.fori_loop(1, count, scatter, 0)
    incoming[rank] = outgoing[rank]
    wait_all(incoming, scatter_sem.at[1])
    summed = incoming[0]
    for source in range(1, count):
        summed = summed + incoming[source]
    shares[rank] = summed

    piece_rows = unpacked(summed, width)
    shift = lax.rem(rank * width, 128)
    if width % 128:
        piece_rows = jnp.where(
            shift > 0, pltpu.roll(piece_rows, width % 128, axis=1), piece_rows
        )
    low_edge = pl.multiple_of(rank * width // 128 * 128, 128)
    piece_hyper = hyper[:, pl.ds(low_edge, padded)]
    coded_part = exact(piece_rows, piece_hyper, ((1,), (1,)))
    hyper_grad = exact(coded_ref[...], piece_rows, ((0,), (0,)))
    square = jnp.sum(
        jnp.sum(hyper_grad * hyper_grad, axis=0, keepdims=True), axis=1, keepdims=True
    )
    summary[0:16, :] = jnp.concatenate(
        [coded_part, jnp.broadcast_to(square, (16, 64))], axis=1
    )
    summary[16:24, :] = totals
    copies = [
        pltpu.make_async_remote_copy(
            src_ref=summary,
            dst_ref=summary_in.at[member],
            send_sem=small_send.at[step],
            recv_sem=small_recv.at[step],
            device_id={"gen": lax.rem(member + step, GEN)},
            device_id_type=MESH,
        )
        for step in range(1, GEN)
    ]
    for copy in copies:
        copy.start()
    summary_in[member] = summary[...]
    lax.fori_loop(1, count, share, 0)
    for copy in copies:
        copy.wait_recv()
    verdict_in[rank] = (summary_in[0] + summary_in[1]) + (summary_in[2] + summary_in[3])
    lax.fori_loop(1, count, announce, 0)
    for order in range(1, GEN):
        source_copy(member, peer(order)).wait_send()
        adapter_copy(member, peer(order)).wait_send()
        target_copy(member, peer(order)).wait_send()
        feature_copy(order).wait_send()
        result_copy(order).wait_send()
        stat_copy(order).wait_send()
        for layer in range(LAYERS):
            grad_copy(layer, member, peer(order)).wait_send()
    for copy in copies:
        copy.wait_send()
    wait_all(outgoing, scatter_sem.at[0])
    wait_all(shares, share_sem.at[1])
    for piece in range(0, count, 2 if width % 128 else 1):
        first = unpacked(shares[piece], width)
        if width % 128:
            second = pltpu.roll(unpacked(shares[piece + 1], width), width % 128, axis=1)
            middle = width // 128 * 128
            begin = piece * width
            lane128 = lax.broadcasted_iota(jnp.int32, (1, 128), 1)
            out_ref[:, begin : begin + middle] = first[:, :middle]
            out_ref[:, begin + middle : begin + middle + 128] = jnp.where(
                lane128 < width % 128, first[:, middle : middle + 128], second[:, :128]
            )
            out_ref[:, begin + middle + 128 : begin + 2 * width] = second[
                :, 128 : 2 * width - middle
            ]
        else:
            out_ref[:, piece * width : (piece + 1) * width] = first[:, :width]
    wait_all(verdict_in, verdict_sem.at[1])
    result = verdict_in[0]
    for source in range(1, count):
        result = result + verdict_in[source]
    small_ref[...] = result
    missing_ref[0] = jnp.max(result[16:17, 2:3]).astype(jnp.int32)
    wait_all(shares, share_sem.at[0])
    wait_all(verdict_in, verdict_sem.at[0])


def packed(window, width):
    tiles = [window[:, 128 * i : 128 * (i + 1)] for i in range(width // 128)]
    if width % 128:
        rest = window[:, width // 128 * 128 :]
        rows = rest.shape[0] // 2
        lane = lax.broadcasted_iota(jnp.int32, (1, 128), 1)
        tiles.append(jnp.where(lane < 64, rest[:rows], pltpu.roll(rest[rows:], 64, axis=1)))
    return jnp.concatenate(tiles, axis=0)


def unpacked(rows, width):
    pairs = TASKS * LAYERS
    tiles = [rows[pairs * i : pairs * (i + 1)] for i in range(width // 128)]
    if width % 128:
        rest = rows[width // 128 * pairs :]
        lane = lax.broadcasted_iota(jnp.int32, (1, 128), 1)
        both = jnp.concatenate([rest, pltpu.roll(rest, 64, axis=1)], axis=0)
        tiles.append(jnp.where(lane < 64, both, 0.0))
    return jnp.concatenate(tiles, axis=1)


def unpack_adapters(entries, flat, spread, down_ref, up_ref):
    lane = lax.broadcasted_iota(jnp.int32, (1, 128), 1)
    kept = lane < ADAPTER
    run = D // 32
    for owner in range(GEN):
        flat(owner)[...] = entries[owner].astype(jnp.float32)
    up_ref[...] = jnp.zeros(up_ref.shape, jnp.bfloat16)
    for layer in range(LAYERS):
        for seq in range(SEQ_DEV):
            base = (seq * LAYERS + layer) * FLAT
            for owner in range(GEN // 2):
                tiles = [flat(owner)[pl.ds(base + j, run, stride=3), :] for j in range(3)]
                for step in range(run):
                    tile, shift = divmod(ADAPTER * step, 128)
                    piece = tiles[tile]
                    if shift:
                        piece = pltpu.roll(piece, 128 - shift, axis=1)
                    if shift + ADAPTER > 128:
                        tail = pltpu.roll(tiles[tile + 1], 128 - shift, axis=1)
                        piece = jnp.where(lane < 128 - shift, piece, tail)
                    spread[pl.ds(owner * (D // 2) + step, run, stride=run), :] = jnp.where(
                        kept, piece, 0.0
                    )
            down_ref[layer, seq] = spread[pl.ds(0, D), :].astype(jnp.bfloat16)
            halves_up = []
            for owner in range(GEN // 2, GEN):
                halves_up.append(
                    jnp.concatenate(
                        [
                            flat(owner)[pl.ds(base + k, ADAPTER // 2, stride=4), :]
                            for k in range(4)
                        ],
                        axis=1,
                    )
                )
            joined = jnp.concatenate(halves_up + [jnp.zeros((8, D), jnp.float32)], axis=0)
            up_ref[layer, seq, 0:32, :] = joined.astype(jnp.bfloat16)


def pack_grads(grad_down, grad_up, pack):
    lane = lax.broadcasted_iota(jnp.int32, (1, 128), 1)
    run = D // 32
    for seq in range(SEQ_DEV):
        base = seq * FLAT
        for owner in range(GEN // 2):
            tiles = [jnp.zeros((run, 128), jnp.float32) for _ in range(3)]
            for step in range(run):
                tile, shift = divmod(ADAPTER * step, 128)
                piece = grad_down(seq)[pl.ds(owner * (D // 2) + step, run, stride=run), :]
                if shift:
                    piece = pltpu.roll(piece, shift, axis=1)
                if shift + ADAPTER > 128:
                    tiles[tile] = tiles[tile] + jnp.where(lane >= shift, piece, 0.0)
                    tiles[tile + 1] = tiles[tile + 1] + jnp.where(lane < shift, piece, 0.0)
                else:
                    tiles[tile] = tiles[tile] + piece
            for j in range(3):
                pack[owner, pl.ds(base + j, run, stride=3), :] = tiles[j]
        for half in range(GEN // 2):
            rows = slice(half * (ADAPTER // 2), (half + 1) * (ADAPTER // 2))
            for k in range(4):
                pack[GEN // 2 + half, pl.ds(base + k, ADAPTER // 2, stride=4), :] = grad_up(seq)[
                    rows, 128 * k : 128 * (k + 1)
                ]


def step(done, known, task_ids, task_len, tgt_count, src_ids, tgt_ids, embeds, one, two, gains,
         hyper, attn_w, ffn_in, ffn_out, table):
    vmem = pl.BlockSpec(memory_space=pltpu.VMEM)
    smem = pl.BlockSpec(memory_space=pltpu.SMEM)
    whole = pl.BlockSpec(memory_space=pl.ANY)
    low, full = jnp.bfloat16, jnp.float32
    sources, targets = SEQ_DEV * SRC, SEQ_DEV * TGT
    pairs = TASKS * LAYERS
    count = lax.axis_size("dp")
    width = FLAT * 128 // count
    dma = pltpu.SemaphoreType.DMA
    return pl.pallas_call(
        step_kernel,
        out_shape=(
            jax.ShapeDtypeStruct((pairs, FLAT * 128), full),
            jax.ShapeDtypeStruct((24, 128), full),
            jax.ShapeDtypeStruct((pairs, two.shape[0]), full),
            jax.ShapeDtypeStruct((1,), jnp.int32),
        ),
        in_specs=[smem] * 3 + [vmem] * 7 + [whole] * 6,
        out_specs=(vmem, vmem, vmem, smem),
        scratch_shapes=[
            pltpu.VMEM(attn_w.shape, low),
            pltpu.VMEM(ffn_in.shape, low),
            pltpu.VMEM(ffn_out.shape, low),
            pltpu.VMEM(table.shape, low),
            pltpu.VMEM(table.shape, full),
            pltpu.VMEM((sources, D), low),
            pltpu.VMEM((sources, 3 * D), low),
            pltpu.VMEM((sources, D), low),
            pltpu.VMEM((sources, FF), low),
            pltpu.VMEM((GEN, targets, D), low),
            pltpu.VMEM((GEN, 8, targets), full),
            pltpu.VMEM((GEN, 8, targets), full),
            pltpu.VMEM((GEN, SRC_CAP + TGT_CAP, D), low),
            pltpu.VMEM((SRC_CAP, D), full),
            pltpu.VMEM((8, 384), jnp.int32),
            pltpu.SMEM((8, 384), jnp.int32),
            pltpu.VMEM((sources + 2 * targets, D), low),
            pltpu.VMEM((GEN, SRC_CAP, D), low),
            pltpu.VMEM((GEN, TGT_CAP, D), low),
            pltpu.VMEM((pairs * FLAT, 128), full),
            pltpu.VMEM((SEQ_DEV * D, LOW), full),
            pltpu.VMEM((GEN, SEQ_DEV * LAYERS * FLAT, 128), low),
            pltpu.VMEM((GEN, SEQ_DEV * LAYERS * FLAT, 128), low),
            pltpu.VMEM((pairs, pairs), full),
            pltpu.VMEM((LAYERS, SEQ_DEV, D, LOW), low),
            pltpu.VMEM((LAYERS, SEQ_DEV, LOW, D), low),
            pltpu.VMEM((LAYERS, GEN, SEQ_DEV * FLAT, 128), full),
            pltpu.VMEM((GEN, SEQ_DEV * FLAT, 128), low),
            pltpu.VMEM((GEN, SEQ_DEV * FLAT, 128), low),
            pltpu.VMEM((LAYERS * GEN * SEQ_DEV * FLAT, 128), full),
            pltpu.VMEM(hyper.shape, full),
            pltpu.VMEM((count, pairs * width // 128, 128), full),
            pltpu.VMEM((count, pairs * width // 128, 128), full),
            pltpu.VMEM((count, pairs * width // 128, 128), full),
            pltpu.VMEM((24, 128), full),
            pltpu.VMEM((GEN, 24, 128), full),
            pltpu.VMEM((count, 24, 128), full),
            dma((14,)),
            dma((3, GEN)),
            dma((GEN,)),
            dma((GEN,)),
            dma((GEN,)),
            dma((LAYERS, GEN)),
            dma((LAYERS, GEN)),
            dma((2,)),
            dma((2,)),
            dma((GEN,)),
            dma((GEN,)),
            dma((2,)),
            dma,
            dma((GEN,)),
            dma((GEN,)),
            dma((GEN,)),
            dma((GEN,)),
            dma((GEN,)),
            dma((GEN,)),
        ],
        compiler_params=pltpu.CompilerParams(
            collective_id=1, has_side_effects=True, vmem_limit_bytes=VMEM_LIMIT
        ),
        name="rows_forward_vocab_backward_sum",
    )(done, task_ids, tgt_count, task_len.reshape(1, -1), src_ids, tgt_ids, embeds, one, two, gains,
      known, hyper, attn_w, ffn_in, ffn_out, table)


def update_kernel(
    slots_ref,
    small_ref,
    coded_ref,
    embeds,
    embeds_m,
    embeds_v,
    one,
    one_m,
    one_v,
    two,
    two_m,
    two_v,
    hyper,
    hyper_m,
    hyper_v,
    loss_ref,
    tokens_ref,
    norm_ref,
    new_embeds,
    new_embeds_m,
    new_embeds_v,
    new_one,
    new_one_m,
    new_one_v,
    new_two,
    new_two_m,
    new_two_v,
    new_hyper,
    new_hyper_m,
    new_hyper_v,
    held,
    fresh,
    load_sem,
    store_sem,
):
    block = held.shape[3]

    def span(step):
        return pl.ds(step * block, block)

    loads = [
        [
            pltpu.make_async_copy(
                array.at[:, span(step)], held.at[step, index], load_sem.at[step, index]
            )
            for index, array in enumerate((hyper, hyper_m, hyper_v))
        ]
        for step in range(UPDATE_STEPS)
    ]
    for group in loads:
        for load in group:
            load.start()
    coded_grad = small_ref[0:16, 0:64]
    tokens = small_ref[16:17, 1:2]
    loss_ref[...] = small_ref[16:17, 0:1]
    tokens_ref[...] = tokens
    spread = stacked_left(coded_ref[...])
    for step in range(UPDATE_STEPS):
        columns = slice(step * block, (step + 1) * block)
        fresh[step, 0] = mm_first(spread, stacked_right(slots_ref[:, columns]))
    pairs = pair_rows(embeds[...])
    before = exact(pairs, one[...], ((1,), (0,)))
    tanh = gelu_tanh(before)
    active = (0.5 * before) * (1.0 + tanh)
    grad_two = exact(coded_grad, active, ((0,), (0,)))
    grad_before = exact(coded_grad, two[...], ((1,), (0,))) * gelu_slope(before, tanh)
    grad_one = exact(pairs, grad_before, ((0,), (0,)))
    grad_pairs = exact(grad_before, one[...], ((1,), (1,)))
    row = lax.broadcasted_iota(jnp.int32, (16, TASKS * LAYERS), 0)
    column = lax.broadcasted_iota(jnp.int32, (16, TASKS * LAYERS), 1)
    chosen = (row == column // LAYERS) & (row < TASKS) | (row == TASKS + column % LAYERS)
    grad_embeds = exact(chosen.astype(jnp.float32), grad_pairs, ((1,), (0,)))
    grad_embeds = grad_embeds[: TASKS + LAYERS]
    scale = 1.0 / tokens
    grads = [grad * scale for grad in (grad_embeds, grad_one, grad_two)]
    square = small_ref[0:1, 64:65] * scale * scale
    for grad in grads:
        square = square + jnp.sum(
            jnp.sum(grad * grad, axis=1, keepdims=True), axis=0, keepdims=True
        )
    norm = jnp.sqrt(square)
    norm_ref[...] = norm
    factor = jnp.minimum(1.0, clip_limit / (norm + 1e-06))
    for index, (weight, first, second, outs) in enumerate(
        (
            (embeds, embeds_m, embeds_v, (new_embeds, new_embeds_m, new_embeds_v)),
            (one, one_m, one_v, (new_one, new_one_m, new_one_v)),
            (two, two_m, two_v, (new_two, new_two_m, new_two_v)),
        )
    ):
        for out, value in zip(
            outs,
            adamw(weight[...], first[...], second[...], grads[index] * factor, rates[index]),
        ):
            out[...] = value

    stores = []
    clip = scale * factor
    for step in range(UPDATE_STEPS):
        for load in loads[step]:
            load.wait()
        grad = fresh[step, 0] * clip
        values = adamw(held[step, 0], held[step, 1], held[step, 2], grad, rates[3])
        for index, (array, value) in enumerate(zip((new_hyper, new_hyper_m, new_hyper_v), values)):
            fresh[step, index] = value
            stores.append(
                pltpu.make_async_copy(
                    fresh.at[step, index], array.at[:, span(step)], store_sem.at[step, index]
                )
            )
            stores[-1].start()
    for store in stores:
        store.wait()


def split(value):
    high = value.astype(jnp.bfloat16)
    rest = value - high.astype(jnp.float32)
    middle = rest.astype(jnp.bfloat16)
    return high, middle, (rest - middle.astype(jnp.float32)).astype(jnp.bfloat16)


def stacked_left(value, axis=0):
    high, middle, low = split(value)
    return jnp.concatenate([high, high, middle, high, middle, low], axis=axis)


def stacked_right(value):
    high, middle, low = split(value)
    return jnp.concatenate([high, middle, high, low, middle, high], axis=0)


def update(slots, small, coded, *weights):
    full = jnp.float32
    vmem = pl.BlockSpec(memory_space=pltpu.VMEM)
    whole = pl.BlockSpec(memory_space=pl.ANY)
    block = slots.shape[1] // UPDATE_STEPS
    one_value = jax.ShapeDtypeStruct((1, 1), full)
    buffer = pltpu.VMEM((UPDATE_STEPS, 3, weights[9].shape[0], block), full)
    return pl.pallas_call(
        update_kernel,
        out_shape=[one_value] * 3 + [jax.ShapeDtypeStruct(w.shape, full) for w in weights],
        in_specs=[vmem] * 12 + [whole] * 3,
        out_specs=[vmem] * 12 + [whole] * 3,
        scratch_shapes=[
            buffer,
            buffer,
            pltpu.SemaphoreType.DMA((UPDATE_STEPS, 3)),
            pltpu.SemaphoreType.DMA((UPDATE_STEPS, 3)),
        ],
        compiler_params=pltpu.CompilerParams(vmem_limit_bytes=VMEM_LIMIT),
        name="update",
    )(slots, small, coded, *weights)


def ring_rows(src_ids, tgt_ids, table):
    member = lax.axis_index("gen")
    inputs = jnp.concatenate([jnp.zeros_like(tgt_ids[:, :1]), tgt_ids[:, :-1]], axis=1)
    tokens = jnp.concatenate(
        [ids.reshape(GEN, -1) for ids in (src_ids, inputs, tgt_ids)], axis=1
    )
    ring = [(source, (source + 1) % GEN) for source in range(GEN)]

    def held(target):
        token = lax.dynamic_index_in_dim(tokens, target, 0, False) - member * table.shape[0]
        inside = (token >= 0) & (token < table.shape[0])
        rows = jnp.take(table, jnp.clip(token, 0, table.shape[0] - 1), axis=0)
        return jnp.where(inside[:, None], rows, jnp.zeros_like(rows))

    def pass_on(hop, rows):
        rows = lax.ppermute(rows, "gen", ring)
        return rows + held(lax.rem(member - 1 - hop + 2 * GEN, GEN))

    rows = lax.fori_loop(1, GEN, pass_on, held(lax.rem(member - 1 + GEN, GEN)))
    return jnp.pad(rows, ((0, table.shape[0] - rows.shape[0]), (0, 0)))


def per_device(
    src_ids,
    tgt_ids,
    task_ids,
    task_len,
    tgt_count,
    table,
    attn_w,
    ffn_in,
    ffn_out,
    gains,
    embeds,
    embeds_m,
    embeds_v,
    proj_one,
    proj_one_m,
    proj_one_v,
    proj_two,
    proj_two_m,
    proj_two_v,
    hyper,
    hyper_m,
    hyper_v,
):
    weights = (
        embeds, embeds_m, embeds_v,
        proj_one, proj_one_m, proj_one_v,
        proj_two.T, proj_two_m.T, proj_two_v.T,
        hyper, hyper_m, hyper_v,
    )
    inputs = (
        task_ids, task_len, tgt_count, src_ids, tgt_ids, embeds, proj_one, proj_two.T, gains,
        hyper, attn_w, ffn_in, ffn_out, table,
    )
    slots, small, coded, crowded = step(jnp.zeros((1,), jnp.int32), table, *inputs)

    def again(state):
        rows = ring_rows(src_ids, tgt_ids, table)
        slots, small, coded, _ = step(jnp.ones((1,), jnp.int32), rows, *inputs)
        return jnp.zeros((1,), jnp.int32), slots, small, coded

    _, slots, small, coded = lax.while_loop(
        lambda state: state[0][0] > 0, again, (crowded, slots, small, coded)
    )
    loss_sum, token_count, grad_norm, *updated = update(slots, small, coded, *weights)
    updated[6:9] = [value.T for value in updated[6:9]]
    return (loss_sum.reshape(()), token_count.reshape(()), grad_norm.reshape(()), *updated)


def solution(mesh):
    return jax.shard_map(
        per_device,
        mesh=mesh,
        in_specs=(
            P("dp", None),
            P("dp", None),
            P("dp"),
            P(),
            P("dp"),
            P("gen", None),
            P(),
            P(),
            P(),
            P(),
            P(),
            P(),
            P(),
            P(),
            P(),
            P(),
            P(),
            P(),
            P(),
            P(None, "gen"),
            P(None, "gen"),
            P(None, "gen"),
        ),
        out_specs=(
            P(),
            P(),
            P(),
            P(),
            P(),
            P(),
            P(),
            P(),
            P(),
            P(),
            P(),
            P(),
            P(None, "gen"),
            P(None, "gen"),
            P(None, "gen"),
        ),
        check_vma=False,
    )
```
